32 devices in a mesh: img: 16 (over z, x, core), txt: 2 (over y).
Axes of the slice: x: 2, y: 2, z: 4, core: 2. Of those that a mesh axis runs over, the one named last changes fastest.
Arguments:
- image_emb: bfloat16 [512, 1152], P(('img', 'txt')), may hold values from -0.296875 to 0.296875
- text_emb: bfloat16 [512, 1152], P(('img', 'txt')), may hold values from -0.296875 to 0.296875
- pair_class: int32 [512], P(('img', 'txt')), may hold values from 0 to 255
- scale: float32 [], replicated, may hold values from 4 to 12
- shift: float32 [], replicated, may hold values from -2 to -0.5
Outputs:
- row_loss: float32 [512], P(('img', 'txt'))
- grad_image: float32 [512, 1152], P(('img', 'txt'))
- grad_text: float32 [512, 1152], P(('img', 'txt'))
The draws below stay inside these ranges and needn't reach their ends.
All inputs are finite; a program needn't handle non-finite values.
Results may differ from the reference program's by a relative error of at most 0.0012.
Values may be sent and summed in bfloat16 or wider, within the bound.
No kernel may reach another device: no remote copies, remote signals or barrier semaphores. Data moves between devices by JAX's collectives and lax.ppermute only.
A program may use at most 64 MiB of HBM per device.

```python
import math
import jax
import jax.numpy as jnp
import numpy as np
from jax import lax

D = 1152
PAIRS = 512


def shared_parts(key):
    basis_rows = jax.random.normal(jax.random.fold_in(key, 101), (5, D), jnp.float32)
    common = jax.random.normal(jax.random.fold_in(key, 102), (PAIRS, 5), jnp.float32)
    strength = jax.random.uniform(jax.random.fold_in(key, 103), (PAIRS, 1), jnp.float32)
    direction = jax.random.normal(jax.random.fold_in(key, 104), (1, D), jnp.float32)
    return (basis_rows, common, strength, direction)


def mix_rows(key, pieces, directions):
    basis_rows, common, strength, direction = pieces
    fresh_coef = jax.random.normal(jax.random.fold_in(key, 1), (PAIRS, directions), jnp.float32)
    coeffs = strength * common[:, :directions] + jnp.sqrt(1.0 - strength * strength) * fresh_coef
    shared_part = jnp.zeros((PAIRS, D), jnp.float32)
    for position in range(directions):
        shared_part = shared_part + coeffs[:, position:position + 1] * basis_rows[position:position + 1, :]
    return shared_part / math.sqrt(directions)


def spread_rows(key, lowest, highest):
    return jnp.exp(jax.random.uniform(jax.random.fold_in(key, 3), (PAIRS, 1), jnp.float32, math.log(lowest), math.log(highest)))


def draw_image_emb(key, part):
    pieces = shared_parts(key)
    key = jax.random.fold_in(key, 11)
    shared_part = mix_rows(key, pieces, 3)
    noise_part = jax.random.normal(jax.random.fold_in(key, 2), (PAIRS, D), jnp.float32)
    row_scale = spread_rows(key, 0.6, 1.6)
    values = 0.05 * row_scale * (0.84 * shared_part + 0.55 * noise_part)
    return jnp.clip(values, -0.296875, 0.296875).astype(jnp.bfloat16)


def draw_text_emb(key, part):
    pieces = shared_parts(key)
    key = jax.random.fold_in(key, 12)
    shared_part = mix_rows(key, pieces, 3)
    noise_part = jax.random.normal(jax.random.fold_in(key, 2), (PAIRS, D), jnp.float32)
    row_scale = spread_rows(key, 0.6, 1.6)
    values = 0.05 * row_scale * (0.84 * shared_part + 0.55 * noise_part)
    return jnp.clip(values, -0.296875, 0.296875).astype(jnp.bfloat16)


def place_ends(values, stream_key, low, top_value):
    longest = values.shape.index(max(values.shape))
    spots = []
    for shift in (0, 1):
        where = [jax.random.randint(jax.random.fold_in(stream_key, axis), (), 0, length) for axis, length in enumerate(values.shape)]
        where[longest] = (where[longest] + shift) % values.shape[longest]
        spots.append(tuple(where))
    return values.at[spots[0]].set(low).at[spots[1]].set(top_value)


def cumulative_ranks(number_of, slope):
    loads = [(1 << 20) // math.isqrt(standing ** slope) + 1 for standing in range(1, number_of + 1)]
    scale = 1 + sum(loads) // (1 << 30)
    return np.cumsum(np.array([max(1, weight // scale) for weight in loads]))


def ranked(rng, shape, number_of, skew):
    listing = cumulative_ranks(number_of, skew)
    pick = jax.random.randint(jax.random.fold_in(rng, 1), shape, 0, int(listing[number_of - 1]))
    grade = jnp.searchsorted(jnp.asarray(listing, jnp.int32), pick, side="right")
    return jax.random.permutation(jax.random.fold_in(rng, 2), number_of)[grade].astype(jnp.int32)


def setup_inputs(seed: int = 0) -> dict:
    arg_keys = jax.random.split(jax.random.key(seed), 6)
    return {
        "image_emb": draw_image_emb(jax.random.fold_in(arg_keys[5], 71), 0),
        "text_emb": draw_text_emb(jax.random.fold_in(arg_keys[5], 71), 0),
        "pair_class": place_ends(ranked(arg_keys[2], (PAIRS,), PAIRS // 2, 2), jax.random.fold_in(arg_keys[2], 3), 0, (PAIRS // 2) - 1).astype(jnp.int32),
        "scale": jnp.clip(jax.random.uniform(arg_keys[3], (), jnp.float32, 4.0, 12.0), 4.0, 12.0),
        "shift": jnp.clip(jax.random.uniform(arg_keys[4], (), jnp.float32, -2.0, -0.5), -2.0, -0.5),
    }


def unit_rows(rows):
    wide = rows.astype(jnp.float32)
    inverse = 1.0 / jnp.sqrt(lax.optimization_barrier(jnp.sum(wide * wide, axis=1, keepdims=True)) + 1e-06)
    return (wide * inverse, inverse)

def project_back(unit, inverse, pull):
    inner = lax.optimization_barrier(jnp.sum(unit * pull, axis=1, keepdims=True))
    return (pull - unit * inner) * inverse

def reference(image_emb, text_emb, pair_class, scale, shift):
    image_unit, image_inv = unit_rows(image_emb)
    text_unit, text_inv = unit_rows(text_emb)
    image_half = image_unit.astype(jnp.bfloat16)
    text_half = text_unit.astype(jnp.bfloat16)
    logits = scale * jnp.dot(image_half, text_half.T, preferred_element_type=jnp.float32) + shift
    sign = jnp.where(pair_class[:, None] == pair_class[None, :], 1.0, -1.0).astype(jnp.float32)
    margin = sign * logits
    total = image_emb.shape[0]
    row_loss = -lax.optimization_barrier(jnp.sum(jax.nn.log_sigmoid(margin), axis=1)) / total
    coef = (-sign * jax.nn.sigmoid(-margin) * scale).astype(jnp.bfloat16)
    image_pull = jnp.dot(coef, text_half, preferred_element_type=jnp.float32)
    text_pull = jnp.dot(coef.T, image_half, preferred_element_type=jnp.float32)
    grad_image = project_back(image_unit, image_inv, image_pull)
    grad_text = project_back(text_unit, text_inv, text_pull)
    return (row_loss, grad_image, grad_text)
```

```python
import jax
import jax.numpy as jnp
from jax import lax
from jax.experimental import pallas as pl
from jax.experimental.pallas import tpu as pltpu
from jax.sharding import PartitionSpec as P

GATHER_LIMIT_BYTES = 8 << 20
DIGITS = 4
LANES = 128


def unit_rows(rows):
    wide = rows.astype(jnp.float32)
    inverse = 1.0 / jnp.sqrt(jnp.sum(wide * wide, axis=1, keepdims=True) + 1e-06)
    return (wide * inverse, inverse)


def project_back(unit, inverse, pull):
    inner = jnp.sum(unit * pull, axis=1, keepdims=True)
    return (pull - unit * inner) * inverse


def tile_terms(rows_half, row_class, cols_half, col_class, scale, shift):
    logits = (
        scale
        * lax.dot_general(
            rows_half, cols_half, (((1,), (1,)), ((), ())), preferred_element_type=jnp.float32
        )
        + shift
    )
    sign = jnp.where(row_class[:, None] == col_class[None, :], 1.0, -1.0).astype(jnp.float32)
    margin = sign * logits
    loss_part = -jnp.sum(jax.nn.log_sigmoid(margin), axis=1)
    coef = (-sign * jax.nn.sigmoid(-margin) * scale).astype(jnp.bfloat16)
    return (coef, loss_part)


def tile_plan(image_emb, text_emb, pair_class, scale, shift):
    image_unit, image_inv = unit_rows(image_emb)
    text_unit, text_inv = unit_rows(text_emb)
    own_rows = text_emb.shape[0]
    pairs = own_rows * lax.axis_size("img") * lax.axis_size("txt")
    text_half = text_unit.astype(jnp.bfloat16)
    rows_half, row_class = (
        lax.all_gather(image_unit.astype(jnp.bfloat16), "txt", axis=0, tiled=True),
        lax.all_gather(pair_class, "txt", axis=0, tiled=True),
    )
    cols_half, col_class = (
        lax.all_gather(text_half, "img", axis=0, tiled=True),
        lax.all_gather(pair_class, "img", axis=0, tiled=True),
    )
    coef, loss_part = tile_terms(rows_half, row_class, cols_half, col_class, scale, shift)
    image_pull = jnp.dot(coef, cols_half, preferred_element_type=jnp.float32)
    text_pull = lax.psum_scatter(
        lax.dot_general(
            coef, rows_half, (((0,), (0,)), ((), ())), preferred_element_type=jnp.float32
        ),
        "img",
        scatter_dimension=0,
        tiled=True,
    )
    image_sum, loss_sum = (
        lax.psum_scatter(image_pull, "txt", scatter_dimension=0, tiled=True),
        lax.psum_scatter(loss_part, "txt", scatter_dimension=0, tiled=True),
    )
    row_loss = loss_sum / pairs
    grad_image = project_back(image_unit, image_inv, image_sum)
    grad_text = project_back(text_unit, text_inv, text_pull)
    return (row_loss, grad_image, grad_text)


def class_digits(class_ref, rows):
    row = lax.broadcasted_iota(jnp.int32, (rows, LANES), 0)
    lane = lax.broadcasted_iota(jnp.int32, (rows, LANES), 1)
    spread = jnp.zeros((rows, LANES), jnp.int32)
    for i in range(rows):
        spread = jnp.where(row == i, class_ref[i], spread)
    digit = lax.shift_right_logical(spread, 8 * jnp.minimum(lane, DIGITS - 1)) & 255
    return jnp.where(lane < DIGITS, digit, 0).astype(jnp.float32)


def pack_kernel(image_ref, text_ref, class_ref, packed_ref):
    rows, depth = image_ref.shape
    packed_ref[:, :depth] = unit_rows(image_ref[...])[0].astype(jnp.bfloat16)
    packed_ref[:, depth : 2 * depth] = unit_rows(text_ref[...])[0].astype(jnp.bfloat16)
    packed_ref[:, 2 * depth :] = class_digits(class_ref, rows).astype(jnp.bfloat16)


def side(own_half, others, sign, scale, shift):
    logits = (
        scale
        * lax.dot_general(
            own_half, others, (((1,), (1,)), ((), ())), preferred_element_type=jnp.float32
        )
        + shift
    )
    margin = sign * logits
    small = jnp.exp(-jnp.abs(margin))
    over = 1.0 / (1.0 + small)
    coef = -sign * jnp.where(margin >= 0, small * over, over) * scale
    pull = jnp.dot(coef.astype(jnp.bfloat16), others, preferred_element_type=jnp.float32)
    return margin, small, pull


def main_kernel(
    image_ref, text_ref, class_ref, scale_ref, shift_ref, all_ref, loss_ref, grad_image_ref, grad_text_ref
):
    rows, depth = image_ref.shape
    pairs = all_ref.shape[0]
    scale, shift = scale_ref[0], shift_ref[0]
    image_unit, image_inv = unit_rows(image_ref[...])
    text_unit, text_inv = unit_rows(text_ref[...])

    own_digits = class_digits(class_ref, rows)
    pick = (
        lax.broadcasted_iota(jnp.int32, (8, LANES), 0)
        == lax.broadcasted_iota(jnp.int32, (8, LANES), 1)
    )
    all_digits = lax.dot_general(
        pick.astype(jnp.bfloat16),
        all_ref[:, 2 * depth :],
        (((1,), (1,)), ((), ())),
        preferred_element_type=jnp.float32,
    )
    same = None
    for k in range(DIGITS):
        equal = own_digits[:, k : k + 1] == all_digits[k : k + 1, :]
        same = equal if same is None else same & equal
    sign = jnp.where(same, 1.0, -1.0).astype(jnp.float32)

    margin, small, image_pull = side(
        image_unit.astype(jnp.bfloat16), all_ref[:, depth : 2 * depth], sign, scale, shift
    )
    grad_image_ref[...] = project_back(image_unit, image_inv, image_pull)
    loss = jnp.log1p(small) - jnp.minimum(margin, 0.0)
    folded = loss[:, :LANES]
    for start in range(LANES, pairs, LANES):
        folded = folded + loss[:, start : start + LANES]
    loss_ref[...] = jnp.sum(folded.T, axis=0, keepdims=True) / pairs

    _, _, text_pull = side(
        text_unit.astype(jnp.bfloat16), all_ref[:, :depth], sign, scale, shift
    )
    grad_text_ref[...] = project_back(text_unit, text_inv, text_pull)


def gather_plan(image_emb, text_emb, pair_class, scale, shift):
    rows, depth = image_emb.shape
    pairs = rows * lax.axis_size("img") * lax.axis_size("txt")
    vmem = pl.BlockSpec(memory_space=pltpu.VMEM)
    smem = pl.BlockSpec(memory_space=pltpu.SMEM)
    width = 2 * depth + LANES
    packed = pl.pallas_call(
        pack_kernel,
        out_shape=jax.ShapeDtypeStruct((rows, width), jnp.bfloat16),
        in_specs=[vmem, vmem, smem],
        out_specs=vmem,
        name="pack",
    )(image_emb, text_emb, pair_class)
    everything = lax.all_gather(packed, ("img", "txt"), axis=0, tiled=True)
    loss, grad_image, grad_text = pl.pallas_call(
        main_kernel,
        out_shape=(
            jax.ShapeDtypeStruct((1, rows), jnp.float32),
            jax.ShapeDtypeStruct((rows, depth), jnp.float32),
            jax.ShapeDtypeStruct((rows, depth), jnp.float32),
        ),
        in_specs=[vmem, vmem, smem, smem, smem, vmem],
        out_specs=(vmem, vmem, vmem),
        compiler_params=pltpu.CompilerParams(vmem_limit_bytes=32 << 20),
        name="contrast",
    )(image_emb, text_emb, pair_class, scale[None], shift[None], everything)
    return (loss[0], grad_image, grad_text)


def local(image_emb, text_emb, pair_class, scale, shift):
    rows, depth = image_emb.shape
    pairs = rows * lax.axis_size("img") * lax.axis_size("txt")
    if 2 * pairs * depth * image_emb.dtype.itemsize <= GATHER_LIMIT_BYTES:
        return gather_plan(image_emb, text_emb, pair_class, scale, shift)
    return tile_plan(image_emb, text_emb, pair_class, scale, shift)


def solution(mesh):
    in_specs = (P(("img", "txt"), None), P(("img", "txt"), None), P(("img", "txt")), P(), P())
    out_specs = (P(("img", "txt")), P(("img", "txt"), None), P(("img", "txt"), None))
    return jax.shard_map(local, mesh=mesh, in_specs=in_specs, out_specs=out_specs, check_vma=False)
```

```python
import jax
import jax.numpy as jnp
from jax import lax
from jax.experimental import pallas as pl
from jax.experimental.pallas import tpu as pltpu
from jax.sharding import PartitionSpec as P

GATHER_LIMIT_BYTES = 8 << 20
DIGITS = 4
LANES = 128


def unit_rows(rows):
    wide = rows.astype(jnp.float32)
    inverse = 1.0 / jnp.sqrt(jnp.sum(wide * wide, axis=1, keepdims=True) + 1e-06)
    return (wide * inverse, inverse)


def project_back(unit, inverse, pull):
    inner = jnp.sum(unit * pull, axis=1, keepdims=True)
    return (pull - unit * inner) * inverse


def tile_terms(rows_half, row_class, cols_half, col_class, scale, shift):
    logits = (
        scale
        * lax.dot_general(
            rows_half, cols_half, (((1,), (1,)), ((), ())), preferred_element_type=jnp.float32
        )
        + shift
    )
    sign = jnp.where(row_class[:, None] == col_class[None, :], 1.0, -1.0).astype(jnp.float32)
    margin = sign * logits
    loss_part = -jnp.sum(jax.nn.log_sigmoid(margin), axis=1)
    coef = (-sign * jax.nn.sigmoid(-margin) * scale).astype(jnp.bfloat16)
    return (coef, loss_part)


def tile_plan(image_emb, text_emb, pair_class, scale, shift):
    image_unit, image_inv = unit_rows(image_emb)
    text_unit, text_inv = unit_rows(text_emb)
    own_rows = text_emb.shape[0]
    pairs = own_rows * lax.axis_size("img") * lax.axis_size("txt")
    text_half = text_unit.astype(jnp.bfloat16)
    rows_half, row_class = (
        lax.all_gather(image_unit.astype(jnp.bfloat16), "txt", axis=0, tiled=True),
        lax.all_gather(pair_class, "txt", axis=0, tiled=True),
    )
    cols_half, col_class = (
        lax.all_gather(text_half, "img", axis=0, tiled=True),
        lax.all_gather(pair_class, "img", axis=0, tiled=True),
    )
    coef, loss_part = tile_terms(rows_half, row_class, cols_half, col_class, scale, shift)
    image_pull = jnp.dot(coef, cols_half, preferred_element_type=jnp.float32)
    text_pull = lax.psum_scatter(
        lax.dot_general(
            coef, rows_half, (((0,), (0,)), ((), ())), preferred_element_type=jnp.float32
        ),
        "img",
        scatter_dimension=0,
        tiled=True,
    )
    image_sum, loss_sum = (
        lax.psum_scatter(image_pull, "txt", scatter_dimension=0, tiled=True),
        lax.psum_scatter(loss_part, "txt", scatter_dimension=0, tiled=True),
    )
    row_loss = loss_sum / pairs
    grad_image = project_back(image_unit, image_inv, image_sum)
    grad_text = project_back(text_unit, text_inv, text_pull)
    return (row_loss, grad_image, grad_text)


def class_digits(class_ref, rows):
    row = lax.broadcasted_iota(jnp.int32, (rows, LANES), 0)
    lane = lax.broadcasted_iota(jnp.int32, (rows, LANES), 1)
    spread = jnp.zeros((rows, LANES), jnp.int32)
    for i in range(rows):
        spread = jnp.where(row == i, class_ref[i], spread)
    digit = lax.shift_right_logical(spread, 8 * jnp.minimum(lane, DIGITS - 1)) & 255
    return jnp.where(lane < DIGITS, digit, 0).astype(jnp.float32)


def pack_kernel(image_ref, text_ref, class_ref, packed_ref):
    rows, depth = image_ref.shape
    packed_ref[:, :depth] = unit_rows(image_ref[...])[0].astype(jnp.bfloat16)
    packed_ref[:, depth : 2 * depth] = unit_rows(text_ref[...])[0].astype(jnp.bfloat16)
    packed_ref[:, 2 * depth :] = class_digits(class_ref, rows).astype(jnp.bfloat16)


def side(own_half, others, sign, scale, shift):
    logits = (
        scale
        * lax.dot_general(
            own_half, others, (((1,), (1,)), ((), ())), preferred_element_type=jnp.float32
        )
        + shift
    )
    margin = sign * logits
    small = jnp.exp(-jnp.abs(margin))
    over = 1.0 / (1.0 + small)
    coef = -sign * jnp.where(margin >= 0, small * over, over) * scale
    pull = jnp.dot(coef.astype(jnp.bfloat16), others, preferred_element_type=jnp.float32)
    return margin, small, pull


def main_kernel(
    image_ref, text_ref, class_ref, scale_ref, shift_ref, *refs
):
    block_refs, (loss_ref, grad_image_ref, grad_text_ref, all_ref) = refs[:-4], refs[-4:]
    rows, depth = image_ref.shape
    pairs = all_ref.shape[0]
    start = 0
    for block_ref in block_refs:
        all_ref[start : start + block_ref.shape[0], :] = block_ref[...]
        start += block_ref.shape[0]
    scale, shift = scale_ref[0], shift_ref[0]
    image_unit, image_inv = unit_rows(image_ref[...])
    text_unit, text_inv = unit_rows(text_ref[...])

    own_digits = class_digits(class_ref, rows)
    pick = (
        lax.broadcasted_iota(jnp.int32, (8, LANES), 0)
        == lax.broadcasted_iota(jnp.int32, (8, LANES), 1)
    )
    all_digits = lax.dot_general(
        pick.astype(jnp.bfloat16),
        all_ref[:, 2 * depth :],
        (((1,), (1,)), ((), ())),
        preferred_element_type=jnp.float32,
    )
    same = None
    for k in range(DIGITS):
        equal = own_digits[:, k : k + 1] == all_digits[k : k + 1, :]
        same = equal if same is None else same & equal
    sign = jnp.where(same, 1.0, -1.0).astype(jnp.float32)

    margin, small, image_pull = side(
        image_unit.astype(jnp.bfloat16), all_ref[:, depth : 2 * depth], sign, scale, shift
    )
    grad_image_ref[...] = project_back(image_unit, image_inv, image_pull)
    loss = jnp.log1p(small) - jnp.minimum(margin, 0.0)
    folded = loss[:, :LANES]
    for start in range(LANES, pairs, LANES):
        folded = folded + loss[:, start : start + LANES]
    loss_ref[...] = jnp.sum(folded.T, axis=0, keepdims=True) / pairs

    _, _, text_pull = side(
        text_unit.astype(jnp.bfloat16), all_ref[:, :depth], sign, scale, shift
    )
    grad_text_ref[...] = project_back(text_unit, text_inv, text_pull)


def exchange(rows, n, stride):
    return lax.ppermute(rows, ("img", "txt"), [(i, i ^ stride) for i in range(n)])


def spread(rows, n):
    quarter = n // 4
    line = [rows] + [exchange(rows, n, k * quarter) for k in (1, 2, 3)]
    line = jnp.concatenate(line, axis=0)
    plane = [line] + [exchange(line, n, k) for k in (quarter // 2, 1, quarter // 2 + 1)]
    return plane + [exchange(block, n, quarter // 4) for block in plane]


def gather_plan(image_emb, text_emb, pair_class, scale, shift):
    rows, depth = image_emb.shape
    pairs = rows * lax.axis_size("img") * lax.axis_size("txt")
    vmem = pl.BlockSpec(memory_space=pltpu.VMEM)
    smem = pl.BlockSpec(memory_space=pltpu.SMEM)
    width = 2 * depth + LANES
    packed = pl.pallas_call(
        pack_kernel,
        out_shape=jax.ShapeDtypeStruct((rows, width), jnp.bfloat16),
        in_specs=[vmem, vmem, smem],
        out_specs=vmem,
        name="pack",
    )(image_emb, text_emb, pair_class)
    blocks = spread(packed, lax.axis_size("img") * lax.axis_size("txt"))
    loss, grad_image, grad_text = pl.pallas_call(
        main_kernel,
        out_shape=(
            jax.ShapeDtypeStruct((1, rows), jnp.float32),
            jax.ShapeDtypeStruct((rows, depth), jnp.float32),
            jax.ShapeDtypeStruct((rows, depth), jnp.float32),
        ),
        in_specs=[vmem, vmem, smem, smem, smem] + [vmem] * len(blocks),
        out_specs=(vmem, vmem, vmem),
        scratch_shapes=[pltpu.VMEM((pairs, width), jnp.bfloat16)],
        compiler_params=pltpu.CompilerParams(vmem_limit_bytes=32 << 20),
        name="contrast",
    )(image_emb, text_emb, pair_class, scale[None], shift[None], *blocks)
    return (loss[0], grad_image, grad_text)


def local(image_emb, text_emb, pair_class, scale, shift):
    rows, depth = image_emb.shape
    pairs = rows * lax.axis_size("img") * lax.axis_size("txt")
    devices = lax.axis_size("img") * lax.axis_size("txt")
    small = 2 * pairs * depth * image_emb.dtype.itemsize <= GATHER_LIMIT_BYTES
    if small and devices == 32:
        return gather_plan(image_emb, text_emb, pair_class, scale, shift)
    return tile_plan(image_emb, text_emb, pair_class, scale, shift)


def solution(mesh):
    in_specs = (P(("img", "txt"), None), P(("img", "txt"), None), P(("img", "txt")), P(), P())
    out_specs = (P(("img", "txt")), P(("img", "txt"), None), P(("img", "txt"), None))
    return jax.shard_map(local, mesh=mesh, in_specs=in_specs, out_specs=out_specs, check_vma=False)
```

```python
import jax
import jax.numpy as jnp
from jax import lax
from jax.experimental import pallas as pl
from jax.experimental.pallas import tpu as pltpu
from jax.sharding import PartitionSpec as P

AXES = ("img", "txt")
DIGITS = 4
LANES = 128
TOP = 32767.0


def unit_rows(rows):
    wide = rows.astype(jnp.float32)
    inverse = 1.0 / jnp.sqrt(jnp.sum(wide * wide, axis=1, keepdims=True) + 1e-06)
    return (wide * inverse, inverse)


def project_back(unit, inverse, pull):
    inner = jnp.sum(unit * pull, axis=1, keepdims=True)
    return (pull - unit * inner) * inverse


def class_digits(class_ref, rows):
    row = lax.broadcasted_iota(jnp.int32, (rows, LANES), 0)
    lane = lax.broadcasted_iota(jnp.int32, (rows, LANES), 1)
    spread = jnp.zeros((rows, LANES), jnp.int32)
    for i in range(rows):
        spread = jnp.where(row == i, class_ref[i], spread)
    digit = lax.shift_right_logical(spread, 8 * jnp.minimum(lane, DIGITS - 1)) & 255
    return jnp.where(lane < DIGITS, digit, 0).astype(jnp.float32).astype(jnp.bfloat16)


def pack_kernel(image_ref, text_ref, class_ref, image_out, text_out):
    rows, depth = image_ref.shape
    digits = class_digits(class_ref, rows)
    for source, out in ((image_ref, image_out), (text_ref, text_out)):
        half = unit_rows(source[...])[0].astype(jnp.bfloat16)
        for k in range(out.shape[0]):
            out[k, :, :depth] = half
            out[k, :, depth:] = digits


def power_above(size):
    return jnp.ceil(jnp.log2(jnp.maximum(size, 1e-30)) + 0.01)


def code(values, power):
    steps = jnp.clip(jnp.round(values * (TOP / jnp.exp2(power))), -TOP, TOP)
    return steps.astype(jnp.int32).astype(jnp.int16)


def decode(steps, power):
    return steps.astype(jnp.int32).astype(jnp.float32) * (jnp.exp2(power) * (1.0 / TOP))


def put_rows(out, pull, extra):
    blocks, rows, width = out.shape
    depth = width - LANES
    power = power_above(jnp.max(jnp.abs(pull), axis=1, keepdims=True))
    steps = code(pull, power)
    lane = lax.broadcasted_iota(jnp.int32, (blocks * rows, LANES), 1)
    tail = jnp.where(lane == 0, power, 0.0)
    if extra is not None:
        loss_power = power_above(extra)
        tail = jnp.where(lane == 1, loss_power, tail)
        tail = jnp.where(lane == 2, jnp.round(extra * (TOP / jnp.exp2(loss_power))), tail)
    tail = tail.astype(jnp.int32).astype(jnp.int16)
    for k in range(blocks):
        out[k, :, :depth] = steps[k * rows : (k + 1) * rows]
        out[k, :, depth:] = tail[k * rows : (k + 1) * rows]


def tile_kernel(image_ref, text_ref, scale_ref, shift_ref, image_out, text_out):
    a, rows, width = image_ref.shape
    b = text_ref.shape[0]
    depth = width - LANES
    scale, shift = scale_ref[0], shift_ref[0]
    image = image_ref[...].reshape(a * rows, width)
    text = text_ref[...].reshape(b * rows, width)
    logits = (
        scale
        * lax.dot_general(
            image[:, :depth],
            text[:, :depth],
            (((1,), (1,)), ((), ())),
            preferred_element_type=jnp.float32,
        )
        + shift
    )
    pick = (
        lax.broadcasted_iota(jnp.int32, (8, LANES), 0)
        == lax.broadcasted_iota(jnp.int32, (8, LANES), 1)
    )
    text_digits = lax.dot_general(
        pick.astype(jnp.bfloat16),
        text[:, depth:],
        (((1,), (1,)), ((), ())),
        preferred_element_type=jnp.float32,
    )
    image_digits = image[:, depth:].astype(jnp.float32)
    same = None
    for k in range(DIGITS):
        equal = image_digits[:, k : k + 1] == text_digits[k : k + 1, :]
        same = equal if same is None else same & equal
    sign = jnp.where(same, 1.0, -1.0).astype(jnp.float32)
    margin = sign * logits
    small = jnp.exp(-jnp.abs(margin))
    over = 1.0 / (1.0 + small)
    coef = -sign * jnp.where(margin >= 0, small * over, over) * scale
    image_pull = jnp.dot(
        coef.astype(jnp.bfloat16), text[:, :depth], preferred_element_type=jnp.float32
    )
    text_pull = jnp.dot(
        coef.T.astype(jnp.bfloat16), image[:, :depth], preferred_element_type=jnp.float32
    )
    loss = jnp.sum(jnp.log1p(small) - jnp.minimum(margin, 0.0), axis=1, keepdims=True)
    put_rows(image_out, image_pull, loss)
    put_rows(text_out, text_pull, None)


def final_kernel(image_ref, text_ref, image_parts, text_parts, loss_ref, grad_image_ref, grad_text_ref):
    rows, depth = image_ref.shape
    pairs = rows * image_parts.shape[0] * text_parts.shape[0]
    for source, parts, out in (
        (image_ref, image_parts, grad_image_ref),
        (text_ref, text_parts, grad_text_ref),
    ):
        unit, inverse = unit_rows(source[...])
        pull = jnp.zeros((rows, depth), jnp.float32)
        loss = jnp.zeros((rows, 1), jnp.float32)
        for k in range(parts.shape[0]):
            tail = parts[k, :, depth:].astype(jnp.int32).astype(jnp.float32)
            pull = pull + decode(parts[k, :, :depth], tail[:, 0:1])
            loss = loss + tail[:, 2:3] * (jnp.exp2(tail[:, 1:2]) * (1.0 / TOP))
        out[...] = project_back(unit, inverse, pull)
        if out is grad_image_ref:
            row = lax.broadcasted_iota(jnp.int32, (rows, rows), 0)
            column = lax.broadcasted_iota(jnp.int32, (rows, rows), 1)
            across = jnp.where(row == column, loss / pairs, 0.0)
            loss_ref[...] = jnp.sum(across, axis=0, keepdims=True)


def local(image_emb, text_emb, pair_class, scale, shift):
    rows, depth = image_emb.shape
    n = lax.axis_size("img") * lax.axis_size("txt")
    b = min(d for d in range(1, n + 1) if n % d == 0 and d * d >= n)
    a = n // b
    along_a = [[i * b + j for i in range(a)] for j in range(b)]
    along_b = [[i * b + j for j in range(b)] for i in range(a)]
    width = depth + LANES
    vmem = pl.BlockSpec(memory_space=pltpu.VMEM)
    smem = pl.BlockSpec(memory_space=pltpu.SMEM)
    params = pltpu.CompilerParams(vmem_limit_bytes=32 << 20)

    def swap(blocks, groups):
        return lax.all_to_all(blocks, AXES, 0, 0, axis_index_groups=groups)

    image_rows, text_rows = pl.pallas_call(
        pack_kernel,
        out_shape=(
            jax.ShapeDtypeStruct((a, rows, width), jnp.bfloat16),
            jax.ShapeDtypeStruct((b, rows, width), jnp.bfloat16),
        ),
        in_specs=[vmem, vmem, smem],
        out_specs=(vmem, vmem),
        compiler_params=params,
        name="pack",
    )(image_emb, text_emb, pair_class)
    image_parts, text_parts = pl.pallas_call(
        tile_kernel,
        out_shape=(
            jax.ShapeDtypeStruct((a, rows, width), jnp.int16),
            jax.ShapeDtypeStruct((b, rows, width), jnp.int16),
        ),
        in_specs=[vmem, vmem, smem, smem],
        out_specs=(vmem, vmem),
        compiler_params=params,
        name="tile",
    )(swap(image_rows, along_a), swap(text_rows, along_b), scale[None], shift[None])
    loss, grad_image, grad_text = pl.pallas_call(
        final_kernel,
        out_shape=(
            jax.ShapeDtypeStruct((1, rows), jnp.float32),
            jax.ShapeDtypeStruct((rows, depth), jnp.float32),
            jax.ShapeDtypeStruct((rows, depth), jnp.float32),
        ),
        in_specs=[vmem, vmem, vmem, vmem],
        out_specs=(vmem, vmem, vmem),
        compiler_params=params,
        name="final",
    )(image_emb, text_emb, swap(image_parts, along_a), swap(text_parts, along_b))
    return (loss[0], grad_image, grad_text)


def solution(mesh):
    in_specs = (P(AXES, None), P(AXES, None), P(AXES), P(), P())
    out_specs = (P(AXES), P(AXES, None), P(AXES, None))
    return jax.shard_map(local, mesh=mesh, in_specs=in_specs, out_specs=out_specs, check_vma=False)
```

```python
import functools

import jax
import jax.numpy as jnp
from jax import lax
from jax.experimental import pallas as pl
from jax.experimental.pallas import tpu as pltpu
from jax.sharding import PartitionSpec as P

AXES = ("img", "txt")
DIGITS = 4
LANES = 128
TOP = 32767.0


def unit_rows(rows):
    wide = rows.astype(jnp.float32)
    inverse = 1.0 / jnp.sqrt(jnp.sum(wide * wide, axis=1, keepdims=True) + 1e-06)
    return (wide * inverse, inverse)


def project_back(unit, inverse, pull):
    inner = jnp.sum(unit * pull, axis=1, keepdims=True)
    return (pull - unit * inner) * inverse


def class_digits(class_ref, rows):
    row = lax.broadcasted_iota(jnp.int32, (rows, LANES), 0)
    lane = lax.broadcasted_iota(jnp.int32, (rows, LANES), 1)
    spread = jnp.zeros((rows, LANES), jnp.int32)
    for i in range(rows):
        spread = jnp.where(row == i, class_ref[i], spread)
    digit = lax.shift_right_logical(spread, 8 * jnp.minimum(lane, DIGITS - 1)) & 255
    return jnp.where(lane < DIGITS, digit, 0).astype(jnp.float32).astype(jnp.bfloat16)


def pack_kernel(image_ref, text_ref, class_ref, image_out, text_out):
    rows, depth = image_ref.shape
    digits = class_digits(class_ref, rows)
    for source, out in ((image_ref, image_out), (text_ref, text_out)):
        half = unit_rows(source[...])[0].astype(jnp.bfloat16)
        out[:, :depth] = half
        out[:, depth:] = digits


def power_above(size):
    return jnp.ceil(jnp.log2(jnp.maximum(size, 1e-30)) + 0.01)


def code(values, power):
    steps = jnp.clip(jnp.round(values * (TOP / jnp.exp2(power))), -TOP, TOP)
    return steps.astype(jnp.int32).astype(jnp.int16)


def decode(steps, power):
    return steps.astype(jnp.int32).astype(jnp.float32) * (jnp.exp2(power) * (1.0 / TOP))


def put_rows(outs, pull, extra):
    blocks, (rows, width) = len(outs), outs[0].shape
    depth = width - LANES
    power = power_above(jnp.max(jnp.abs(pull), axis=1, keepdims=True))
    steps = code(pull, power)
    lane = lax.broadcasted_iota(jnp.int32, (blocks * rows, LANES), 1)
    tail = jnp.where(lane == 0, power, 0.0)
    if extra is not None:
        loss_power = power_above(extra)
        tail = jnp.where(lane == 1, loss_power, tail)
        tail = jnp.where(lane == 2, jnp.round(extra * (TOP / jnp.exp2(loss_power))), tail)
    tail = tail.astype(jnp.int32).astype(jnp.int16)
    for k, out in enumerate(outs):
        out[:, :depth] = steps[k * rows : (k + 1) * rows]
        out[:, depth:] = tail[k * rows : (k + 1) * rows]


def tile_kernel(a, b, scale_ref, shift_ref, *refs):
    image_refs, text_refs = refs[:a], refs[a : a + b]
    image_outs, text_outs = refs[a + b : 2 * a + b], refs[2 * a + b :]
    depth = image_refs[0].shape[1] - LANES
    scale, shift = scale_ref[0], shift_ref[0]
    image = jnp.concatenate([ref[...] for ref in image_refs], axis=0)
    text = jnp.concatenate([ref[...] for ref in text_refs], axis=0)
    logits = (
        scale
        * lax.dot_general(
            image[:, :depth],
            text[:, :depth],
            (((1,), (1,)), ((), ())),
            preferred_element_type=jnp.float32,
        )
        + shift
    )
    pick = (
        lax.broadcasted_iota(jnp.int32, (8, LANES), 0)
        == lax.broadcasted_iota(jnp.int32, (8, LANES), 1)
    )
    text_digits = lax.dot_general(
        pick.astype(jnp.bfloat16),
        text[:, depth:],
        (((1,), (1,)), ((), ())),
        preferred_element_type=jnp.float32,
    )
    image_digits = image[:, depth:].astype(jnp.float32)
    same = None
    for k in range(DIGITS):
        equal = image_digits[:, k : k + 1] == text_digits[k : k + 1, :]
        same = equal if same is None else same & equal
    sign = jnp.where(same, 1.0, -1.0).astype(jnp.float32)
    margin = sign * logits
    small = jnp.exp(-jnp.abs(margin))
    over = 1.0 / (1.0 + small)
    coef = -sign * jnp.where(margin >= 0, small * over, over) * scale
    image_pull = jnp.dot(
        coef.astype(jnp.bfloat16), text[:, :depth], preferred_element_type=jnp.float32
    )
    text_pull = jnp.dot(
        coef.T.astype(jnp.bfloat16), image[:, :depth], preferred_element_type=jnp.float32
    )
    loss = jnp.sum(jnp.log1p(small) - jnp.minimum(margin, 0.0), axis=1, keepdims=True)
    put_rows(image_outs, image_pull, loss)
    put_rows(text_outs, text_pull, None)


def final_kernel(a, b, image_ref, text_ref, *refs):
    image_parts, text_parts = refs[:a], refs[a : a + b]
    loss_ref, grad_image_ref, grad_text_ref = refs[a + b :]
    rows, depth = image_ref.shape
    pairs = rows * a * b
    for source, parts, out in (
        (image_ref, image_parts, grad_image_ref),
        (text_ref, text_parts, grad_text_ref),
    ):
        unit, inverse = unit_rows(source[...])
        pull = jnp.zeros((rows, depth), jnp.float32)
        loss = jnp.zeros((rows, 1), jnp.float32)
        for part in parts:
            tail = part[:, depth:].astype(jnp.int32).astype(jnp.float32)
            pull = pull + decode(part[:, :depth], tail[:, 0:1])
            loss = loss + tail[:, 2:3] * (jnp.exp2(tail[:, 1:2]) * (1.0 / TOP))
        out[...] = project_back(unit, inverse, pull)
        if out is grad_image_ref:
            row = lax.broadcasted_iota(jnp.int32, (rows, rows), 0)
            column = lax.broadcasted_iota(jnp.int32, (rows, rows), 1)
            across = jnp.where(row == column, loss / pairs, 0.0)
            loss_ref[...] = jnp.sum(across, axis=0, keepdims=True)


def partner(place, k, size):
    return place ^ k if size & (size - 1) == 0 else (place + k) % size


def local(image_emb, text_emb, pair_class, scale, shift):
    rows, depth = image_emb.shape
    n = lax.axis_size("img") * lax.axis_size("txt")
    b = min(d for d in range(1, n + 1) if n % d == 0 and d * d >= n)
    a = n // b
    width = depth + LANES
    vmem = pl.BlockSpec(memory_space=pltpu.VMEM)
    smem = pl.BlockSpec(memory_space=pltpu.SMEM)
    params = pltpu.CompilerParams(vmem_limit_bytes=32 << 20)

    def along_a(i, k):
        return partner(i // b, k, a) * b + i % b

    def along_b(i, k):
        return i // b * b + partner(i % b, k, b)

    def collect(block, size, along):
        pairs = [[(along(i, k), i) for i in range(n)] for k in range(1, size)]
        return [block] + [lax.ppermute(block, AXES, pair) for pair in pairs]

    def give_back(blocks, along):
        pairs = [[(i, along(i, k)) for i in range(n)] for k in range(len(blocks))]
        return blocks[:1] + [lax.ppermute(x, AXES, p) for x, p in zip(blocks[1:], pairs[1:])]

    image_rows, text_rows = pl.pallas_call(
        pack_kernel,
        out_shape=(jax.ShapeDtypeStruct((rows, width), jnp.bfloat16),) * 2,
        in_specs=[vmem, vmem, smem],
        out_specs=(vmem, vmem),
        compiler_params=params,
        name="pack",
    )(image_emb, text_emb, pair_class)
    images, texts = collect(image_rows, a, along_a), collect(text_rows, b, along_b)
    parts = pl.pallas_call(
        functools.partial(tile_kernel, a, b),
        out_shape=(jax.ShapeDtypeStruct((rows, width), jnp.int16),) * (a + b),
        in_specs=[smem, smem] + [vmem] * (a + b),
        out_specs=(vmem,) * (a + b),
        compiler_params=params,
        name="tile",
    )(scale[None], shift[None], *images, *texts)
    parts = give_back(list(parts[:a]), along_a) + give_back(list(parts[a:]), along_b)
    loss, grad_image, grad_text = pl.pallas_call(
        functools.partial(final_kernel, a, b),
        out_shape=(
            jax.ShapeDtypeStruct((1, rows), jnp.float32),
            jax.ShapeDtypeStruct((rows, depth), jnp.float32),
            jax.ShapeDtypeStruct((rows, depth), jnp.float32),
        ),
        in_specs=[vmem] * (2 + a + b),
        out_specs=(vmem, vmem, vmem),
        compiler_params=params,
        name="final",
    )(image_emb, text_emb, *parts)
    return (loss[0], grad_image, grad_text)


def solution(mesh):
    in_specs = (P(AXES, None), P(AXES, None), P(AXES), P(), P())
    out_specs = (P(AXES), P(AXES, None), P(AXES, None))
    return jax.shard_map(local, mesh=mesh, in_specs=in_specs, out_specs=out_specs, check_vma=False)
```

```python
import functools
import math

import jax
import jax.numpy as jnp
from jax import lax
from jax.experimental import pallas as pl
from jax.experimental.pallas import tpu as pltpu
from jax.sharding import PartitionSpec as P

AXES = ("img", "txt")
DIGITS = 4
LANES = 128
TOP = 32767.0


def unit_rows(rows):
    wide = rows.astype(jnp.float32)
    inverse = 1.0 / jnp.sqrt(jnp.sum(wide * wide, axis=1, keepdims=True) + 1e-06)
    return (wide * inverse, inverse)


def project_back(unit, inverse, pull):
    inner = jnp.sum(unit * pull, axis=1, keepdims=True)
    return (pull - unit * inner) * inverse


def tile_terms(rows_half, row_class, cols_half, col_class, scale, shift):
    logits = (
        scale
        * lax.dot_general(
            rows_half, cols_half, (((1,), (1,)), ((), ())), preferred_element_type=jnp.float32
        )
        + shift
    )
    sign = jnp.where(row_class[:, None] == col_class[None, :], 1.0, -1.0).astype(jnp.float32)
    margin = sign * logits
    loss_part = -jnp.sum(jax.nn.log_sigmoid(margin), axis=1)
    coef = (-sign * jax.nn.sigmoid(-margin) * scale).astype(jnp.bfloat16)
    return (coef, loss_part)


def tile_plan(image_emb, text_emb, pair_class, scale, shift):
    image_unit, image_inv = unit_rows(image_emb)
    text_unit, text_inv = unit_rows(text_emb)
    own_rows = text_emb.shape[0]
    pairs = own_rows * lax.axis_size("img") * lax.axis_size("txt")
    text_half = text_unit.astype(jnp.bfloat16)
    rows_half, row_class = (
        lax.all_gather(image_unit.astype(jnp.bfloat16), "txt", axis=0, tiled=True),
        lax.all_gather(pair_class, "txt", axis=0, tiled=True),
    )
    cols_half, col_class = (
        lax.all_gather(text_half, "img", axis=0, tiled=True),
        lax.all_gather(pair_class, "img", axis=0, tiled=True),
    )
    coef, loss_part = tile_terms(rows_half, row_class, cols_half, col_class, scale, shift)
    image_pull = jnp.dot(coef, cols_half, preferred_element_type=jnp.float32)
    text_pull = lax.psum_scatter(
        lax.dot_general(
            coef, rows_half, (((0,), (0,)), ((), ())), preferred_element_type=jnp.float32
        ),
        "img",
        scatter_dimension=0,
        tiled=True,
    )
    image_sum, loss_sum = (
        lax.psum_scatter(image_pull, "txt", scatter_dimension=0, tiled=True),
        lax.psum_scatter(loss_part, "txt", scatter_dimension=0, tiled=True),
    )
    row_loss = loss_sum / pairs
    grad_image = project_back(image_unit, image_inv, image_sum)
    grad_text = project_back(text_unit, text_inv, text_pull)
    return (row_loss, grad_image, grad_text)


def on_first_core():
    return lax.rem(lax.axis_index("img"), 2) == 0


def pack_kernel(image_ref, text_ref, got_image_ref, got_text_ref, class_ref, other_class_ref, out_ref):
    rows, depth = image_ref.shape
    first = on_first_core()
    own = jnp.where(first, image_ref[...].astype(jnp.float32), text_ref[...].astype(jnp.float32))
    got = got_image_ref[...].astype(jnp.float32) + got_text_ref[...].astype(jnp.float32)
    row = lax.broadcasted_iota(jnp.int32, (2 * rows, LANES), 0)
    lane = lax.broadcasted_iota(jnp.int32, (2 * rows, LANES), 1)
    spread = jnp.zeros((2 * rows, LANES), jnp.int32)
    for i in range(rows):
        spread = jnp.where(row == i, jnp.where(first, class_ref[i], other_class_ref[i]), spread)
        spread = jnp.where(row == rows + i, jnp.where(first, other_class_ref[i], class_ref[i]), spread)
    digit = lax.shift_right_logical(spread, 8 * jnp.minimum(lane, DIGITS - 1)) & 255
    digit = jnp.where(lane < DIGITS, digit, 0).astype(jnp.float32).astype(jnp.bfloat16)
    out_ref[:rows, :depth] = unit_rows(jnp.where(first, own, got))[0].astype(jnp.bfloat16)
    out_ref[rows:, :depth] = unit_rows(jnp.where(first, got, own))[0].astype(jnp.bfloat16)
    out_ref[:, depth:] = digit


def power_above(size):
    return jnp.ceil(jnp.log2(jnp.maximum(size, 1e-30)) + 0.01)


def code(values, power):
    steps = jnp.clip(jnp.round(values * (TOP / jnp.exp2(power))), -TOP, TOP)
    return steps.astype(jnp.int32).astype(jnp.int16)


def decode(steps, power):
    return steps.astype(jnp.int32).astype(jnp.float32) * (jnp.exp2(power) * (1.0 / TOP))


def put_rows(outs, pull, extra):
    blocks, (rows, width) = len(outs), outs[0].shape
    depth = width - LANES
    power = power_above(jnp.max(jnp.abs(pull), axis=1, keepdims=True))
    steps = code(pull, power)
    lane = lax.broadcasted_iota(jnp.int32, (blocks * rows, LANES), 1)
    tail = jnp.where(lane == 0, power, 0.0)
    if extra is not None:
        loss_power = power_above(extra)
        tail = jnp.where(lane == 1, loss_power, tail)
        tail = jnp.where(lane == 2, jnp.round(extra * (TOP / jnp.exp2(loss_power))), tail)
    tail = tail.astype(jnp.int32).astype(jnp.int16)
    for k, out in enumerate(outs):
        out[:, :depth] = steps[k * rows : (k + 1) * rows]
        out[:, depth:] = tail[k * rows : (k + 1) * rows]


def tile_kernel(count, scale_ref, shift_ref, *refs):
    depth = refs[0].shape[1] - LANES
    scale, shift = scale_ref[0], shift_ref[0]
    lines = jnp.concatenate([ref[...] for ref in refs[:count]], axis=0)
    columns = jnp.concatenate([ref[...] for ref in refs[count : 2 * count]], axis=0)
    logits = (
        scale
        * lax.dot_general(
            lines[:, :depth],
            columns[:, :depth],
            (((1,), (1,)), ((), ())),
            preferred_element_type=jnp.float32,
        )
        + shift
    )
    pick = (
        lax.broadcasted_iota(jnp.int32, (8, LANES), 0)
        == lax.broadcasted_iota(jnp.int32, (8, LANES), 1)
    )
    column_digits = lax.dot_general(
        pick.astype(jnp.bfloat16),
        columns[:, depth:],
        (((1,), (1,)), ((), ())),
        preferred_element_type=jnp.float32,
    )
    line_digits = lines[:, depth:].astype(jnp.float32)
    same = None
    for k in range(DIGITS):
        equal = line_digits[:, k : k + 1] == column_digits[k : k + 1, :]
        same = equal if same is None else same & equal
    sign = jnp.where(same, 1.0, -1.0).astype(jnp.float32)
    margin = sign * logits
    small = jnp.exp(-jnp.abs(margin))
    over = 1.0 / (1.0 + small)
    coef = -sign * jnp.where(margin >= 0, small * over, over) * scale
    pull = jnp.dot(
        coef.astype(jnp.bfloat16), columns[:, :depth], preferred_element_type=jnp.float32
    )
    loss = jnp.sum(jnp.log1p(small) - jnp.minimum(margin, 0.0), axis=1, keepdims=True)
    put_rows(refs[2 * count :], pull, loss)


def final_kernel(count, image_ref, text_ref, *refs):
    mine, others = refs[:count], refs[count : 2 * count]
    loss_ref, grad_image_ref, grad_text_ref = refs[2 * count :]
    rows, depth = image_ref.shape
    pairs = rows * 2 * count * count
    first = on_first_core()
    own_rows = pl.ds(pl.multiple_of(jnp.where(first, 0, rows), rows), rows)

    def total(parts):
        pull = jnp.zeros((rows, depth), jnp.float32)
        loss = jnp.zeros((rows, 1), jnp.float32)
        for part in parts:
            tail = part[own_rows, depth:].astype(jnp.int32).astype(jnp.float32)
            pull = pull + decode(part[own_rows, :depth], tail[:, 0:1])
            loss = loss + tail[:, 2:3] * (jnp.exp2(tail[:, 1:2]) * (1.0 / TOP))
        return pull, loss

    (pull, loss), (other_pull, other_loss) = total(mine), total(others)
    for source, side_pull, out in (
        (image_ref, jnp.where(first, pull, other_pull), grad_image_ref),
        (text_ref, jnp.where(first, other_pull, pull), grad_text_ref),
    ):
        unit, inverse = unit_rows(source[...])
        out[...] = project_back(unit, inverse, side_pull)
    loss = jnp.where(first, loss, other_loss)
    row = lax.broadcasted_iota(jnp.int32, (rows, rows), 0)
    column = lax.broadcasted_iota(jnp.int32, (rows, rows), 1)
    across = jnp.where(row == column, loss / pairs, 0.0)
    loss_ref[...] = jnp.sum(across, axis=0, keepdims=True)


def chip_plan(image_emb, text_emb, pair_class, scale, shift, count):
    rows, depth = image_emb.shape
    lanes = lax.axis_size("txt")
    n = lax.axis_size("img") * lanes
    width = depth + LANES
    vmem = pl.BlockSpec(memory_space=pltpu.VMEM)
    smem = pl.BlockSpec(memory_space=pltpu.SMEM)
    params = pltpu.CompilerParams(vmem_limit_bytes=32 << 20)

    def core(i):
        return i // lanes % 2

    def partner(i, k):
        chip = i // (2 * lanes) * lanes + i % lanes
        chip ^= k if core(i) else k * count
        return (chip // lanes * 2 + core(i)) * lanes + chip % lanes

    def swap(x, senders=(0, 1)):
        pairs = [(i, i ^ lanes) for i in range(n) if core(i) in senders]
        return lax.ppermute(x, AXES, pairs)

    def visit(blocks):
        return [
            lax.ppermute(x, AXES, [(i, partner(i, k)) for i in range(n)])
            for k, x in zip(range(1, count), blocks)
        ]

    mine = pl.pallas_call(
        pack_kernel,
        out_shape=jax.ShapeDtypeStruct((2 * rows, width), jnp.bfloat16),
        in_specs=[vmem] * 4 + [smem, smem],
        out_specs=vmem,
        name="pack",
    )(image_emb, text_emb, swap(image_emb, (1,)), swap(text_emb, (0,)), pair_class, swap(pair_class))
    lines = [mine] + visit([mine] * (count - 1))
    columns = [swap(x) for x in lines]
    parts = pl.pallas_call(
        functools.partial(tile_kernel, count),
        out_shape=(jax.ShapeDtypeStruct((2 * rows, width), jnp.int16),) * count,
        in_specs=[smem, smem] + [vmem] * (2 * count),
        out_specs=(vmem,) * count,
        compiler_params=params,
        name="tile",
    )(scale[None], shift[None], *lines, *columns)
    parts = [parts[0]] + visit(parts[1:])
    loss, grad_image, grad_text = pl.pallas_call(
        functools.partial(final_kernel, count),
        out_shape=(
            jax.ShapeDtypeStruct((1, rows), jnp.float32),
            jax.ShapeDtypeStruct((rows, depth), jnp.float32),
            jax.ShapeDtypeStruct((rows, depth), jnp.float32),
        ),
        in_specs=[vmem] * (2 + 2 * count),
        out_specs=(vmem, vmem, vmem),
        compiler_params=params,
        name="final",
    )(image_emb, text_emb, *parts, *[swap(x) for x in parts])
    return (loss[0], grad_image, grad_text)


def local(image_emb, text_emb, pair_class, scale, shift):
    chips = lax.axis_size("img") * lax.axis_size("txt") // 2
    count = math.isqrt(chips)
    if count * count == chips and count & (count - 1) == 0:
        return chip_plan(image_emb, text_emb, pair_class, scale, shift, count)
    return tile_plan(image_emb, text_emb, pair_class, scale, shift)


def solution(mesh):
    in_specs = (P(AXES, None), P(AXES, None), P(AXES), P(), P())
    out_specs = (P(AXES), P(AXES, None), P(AXES, None))
    return jax.shard_map(local, mesh=mesh, in_specs=in_specs, out_specs=out_specs, check_vma=False)
```

```python
import functools
import math

import jax
import jax.numpy as jnp
from jax import lax
from jax.experimental import pallas as pl
from jax.experimental.pallas import tpu as pltpu
from jax.sharding import PartitionSpec as P

AXES = ("img", "txt")
DIGITS = 4
LANES = 128
TOP = 32767.0


def unit_rows(rows):
    wide = rows.astype(jnp.float32)
    inverse = 1.0 / jnp.sqrt(jnp.sum(wide * wide, axis=1, keepdims=True) + 1e-06)
    return (wide * inverse, inverse)


def project_back(unit, inverse, pull):
    inner = jnp.sum(unit * pull, axis=1, keepdims=True)
    return (pull - unit * inner) * inverse


def tile_terms(rows_half, row_class, cols_half, col_class, scale, shift):
    logits = (
        scale
        * lax.dot_general(
            rows_half, cols_half, (((1,), (1,)), ((), ())), preferred_element_type=jnp.float32
        )
        + shift
    )
    sign = jnp.where(row_class[:, None] == col_class[None, :], 1.0, -1.0).astype(jnp.float32)
    margin = sign * logits
    loss_part = -jnp.sum(jax.nn.log_sigmoid(margin), axis=1)
    coef = (-sign * jax.nn.sigmoid(-margin) * scale).astype(jnp.bfloat16)
    return (coef, loss_part)


def tile_plan(image_emb, text_emb, pair_class, scale, shift):
    image_unit, image_inv = unit_rows(image_emb)
    text_unit, text_inv = unit_rows(text_emb)
    own_rows = text_emb.shape[0]
    pairs = own_rows * lax.axis_size("img") * lax.axis_size("txt")
    text_half = text_unit.astype(jnp.bfloat16)
    rows_half, row_class = (
        lax.all_gather(image_unit.astype(jnp.bfloat16), "txt", axis=0, tiled=True),
        lax.all_gather(pair_class, "txt", axis=0, tiled=True),
    )
    cols_half, col_class = (
        lax.all_gather(text_half, "img", axis=0, tiled=True),
        lax.all_gather(pair_class, "img", axis=0, tiled=True),
    )
    coef, loss_part = tile_terms(rows_half, row_class, cols_half, col_class, scale, shift)
    image_pull = jnp.dot(coef, cols_half, preferred_element_type=jnp.float32)
    text_pull = lax.psum_scatter(
        lax.dot_general(
            coef, rows_half, (((0,), (0,)), ((), ())), preferred_element_type=jnp.float32
        ),
        "img",
        scatter_dimension=0,
        tiled=True,
    )
    image_sum, loss_sum = (
        lax.psum_scatter(image_pull, "txt", scatter_dimension=0, tiled=True),
        lax.psum_scatter(loss_part, "txt", scatter_dimension=0, tiled=True),
    )
    row_loss = loss_sum / pairs
    grad_image = project_back(image_unit, image_inv, image_sum)
    grad_text = project_back(text_unit, text_inv, text_pull)
    return (row_loss, grad_image, grad_text)


def on_first_core():
    return lax.rem(lax.axis_index("img"), 2) == 0


def pack_kernel(image_ref, text_ref, class_ref, out_ref):
    rows, depth = image_ref.shape
    row = lax.broadcasted_iota(jnp.int32, (rows, LANES), 0)
    lane = lax.broadcasted_iota(jnp.int32, (rows, LANES), 1)
    spread = jnp.zeros((rows, LANES), jnp.int32)
    for i in range(rows):
        spread = jnp.where(row == i, class_ref[i], spread)
    digit = lax.shift_right_logical(spread, 8 * jnp.minimum(lane, DIGITS - 1)) & 255
    digit = jnp.where(lane < DIGITS, digit, 0).astype(jnp.float32).astype(jnp.bfloat16)
    for start, source in ((0, image_ref), (rows, text_ref)):
        out_ref[start : start + rows, :depth] = unit_rows(source[...])[0].astype(jnp.bfloat16)
        out_ref[start : start + rows, depth:] = digit


def join_kernel(scale_ref, shift_ref, own_ref, got_ref, lines_ref, columns_ref, pair_ref):
    first = on_first_core()
    rows = own_ref.shape[0] // 2
    own, got = own_ref[...].astype(jnp.float32), got_ref[...].astype(jnp.float32)
    low, high = jnp.where(first, own, got), jnp.where(first, got, own)
    images = jnp.concatenate([low[:rows], high[:rows]], axis=0)
    texts = jnp.concatenate([low[rows:], high[rows:]], axis=0)
    lines_ref[...] = jnp.where(first, images, texts).astype(jnp.bfloat16)
    columns_ref[...] = jnp.where(first, texts, images).astype(jnp.bfloat16)
    row = lax.broadcasted_iota(jnp.int32, pair_ref.shape, 0)
    pair_ref[...] = jnp.where(row == 0, scale_ref[0], shift_ref[0])


def power_above(size):
    return jnp.ceil(jnp.log2(jnp.maximum(size, 1e-30)) + 0.01)


def code(values, power):
    steps = jnp.clip(jnp.round(values * (TOP / jnp.exp2(power))), -TOP, TOP)
    return steps.astype(jnp.int32).astype(jnp.int16)


def decode(steps, power):
    return steps.astype(jnp.int32).astype(jnp.float32) * (jnp.exp2(power) * (1.0 / TOP))


def put_rows(outs, pull, extra):
    blocks, (rows, width) = len(outs), outs[0].shape
    depth = width - LANES
    power = power_above(jnp.max(jnp.abs(pull), axis=1, keepdims=True))
    steps = code(pull, power)
    lane = lax.broadcasted_iota(jnp.int32, (blocks * rows, LANES), 1)
    tail = jnp.where(lane == 0, power, 0.0)
    if extra is not None:
        loss_power = power_above(extra)
        tail = jnp.where(lane == 1, loss_power, tail)
        tail = jnp.where(lane == 2, jnp.round(extra * (TOP / jnp.exp2(loss_power))), tail)
    tail = tail.astype(jnp.int32).astype(jnp.int16)
    for k, out in enumerate(outs):
        out[:, :depth] = steps[k * rows : (k + 1) * rows]
        out[:, depth:] = tail[k * rows : (k + 1) * rows]


def tile_kernel(count, pair_ref, *refs):
    depth = refs[0].shape[1] - LANES
    scale, shift = pair_ref[0:1, 0:1], pair_ref[1:2, 0:1]
    lines = jnp.concatenate([ref[...] for ref in refs[:count]], axis=0)
    columns = jnp.concatenate([ref[...] for ref in refs[count : 2 * count]], axis=0)
    logits = (
        scale
        * lax.dot_general(
            lines[:, :depth],
            columns[:, :depth],
            (((1,), (1,)), ((), ())),
            preferred_element_type=jnp.float32,
        )
        + shift
    )
    pick = (
        lax.broadcasted_iota(jnp.int32, (8, LANES), 0)
        == lax.broadcasted_iota(jnp.int32, (8, LANES), 1)
    )
    column_digits = lax.dot_general(
        pick.astype(jnp.bfloat16),
        columns[:, depth:],
        (((1,), (1,)), ((), ())),
        preferred_element_type=jnp.float32,
    )
    line_digits = lines[:, depth:].astype(jnp.float32)
    same = None
    for k in range(DIGITS):
        equal = line_digits[:, k : k + 1] == column_digits[k : k + 1, :]
        same = equal if same is None else same & equal
    sign = jnp.where(same, 1.0, -1.0).astype(jnp.float32)
    margin = sign * logits
    small = jnp.exp(-jnp.abs(margin))
    over = 1.0 / (1.0 + small)
    coef = -sign * jnp.where(margin >= 0, small * over, over) * scale
    pull = jnp.dot(
        coef.astype(jnp.bfloat16), columns[:, :depth], preferred_element_type=jnp.float32
    )
    loss = jnp.sum(jnp.log1p(small) - jnp.minimum(margin, 0.0), axis=1, keepdims=True)
    put_rows(refs[2 * count :], pull, loss)


def final_kernel(count, image_ref, text_ref, *refs):
    mine, others = refs[:count], refs[count : 2 * count]
    loss_ref, grad_image_ref, grad_text_ref = refs[2 * count :]
    rows, depth = image_ref.shape
    pairs = rows * 2 * count * count
    first = on_first_core()
    own_rows = pl.ds(pl.multiple_of(jnp.where(first, 0, rows), rows), rows)

    def total(parts):
        pull = jnp.zeros((rows, depth), jnp.float32)
        loss = jnp.zeros((rows, 1), jnp.float32)
        for part in parts:
            tail = part[own_rows, depth:].astype(jnp.int32).astype(jnp.float32)
            pull = pull + decode(part[own_rows, :depth], tail[:, 0:1])
            loss = loss + tail[:, 2:3] * (jnp.exp2(tail[:, 1:2]) * (1.0 / TOP))
        return pull, loss

    (pull, loss), (other_pull, other_loss) = total(mine), total(others)
    for source, side_pull, out in (
        (image_ref, jnp.where(first, pull, other_pull), grad_image_ref),
        (text_ref, jnp.where(first, other_pull, pull), grad_text_ref),
    ):
        unit, inverse = unit_rows(source[...])
        out[...] = project_back(unit, inverse, side_pull)
    loss = jnp.where(first, loss, other_loss)
    row = lax.broadcasted_iota(jnp.int32, (rows, rows), 0)
    column = lax.broadcasted_iota(jnp.int32, (rows, rows), 1)
    across = jnp.where(row == column, loss / pairs, 0.0)
    loss_ref[...] = jnp.sum(across, axis=0, keepdims=True)


def chip_plan(image_emb, text_emb, pair_class, scale, shift, count):
    rows, depth = image_emb.shape
    lanes = lax.axis_size("txt")
    n = lax.axis_size("img") * lanes
    width = depth + LANES
    vmem = pl.BlockSpec(memory_space=pltpu.VMEM)
    smem = pl.BlockSpec(memory_space=pltpu.SMEM)
    params = pltpu.CompilerParams(vmem_limit_bytes=32 << 20)

    def core(i):
        return i // lanes % 2

    def partner(i, k):
        chip = i // (2 * lanes) * lanes + i % lanes
        chip ^= k if core(i) else k * count
        return (chip // lanes * 2 + core(i)) * lanes + chip % lanes

    def swap(x):
        return lax.ppermute(x, AXES, [(i, i ^ lanes) for i in range(n)])

    def visit(x, k):
        return lax.ppermute(x, AXES, [(i, partner(i, k)) for i in range(n)])

    block = jax.ShapeDtypeStruct((2 * rows, width), jnp.bfloat16)
    own = pl.pallas_call(
        pack_kernel,
        out_shape=block,
        in_specs=[vmem, vmem, smem],
        out_specs=vmem,
        name="pack",
    )(image_emb, text_emb, pair_class)
    lines, columns, pair = pl.pallas_call(
        join_kernel,
        out_shape=(block, block, jax.ShapeDtypeStruct((8, LANES), jnp.float32)),
        in_specs=[smem, smem, vmem, vmem],
        out_specs=(vmem, vmem, vmem),
        compiler_params=params,
        name="join",
    )(scale[None], shift[None], own, swap(own))
    got = [visit(lines, k) for k in range(1, count)]
    parts = pl.pallas_call(
        functools.partial(tile_kernel, count),
        out_shape=(jax.ShapeDtypeStruct((2 * rows, width), jnp.int16),) * count,
        in_specs=[vmem] * (1 + 2 * count),
        out_specs=(vmem,) * count,
        compiler_params=params,
        name="tile",
    )(pair, *got[::-1], lines, *[swap(x) for x in got[::-1]], columns)
    parts = [visit(x, k) for x, k in zip(parts, range(count - 1, 0, -1))] + [parts[-1]]
    loss, grad_image, grad_text = pl.pallas_call(
        functools.partial(final_kernel, count),
        out_shape=(
            jax.ShapeDtypeStruct((1, rows), jnp.float32),
            jax.ShapeDtypeStruct((rows, depth), jnp.float32),
            jax.ShapeDtypeStruct((rows, depth), jnp.float32),
        ),
        in_specs=[vmem] * (2 + 2 * count),
        out_specs=(vmem, vmem, vmem),
        compiler_params=params,
        name="final",
    )(image_emb, text_emb, *parts, *[swap(x) for x in parts])
    return (loss[0], grad_image, grad_text)


def local(image_emb, text_emb, pair_class, scale, shift):
    chips = lax.axis_size("img") * lax.axis_size("txt") // 2
    count = math.isqrt(chips)
    if count * count == chips and count & (count - 1) == 0:
        return chip_plan(image_emb, text_emb, pair_class, scale, shift, count)
    return tile_plan(image_emb, text_emb, pair_class, scale, shift)


def solution(mesh):
    in_specs = (P(AXES, None), P(AXES, None), P(AXES), P(), P())
    out_specs = (P(AXES), P(AXES, None), P(AXES, None))
    return jax.shard_map(local, mesh=mesh, in_specs=in_specs, out_specs=out_specs, check_vma=False)
```

```python
import functools

import jax
import jax.numpy as jnp
from jax import lax
from jax.experimental import pallas as pl
from jax.experimental.pallas import tpu as pltpu
from jax.sharding import PartitionSpec as P

AXES = ("img", "txt")
DIGITS = 4
LANES = 128
TOP = 32767.0


def unit_rows(rows):
    wide = rows.astype(jnp.float32)
    inverse = 1.0 / jnp.sqrt(jnp.sum(wide * wide, axis=1, keepdims=True) + 1e-06)
    return (wide * inverse, inverse)


def project_back(unit, inverse, pull):
    inner = jnp.sum(unit * pull, axis=1, keepdims=True)
    return (pull - unit * inner) * inverse


def pack_kernel(image_ref, text_ref, class_ref, image_out, text_out):
    rows, depth = image_ref.shape
    row = lax.broadcasted_iota(jnp.int32, (rows, LANES), 0)
    lane = lax.broadcasted_iota(jnp.int32, (rows, LANES), 1)
    spread = jnp.zeros((rows, LANES), jnp.int32)
    for i in range(rows):
        spread = jnp.where(row == i, class_ref[i], spread)
    digit = lax.shift_right_logical(spread, 8 * jnp.minimum(lane, DIGITS - 1)) & 255
    digit = jnp.where(lane < DIGITS, digit, 0).astype(jnp.float32).astype(jnp.bfloat16)
    for source, out in ((image_ref, image_out), (text_ref, text_out)):
        out[:, :depth] = unit_rows(source[...])[0].astype(jnp.bfloat16)
        out[:, depth:] = digit


def put_blocks(out_ref, refs):
    start = 0
    for ref in refs:
        out_ref[start : start + ref.shape[0], :] = ref[...]
        start += ref.shape[0]


def join_kernel(*refs):
    put_blocks(refs[-1], refs[:-1])


def join_with_pair_kernel(scale_ref, shift_ref, *refs):
    put_blocks(refs[-2], refs[:-2])
    row = lax.broadcasted_iota(jnp.int32, refs[-1].shape, 0)
    refs[-1][...] = jnp.where(row == 0, scale_ref[0], shift_ref[0])


def power_above(size):
    return jnp.ceil(jnp.log2(jnp.maximum(size, 1e-30)) + 0.01)


def code(values, power):
    steps = jnp.clip(jnp.round(values * (TOP / jnp.exp2(power))), -TOP, TOP)
    return steps.astype(jnp.int32).astype(jnp.int16)


def decode(steps, power):
    return steps.astype(jnp.int32).astype(jnp.float32) * (jnp.exp2(power) * (1.0 / TOP))


def put_rows(outs, pull, extra):
    blocks, (rows, width) = len(outs), outs[0].shape
    depth = width - LANES
    power = power_above(jnp.max(jnp.abs(pull), axis=1, keepdims=True))
    steps = code(pull, power)
    lane = lax.broadcasted_iota(jnp.int32, (blocks * rows, LANES), 1)
    tail = jnp.where(lane == 0, power, 0.0)
    if extra is not None:
        loss_power = power_above(extra)
        tail = jnp.where(lane == 1, loss_power, tail)
        tail = jnp.where(lane == 2, jnp.round(extra * (TOP / jnp.exp2(loss_power))), tail)
    tail = tail.astype(jnp.int32).astype(jnp.int16)
    for k, out in enumerate(outs):
        out[:, :depth] = steps[k * rows : (k + 1) * rows]
        out[:, depth:] = tail[k * rows : (k + 1) * rows]


def partial_pull(lines, columns, scale, shift):
    depth = lines.shape[1] - LANES
    logits = (
        scale
        * lax.dot_general(
            lines[:, :depth],
            columns[:, :depth],
            (((1,), (1,)), ((), ())),
            preferred_element_type=jnp.float32,
        )
        + shift
    )
    pick = (
        lax.broadcasted_iota(jnp.int32, (8, LANES), 0)
        == lax.broadcasted_iota(jnp.int32, (8, LANES), 1)
    )
    column_digits = lax.dot_general(
        pick.astype(jnp.bfloat16),
        columns[:, depth:],
        (((1,), (1,)), ((), ())),
        preferred_element_type=jnp.float32,
    )
    line_digits = lines[:, depth:].astype(jnp.float32)
    same = None
    for k in range(DIGITS):
        equal = line_digits[:, k : k + 1] == column_digits[k : k + 1, :]
        same = equal if same is None else same & equal
    sign = jnp.where(same, 1.0, -1.0).astype(jnp.float32)
    margin = sign * logits
    small = jnp.exp(-jnp.abs(margin))
    over = 1.0 / (1.0 + small)
    coef = -sign * jnp.where(margin >= 0, small * over, over) * scale
    pull = jnp.dot(
        coef.astype(jnp.bfloat16), columns[:, :depth], preferred_element_type=jnp.float32
    )
    loss = jnp.sum(jnp.log1p(small) - jnp.minimum(margin, 0.0), axis=1, keepdims=True)
    return pull, loss


def tile_kernel(a, pair_ref, images_ref, texts_ref, other_images_ref, other_texts_ref, *outs):
    scale, shift = pair_ref[0:1, 0:1], pair_ref[1:2, 0:1]
    images, texts = images_ref[...], texts_ref[...]
    pull, loss = partial_pull(
        images, jnp.concatenate([texts, other_texts_ref[...]], axis=0), scale, shift
    )
    put_rows(outs[:a][::-1], pull, loss)
    pull, _ = partial_pull(
        texts, jnp.concatenate([images, other_images_ref[...]], axis=0), scale, shift
    )
    put_rows(outs[a:][::-1], pull, None)


def final_kernel(a, b, image_ref, text_ref, *refs):
    image_parts, text_parts = refs[:a], refs[a : a + b]
    loss_ref, grad_image_ref, grad_text_ref = refs[a + b :]
    rows, depth = image_ref.shape
    pairs = 2 * rows * a * b
    for source, parts, out in (
        (image_ref, image_parts, grad_image_ref),
        (text_ref, text_parts, grad_text_ref),
    ):
        unit, inverse = unit_rows(source[...])
        pull = jnp.zeros((rows, depth), jnp.float32)
        loss = jnp.zeros((rows, 1), jnp.float32)
        for part in parts:
            tail = part[:, depth:].astype(jnp.int32).astype(jnp.float32)
            pull = pull + decode(part[:, :depth], tail[:, 0:1])
            loss = loss + tail[:, 2:3] * (jnp.exp2(tail[:, 1:2]) * (1.0 / TOP))
        out[...] = project_back(unit, inverse, pull)
        if out is grad_image_ref:
            row = lax.broadcasted_iota(jnp.int32, (rows, rows), 0)
            column = lax.broadcasted_iota(jnp.int32, (rows, rows), 1)
            across = jnp.where(row == column, loss / pairs, 0.0)
            loss_ref[...] = jnp.sum(across, axis=0, keepdims=True)


def partner(place, k, size):
    return place ^ k if size & (size - 1) == 0 else (place + k) % size


def local(image_emb, text_emb, pair_class, scale, shift):
    rows, depth = image_emb.shape
    width = depth + LANES
    lanes = lax.axis_size("txt")
    n = lax.axis_size("img") * lanes
    chips = n // 2
    b = min(d for d in range(1, chips + 1) if chips % d == 0 and d * d >= chips)
    a = chips // b
    vmem = pl.BlockSpec(memory_space=pltpu.VMEM)
    smem = pl.BlockSpec(memory_space=pltpu.SMEM)
    params = pltpu.CompilerParams(vmem_limit_bytes=32 << 20)

    def split(i):
        return i // (2 * lanes) * lanes + i % lanes, i // lanes % 2

    def place(chip, core):
        return (chip // lanes * 2 + core) * lanes + chip % lanes

    def along_a(i, k):
        chip, core = split(i)
        return place(partner(chip // b, k, a) * b + chip % b, core)

    def along_b(i, k):
        chip, core = split(i)
        return place(chip // b * b + partner(chip % b, k, b), core)

    def move(x, pairs):
        return lax.ppermute(x, AXES, pairs)

    def collect(x, size, along):
        return [x] + [move(x, [(along(i, k), i) for i in range(n)]) for k in range(1, size)]

    def give_back(parts, along):
        steps = range(len(parts) - 1, 0, -1)
        return [move(x, [(i, along(i, k)) for i in range(n)]) for x, k in zip(parts, steps)] + [parts[-1]]

    def swap(x):
        return move(x, [(i, place(split(i)[0], 1 - split(i)[1])) for i in range(n)])

    block = jax.ShapeDtypeStruct((rows, width), jnp.bfloat16)
    image_rows, text_rows = pl.pallas_call(
        pack_kernel,
        out_shape=(block, block),
        in_specs=[vmem, vmem, smem],
        out_specs=(vmem, vmem),
        name="pack",
    )(image_emb, text_emb, pair_class)
    images = pl.pallas_call(
        join_kernel,
        out_shape=jax.ShapeDtypeStruct((a * rows, width), jnp.bfloat16),
        in_specs=[vmem] * a,
        out_specs=vmem,
        compiler_params=params,
        name="join_images",
    )(*collect(image_rows, a, along_a))
    texts, pair = pl.pallas_call(
        join_with_pair_kernel,
        out_shape=(
            jax.ShapeDtypeStruct((b * rows, width), jnp.bfloat16),
            jax.ShapeDtypeStruct((8, LANES), jnp.float32),
        ),
        in_specs=[smem, smem] + [vmem] * b,
        out_specs=(vmem, vmem),
        compiler_params=params,
        name="join_texts",
    )(scale[None], shift[None], *collect(text_rows, b, along_b))
    parts = pl.pallas_call(
        functools.partial(tile_kernel, a),
        out_shape=(jax.ShapeDtypeStruct((rows, width), jnp.int16),) * (a + b),
        in_specs=[vmem] * 5,
        out_specs=(vmem,) * (a + b),
        compiler_params=params,
        name="tile",
    )(pair, images, texts, swap(images), swap(texts))
    parts = give_back(parts[:a], along_a) + give_back(parts[a:], along_b)
    loss, grad_image, grad_text = pl.pallas_call(
        functools.partial(final_kernel, a, b),
        out_shape=(
            jax.ShapeDtypeStruct((1, rows), jnp.float32),
            jax.ShapeDtypeStruct((rows, depth), jnp.float32),
            jax.ShapeDtypeStruct((rows, depth), jnp.float32),
        ),
        in_specs=[vmem] * (2 + a + b),
        out_specs=(vmem, vmem, vmem),
        compiler_params=params,
        name="final",
    )(image_emb, text_emb, *parts)
    return (loss[0], grad_image, grad_text)


def solution(mesh):
    in_specs = (P(AXES, None), P(AXES, None), P(AXES), P(), P())
    out_specs = (P(AXES), P(AXES, None), P(AXES, None))
    return jax.shard_map(local, mesh=mesh, in_specs=in_specs, out_specs=out_specs, check_vma=False)
```

```python
import functools

import jax
import jax.numpy as jnp
from jax import lax
from jax.experimental import pallas as pl
from jax.experimental.pallas import tpu as pltpu
from jax.sharding import PartitionSpec as P

AXES = ("img", "txt")
DIGITS = 4
LANES = 128
TOP = 32767.0


def unit_rows(rows):
    wide = rows.astype(jnp.float32)
    inverse = 1.0 / jnp.sqrt(jnp.sum(wide * wide, axis=1, keepdims=True) + 1e-06)
    return (wide * inverse, inverse)


def project_back(unit, inverse, pull):
    inner = jnp.sum(unit * pull, axis=1, keepdims=True)
    return (pull - unit * inner) * inverse


def pack_kernel(rows_ref, class_ref, out_ref):
    rows, depth = rows_ref.shape
    row = lax.broadcasted_iota(jnp.int32, (rows, LANES), 0)
    lane = lax.broadcasted_iota(jnp.int32, (rows, LANES), 1)
    spread = jnp.zeros((rows, LANES), jnp.int32)
    for i in range(rows):
        spread = jnp.where(row == i, class_ref[i], spread)
    digit = lax.shift_right_logical(spread, 8 * jnp.minimum(lane, DIGITS - 1)) & 255
    digit = jnp.where(lane < DIGITS, digit, 0).astype(jnp.float32).astype(jnp.bfloat16)
    out_ref[:, :depth] = unit_rows(rows_ref[...])[0].astype(jnp.bfloat16)
    out_ref[:, depth:] = digit


def put_blocks(out_ref, refs):
    start = 0
    for ref in refs:
        out_ref[start : start + ref.shape[0], :] = ref[...]
        start += ref.shape[0]


def join_kernel(*refs):
    put_blocks(refs[-1], refs[:-1])


def join_with_pair_kernel(scale_ref, shift_ref, *refs):
    put_blocks(refs[-2], refs[:-2])
    row = lax.broadcasted_iota(jnp.int32, refs[-1].shape, 0)
    refs[-1][...] = jnp.where(row == 0, scale_ref[0], shift_ref[0])


def power_above(size):
    return jnp.ceil(jnp.log2(jnp.maximum(size, 1e-30)) + 0.01)


def code(values, power):
    steps = jnp.clip(jnp.round(values * (TOP / jnp.exp2(power))), -TOP, TOP)
    return steps.astype(jnp.int32).astype(jnp.int16)


def decode(steps, power):
    return steps.astype(jnp.int32).astype(jnp.float32) * (jnp.exp2(power) * (1.0 / TOP))


def put_rows(outs, pull, loss):
    blocks, (rows, width) = len(outs), outs[0].shape
    depth = width - LANES
    power = power_above(jnp.max(jnp.abs(pull), axis=1, keepdims=True))
    steps = code(pull, power)
    lane = lax.broadcasted_iota(jnp.int32, (blocks * rows, LANES), 1)
    loss_power = power_above(loss)
    tail = jnp.where(lane == 0, power, 0.0)
    tail = jnp.where(lane == 1, loss_power, tail)
    tail = jnp.where(lane == 2, jnp.round(loss * (TOP / jnp.exp2(loss_power))), tail)
    tail = tail.astype(jnp.int32).astype(jnp.int16)
    for k, out in enumerate(outs):
        out[:, :depth] = steps[k * rows : (k + 1) * rows]
        out[:, depth:] = tail[k * rows : (k + 1) * rows]


def partial_pull(lines, columns, scale, shift):
    depth = lines.shape[1] - LANES
    logits = (
        scale
        * lax.dot_general(
            lines[:, :depth],
            columns[:, :depth],
            (((1,), (1,)), ((), ())),
            preferred_element_type=jnp.float32,
        )
        + shift
    )
    pick = (
        lax.broadcasted_iota(jnp.int32, (8, LANES), 0)
        == lax.broadcasted_iota(jnp.int32, (8, LANES), 1)
    )
    column_digits = lax.dot_general(
        pick.astype(jnp.bfloat16),
        columns[:, depth:],
        (((1,), (1,)), ((), ())),
        preferred_element_type=jnp.float32,
    )
    line_digits = lines[:, depth:].astype(jnp.float32)
    same = None
    for k in range(DIGITS):
        equal = line_digits[:, k : k + 1] == column_digits[k : k + 1, :]
        same = equal if same is None else same & equal
    sign = jnp.where(same, 1.0, -1.0).astype(jnp.float32)
    margin = sign * logits
    small = jnp.exp(-jnp.abs(margin))
    over = 1.0 / (1.0 + small)
    coef = -sign * jnp.where(margin >= 0, small * over, over) * scale
    pull = jnp.dot(
        coef.astype(jnp.bfloat16), columns[:, :depth], preferred_element_type=jnp.float32
    )
    loss = jnp.sum(jnp.log1p(small) - jnp.minimum(margin, 0.0), axis=1, keepdims=True)
    return pull, loss


def tile_kernel(count, pair_ref, images_ref, texts_ref, other_images_ref, other_texts_ref, *outs):
    scale, shift = pair_ref[0:1, 0:1], pair_ref[1:2, 0:1]
    images, texts = images_ref[...], texts_ref[...]
    pull, loss = partial_pull(
        images, jnp.concatenate([texts, other_texts_ref[...]], axis=0), scale, shift
    )
    put_rows(outs[:count], pull, loss)
    pull, loss = partial_pull(
        texts, jnp.concatenate([images, other_images_ref[...]], axis=0), scale, shift
    )
    put_rows(outs[count:], pull, loss)


def total(parts, rows, depth):
    pull = jnp.zeros((rows, depth), jnp.float32)
    loss = jnp.zeros((rows, 1), jnp.float32)
    for part in parts:
        tail = part[:, depth:].astype(jnp.int32).astype(jnp.float32)
        pull = pull + decode(part[:, :depth], tail[:, 0:1])
        loss = loss + tail[:, 2:3] * (jnp.exp2(tail[:, 1:2]) * (1.0 / TOP))
    return pull, loss


def add_kernel(count, *refs):
    rows, width = refs[0].shape
    pull, loss = total(refs[:count], rows, width - LANES)
    put_rows(refs[count:], pull, loss)


def final_kernel(count, pairs, image_ref, text_ref, *refs):
    image_parts, text_parts = refs[:count], refs[count:-3]
    loss_ref, grad_image_ref, grad_text_ref = refs[-3:]
    rows, depth = image_ref.shape
    for source, parts, out in (
        (image_ref, image_parts, grad_image_ref),
        (text_ref, text_parts, grad_text_ref),
    ):
        unit, inverse = unit_rows(source[...])
        pull, loss = total(parts, rows, depth)
        out[...] = project_back(unit, inverse, pull)
        if out is grad_image_ref:
            row = lax.broadcasted_iota(jnp.int32, (rows, rows), 0)
            column = lax.broadcasted_iota(jnp.int32, (rows, rows), 1)
            across = jnp.where(row == column, loss / pairs, 0.0)
            loss_ref[...] = jnp.sum(across, axis=0, keepdims=True)


def steps_of(size):
    steps, left = [], size
    while left > 1:
        factor = min(d for d in range(2, left + 1) if left % d == 0)
        left //= factor
        steps.append((factor, left))
    return steps


def local(image_emb, text_emb, pair_class, scale, shift):
    rows, depth = image_emb.shape
    width = depth + LANES
    lanes = lax.axis_size("txt")
    n = lax.axis_size("img") * lanes
    chips = n // 2
    b = min(d for d in range(1, chips + 1) if chips % d == 0 and d * d >= chips)
    a = chips // b
    vmem = pl.BlockSpec(memory_space=pltpu.VMEM)
    smem = pl.BlockSpec(memory_space=pltpu.SMEM)
    params = pltpu.CompilerParams(vmem_limit_bytes=32 << 20)

    def call(kernel, shapes, operands, scalars, name):
        return pl.pallas_call(
            kernel,
            out_shape=shapes,
            in_specs=[smem] * scalars + [vmem] * (len(operands) - scalars),
            out_specs=jax.tree.map(lambda _: vmem, shapes),
            compiler_params=params,
            name=name,
        )(*operands)

    def coded(count, dtype=jnp.int16):
        return jax.ShapeDtypeStruct((count, width), dtype)

    def split(i):
        return i // (2 * lanes) * lanes + i % lanes, i // lanes % 2

    def place(chip, core):
        return (chip // lanes * 2 + core) * lanes + chip % lanes

    def turn(i, k, factor, stride):
        chip, core = split(i)
        digit = chip // stride % factor
        return place(chip + ((digit + k) % factor - digit) * stride, core)

    def move(x, pairs):
        return lax.ppermute(x, AXES, pairs)

    def collect(x, steps, name, extra=()):
        for factor, stride in steps:
            blocks = [x] + [
                move(x, [(turn(i, k, factor, stride), i) for i in range(n)])
                for k in range(1, factor)
            ]
            shape = coded(factor * x.shape[0], jnp.bfloat16)
            if extra and (factor, stride) == steps[-1]:
                pair = jax.ShapeDtypeStruct((8, LANES), jnp.float32)
                return call(join_with_pair_kernel, (shape, pair), [*extra, *blocks], 2, name)
            x = call(join_kernel, shape, blocks, 0, name)
        return x

    def give_back(parts, steps, name):
        for index, (factor, stride) in enumerate(steps):
            parts = [parts[0]] + [
                move(parts[k], [(i, turn(i, k, factor, stride)) for i in range(n)])
                for k in range(1, factor)
            ]
            if index + 1 < len(steps):
                count = steps[index + 1][0]
                shapes = (coded(parts[0].shape[0] // count),) * count
                parts = call(functools.partial(add_kernel, factor), shapes, parts, 0, name)
        return list(parts)

    def swap(x):
        return move(x, [(i, place(split(i)[0], 1 - split(i)[1])) for i in range(n)])

    along_a = [(factor, stride * b) for factor, stride in steps_of(a)]
    along_b = steps_of(b)
    sides = [
        pl.pallas_call(
            pack_kernel,
            out_shape=coded(rows, jnp.bfloat16),
            in_specs=[vmem, smem],
            out_specs=vmem,
            compiler_params=params,
            name=name,
        )(x, pair_class)
        for x, name in ((image_emb, "pack_images"), (text_emb, "pack_texts"))
    ]
    images = collect(sides[0], along_a, "join_images")
    texts, pair = collect(sides[1], along_b, "join_texts", (scale[None], shift[None]))
    back_a, back_b = along_a[::-1], along_b[::-1]
    count = back_a[0][0]
    shapes = (coded(a * rows // count),) * count + (coded(b * rows // back_b[0][0]),) * back_b[0][0]
    parts = call(
        functools.partial(tile_kernel, count),
        shapes,
        [pair, images, texts, swap(images), swap(texts)],
        0,
        "tile",
    )
    image_parts = give_back(parts[:count], back_a, "add_images")
    text_parts = give_back(parts[count:], back_b, "add_texts")
    loss, grad_image, grad_text = call(
        functools.partial(final_kernel, len(image_parts), n * rows),
        (
            jax.ShapeDtypeStruct((1, rows), jnp.float32),
            jax.ShapeDtypeStruct((rows, depth), jnp.float32),
            jax.ShapeDtypeStruct((rows, depth), jnp.float32),
        ),
        [image_emb, text_emb, *image_parts, *text_parts],
        0,
        "final",
    )
    return (loss[0], grad_image, grad_text)


def solution(mesh):
    in_specs = (P(AXES, None), P(AXES, None), P(AXES), P(), P())
    out_specs = (P(AXES), P(AXES, None), P(AXES, None))
    return jax.shard_map(local, mesh=mesh, in_specs=in_specs, out_specs=out_specs, check_vma=False)
```

```python
import functools

import jax
import jax.numpy as jnp
from jax import lax
from jax.experimental import pallas as pl
from jax.experimental.pallas import tpu as pltpu
from jax.sharding import PartitionSpec as P

AXES = ("img", "txt")
DIGITS = 4
LANES = 128
TOP = 32767.0


def unit_rows(rows):
    wide = rows.astype(jnp.float32)
    inverse = 1.0 / jnp.sqrt(jnp.sum(wide * wide, axis=1, keepdims=True) + 1e-06)
    return (wide * inverse, inverse)


def project_back(unit, inverse, pull):
    inner = jnp.sum(unit * pull, axis=1, keepdims=True)
    return (pull - unit * inner) * inverse


def tile_terms(rows_half, row_class, cols_half, col_class, scale, shift):
    logits = (
        scale
        * lax.dot_general(
            rows_half, cols_half, (((1,), (1,)), ((), ())), preferred_element_type=jnp.float32
        )
        + shift
    )
    sign = jnp.where(row_class[:, None] == col_class[None, :], 1.0, -1.0).astype(jnp.float32)
    margin = sign * logits
    loss_part = -jnp.sum(jax.nn.log_sigmoid(margin), axis=1)
    coef = (-sign * jax.nn.sigmoid(-margin) * scale).astype(jnp.bfloat16)
    return (coef, loss_part)


def tile_plan(image_emb, text_emb, pair_class, scale, shift):
    image_unit, image_inv = unit_rows(image_emb)
    text_unit, text_inv = unit_rows(text_emb)
    own_rows = text_emb.shape[0]
    pairs = own_rows * lax.axis_size("img") * lax.axis_size("txt")
    text_half = text_unit.astype(jnp.bfloat16)
    rows_half, row_class = (
        lax.all_gather(image_unit.astype(jnp.bfloat16), "txt", axis=0, tiled=True),
        lax.all_gather(pair_class, "txt", axis=0, tiled=True),
    )
    cols_half, col_class = (
        lax.all_gather(text_half, "img", axis=0, tiled=True),
        lax.all_gather(pair_class, "img", axis=0, tiled=True),
    )
    coef, loss_part = tile_terms(rows_half, row_class, cols_half, col_class, scale, shift)
    image_pull = jnp.dot(coef, cols_half, preferred_element_type=jnp.float32)
    text_pull = lax.psum_scatter(
        lax.dot_general(
            coef, rows_half, (((0,), (0,)), ((), ())), preferred_element_type=jnp.float32
        ),
        "img",
        scatter_dimension=0,
        tiled=True,
    )
    image_sum, loss_sum = (
        lax.psum_scatter(image_pull, "txt", scatter_dimension=0, tiled=True),
        lax.psum_scatter(loss_part, "txt", scatter_dimension=0, tiled=True),
    )
    row_loss = loss_sum / pairs
    grad_image = project_back(image_unit, image_inv, image_sum)
    grad_text = project_back(text_unit, text_inv, text_pull)
    return (row_loss, grad_image, grad_text)


def on_first_core():
    return lax.rem(lax.axis_index("img"), 2) == 0


def class_digits(class_ref):
    rows = class_ref.shape[0]
    across = jnp.broadcast_to(class_ref[...][None, :], (rows, rows))
    row = lax.broadcasted_iota(jnp.int32, (rows, rows), 0)
    column = lax.broadcasted_iota(jnp.int32, (rows, rows), 1)
    lane = lax.broadcasted_iota(jnp.int32, (rows, LANES), 1)
    digits = jnp.zeros((rows, LANES), jnp.float32)
    for k in range(DIGITS):
        byte = (lax.shift_right_logical(across, 8 * k) & 255).astype(jnp.float32)
        down = jnp.sum(jnp.where(row == column, byte, 0.0), axis=1, keepdims=True)
        digits = jnp.where(lane == k, down, digits)
    return digits.astype(jnp.bfloat16)


def pack_kernel(image_ref, text_ref, class_ref, out_ref):
    rows, depth = image_ref.shape
    digits = class_digits(class_ref)
    for start, source in ((0, image_ref), (rows, text_ref)):
        out_ref[start : start + rows, :depth] = unit_rows(source[...])[0].astype(jnp.bfloat16)
        out_ref[start : start + rows, depth:] = digits


def join_kernel(scale_ref, shift_ref, own_ref, got_ref, mine_ref, other_ref, again_ref, pair_ref):
    first = on_first_core()
    rows = own_ref.shape[0] // 2
    own, got = own_ref[...].astype(jnp.float32), got_ref[...].astype(jnp.float32)
    low, high = jnp.where(first, own, got), jnp.where(first, got, own)
    images = jnp.concatenate([low[:rows], high[:rows]], axis=0)
    texts = jnp.concatenate([low[rows:], high[rows:]], axis=0)
    mine = jnp.where(first, images, texts).astype(jnp.bfloat16)
    mine_ref[...] = mine
    again_ref[...] = mine
    other_ref[...] = jnp.where(first, texts, images).astype(jnp.bfloat16)
    row = lax.broadcasted_iota(jnp.int32, pair_ref.shape, 0)
    pair_ref[...] = jnp.where(row == 0, scale_ref[0], shift_ref[0])


def gather_kernel(*refs):
    rows = refs[0].shape[0]
    for k, ref in enumerate(refs[:-1]):
        refs[-1][k * rows : (k + 1) * rows, :] = ref[...]


def power_above(size):
    return jnp.ceil(jnp.log2(jnp.maximum(size, 1e-30)) + 0.01)


def code(values, power):
    steps = jnp.clip(jnp.round(values * (TOP / jnp.exp2(power))), -TOP, TOP)
    return steps.astype(jnp.int32).astype(jnp.int16)


def decode(steps, power):
    return steps.astype(jnp.int32).astype(jnp.float32) * (jnp.exp2(power) * (1.0 / TOP))


def put_rows(outs, pull, loss):
    blocks, (rows, width) = len(outs), outs[0].shape
    depth = width - LANES
    power = power_above(jnp.max(jnp.abs(pull), axis=1, keepdims=True))
    steps = code(pull, power)
    lane = lax.broadcasted_iota(jnp.int32, (blocks * rows, LANES), 1)
    loss_power = power_above(loss)
    tail = jnp.where(lane == 0, power, 0.0)
    tail = jnp.where(lane == 1, loss_power, tail)
    tail = jnp.where(lane == 2, jnp.round(loss * (TOP / jnp.exp2(loss_power))), tail)
    tail = tail.astype(jnp.int32).astype(jnp.int16)
    for k, out in enumerate(outs):
        out[:, :depth] = steps[k * rows : (k + 1) * rows]
        out[:, depth:] = tail[k * rows : (k + 1) * rows]


def partial_pull(lines, columns, scale, shift):
    depth = lines.shape[1] - LANES
    logits = (
        scale
        * lax.dot_general(
            lines[:, :depth],
            columns[:, :depth],
            (((1,), (1,)), ((), ())),
            preferred_element_type=jnp.float32,
        )
        + shift
    )
    pick = (
        lax.broadcasted_iota(jnp.int32, (8, LANES), 0)
        == lax.broadcasted_iota(jnp.int32, (8, LANES), 1)
    )
    column_digits = lax.dot_general(
        pick.astype(jnp.bfloat16),
        columns[:, depth:],
        (((1,), (1,)), ((), ())),
        preferred_element_type=jnp.float32,
    )
    line_digits = lines[:, depth:].astype(jnp.float32)
    same = None
    for k in range(DIGITS):
        equal = line_digits[:, k : k + 1] == column_digits[k : k + 1, :]
        same = equal if same is None else same & equal
    sign = jnp.where(same, 1.0, -1.0).astype(jnp.float32)
    margin = sign * logits
    small = jnp.exp(-jnp.abs(margin))
    over = 1.0 / (1.0 + small)
    coef = -sign * jnp.where(margin >= 0, small * over, over) * scale
    pull = jnp.dot(
        coef.astype(jnp.bfloat16), columns[:, :depth], preferred_element_type=jnp.float32
    )
    loss = jnp.sum(jnp.log1p(small) - jnp.minimum(margin, 0.0), axis=1, keepdims=True)
    return pull, loss


def tile_kernel(pair_ref, mine_ref, other_ref, got_ref, swapped_ref, *outs):
    rows = mine_ref.shape[0]
    scale, shift = pair_ref[0:1, 0:1], pair_ref[1:2, 0:1]
    got = [got_ref[k * rows : (k + 1) * rows, :] for k in range(3)]
    swapped = [swapped_ref[k * rows : (k + 1) * rows, :] for k in range(3)]
    mine_side = jnp.concatenate([mine_ref[...], got[0], swapped[1], got[2]], axis=0)
    other_side = jnp.concatenate([other_ref[...], swapped[0], got[1], swapped[2]], axis=0)
    lines = jnp.concatenate([got[0], got[2], mine_ref[...]], axis=0)
    put_rows([outs[0], outs[2], outs[3]], *partial_pull(lines, other_side, scale, shift))
    put_rows([outs[1]], *partial_pull(got[1], mine_side, scale, shift))


def total(parts, rows, depth):
    pull = jnp.zeros((rows, depth), jnp.float32)
    loss = jnp.zeros((rows, 1), jnp.float32)
    for part in parts:
        tail = part[:, depth:].astype(jnp.int32).astype(jnp.float32)
        pull = pull + decode(part[:, :depth], tail[:, 0:1])
        loss = loss + tail[:, 2:3] * (jnp.exp2(tail[:, 1:2]) * (1.0 / TOP))
    return pull, loss


def place_of(first, rows):
    own = pl.multiple_of(jnp.where(first, 0, rows), rows)
    return pl.ds(own, rows), pl.ds(pl.multiple_of(rows - own, rows), rows)


def add_kernel(own_ref, back_0, back_1, back_2, keep_ref, loss_ref, give_ref):
    rows, depth = keep_ref.shape[1:]
    own, other = place_of(on_first_core(), rows)
    for side, parts in enumerate(((own_ref, back_0, back_2), (back_1,))):
        keep_ref[side], loss = total([part[own, :] for part in parts], rows, depth)
        loss_ref[side] = jnp.broadcast_to(loss, loss_ref.shape[1:])
        pull, loss = total([part[other, :] for part in parts], rows, depth)
        put_rows([give_ref.at[side * rows : (side + 1) * rows, :]], pull, loss)


def final_kernel(pairs, image_ref, text_ref, keep_ref, kept_loss_ref, got_ref, loss_ref, grad_image_ref, grad_text_ref):
    first = on_first_core()
    rows, depth = image_ref.shape
    pulls, losses = [], []
    for side in (0, 1):
        pull, loss = total([got_ref[(1 - side) * rows : (2 - side) * rows, :]], rows, depth)
        pulls.append(keep_ref[side] + pull)
        losses.append(kept_loss_ref[side][:, 0:1] + loss)
    for source, pull, out in (
        (image_ref, jnp.where(first, pulls[0], pulls[1]), grad_image_ref),
        (text_ref, jnp.where(first, pulls[1], pulls[0]), grad_text_ref),
    ):
        unit, inverse = unit_rows(source[...])
        out[...] = project_back(unit, inverse, pull)
    row = lax.broadcasted_iota(jnp.int32, (rows, rows), 0)
    column = lax.broadcasted_iota(jnp.int32, (rows, rows), 1)
    loss = jnp.where(first, losses[0], losses[1])
    across = jnp.where(row == column, loss / pairs, 0.0)
    loss_ref[...] = jnp.sum(across, axis=0, keepdims=True)


def chip_plan(image_emb, text_emb, pair_class, scale, shift):
    rows, depth = image_emb.shape
    width = depth + LANES
    lanes = lax.axis_size("txt")
    n = lax.axis_size("img") * lanes
    vmem = pl.BlockSpec(memory_space=pltpu.VMEM)
    smem = pl.BlockSpec(memory_space=pltpu.SMEM)

    def call(kernel, shapes, operands, name, scalars=0):
        return pl.pallas_call(
            kernel,
            out_shape=shapes,
            in_specs=[smem] * scalars + [vmem] * (len(operands) - scalars),
            out_specs=jax.tree.map(lambda _: vmem, shapes),
            compiler_params=pltpu.CompilerParams(vmem_limit_bytes=32 << 20),
            name=name,
        )(*operands)

    def block(count, dtype=jnp.bfloat16):
        return jax.ShapeDtypeStruct((count * rows, width), dtype)

    def wide(*shape):
        return jax.ShapeDtypeStruct(shape, jnp.float32)

    def core(i):
        return i // lanes % 2

    def visit(x, masks):
        pairs = []
        for i in range(n):
            chip = (i // (2 * lanes) * lanes + i % lanes) ^ masks[core(i)]
            pairs.append((i, (chip // lanes * 2 + core(i)) * lanes + chip % lanes))
        return lax.ppermute(x, AXES, pairs)

    def swap(x):
        return lax.ppermute(x, AXES, [(i, i ^ lanes) for i in range(n)])

    visits = ((12, 3), (2, 8), (4, 1))
    own = call(pack_kernel, block(2), [image_emb, text_emb, pair_class], "pack")
    mine, other, again, pair = call(
        join_kernel,
        (block(2), block(2), block(2), wide(8, LANES)),
        [scale[None], shift[None], own, swap(own)],
        "join",
        2,
    )
    got = [visit(x, masks) for x, masks in zip((mine, other, again), visits)]
    got = call(gather_kernel, block(6), got, "gather")
    parts = call(
        tile_kernel, (block(2, jnp.int16),) * 4, [pair, mine, other, got, swap(got)], "tile"
    )
    back = [visit(x, masks) for x, masks in zip(parts, visits)]
    keep, kept_loss, give = call(
        add_kernel,
        (wide(2, rows, depth), wide(2, rows, LANES), block(2, jnp.int16)),
        [parts[3], *back],
        "add",
    )
    loss, grad_image, grad_text = call(
        functools.partial(final_kernel, n * rows),
        (wide(1, rows), wide(rows, depth), wide(rows, depth)),
        [image_emb, text_emb, keep, kept_loss, swap(give)],
        "final",
    )
    return (loss[0], grad_image, grad_text)


def local(image_emb, text_emb, pair_class, scale, shift):
    if lax.axis_size("img") * lax.axis_size("txt") == 2 * 4 * 4 and lax.axis_size("txt") in (1, 2, 4):
        return chip_plan(image_emb, text_emb, pair_class, scale, shift)
    return tile_plan(image_emb, text_emb, pair_class, scale, shift)


def solution(mesh):
    in_specs = (P(AXES, None), P(AXES, None), P(AXES), P(), P())
    out_specs = (P(AXES), P(AXES, None), P(AXES, None))
    return jax.shard_map(local, mesh=mesh, in_specs=in_specs, out_specs=out_specs, check_vma=False)
```

```python
import functools

import jax
import jax.numpy as jnp
from jax import lax
from jax.experimental import pallas as pl
from jax.experimental.pallas import tpu as pltpu
from jax.sharding import PartitionSpec as P

AXES = ("img", "txt")
DIGITS = 4
LANES = 128
TOP = 32767.0


def unit_rows(rows):
    wide = rows.astype(jnp.float32)
    inverse = 1.0 / jnp.sqrt(jnp.sum(wide * wide, axis=1, keepdims=True) + 1e-06)
    return (wide * inverse, inverse)


def project_back(unit, inverse, pull):
    inner = jnp.sum(unit * pull, axis=1, keepdims=True)
    return (pull - unit * inner) * inverse


def class_digits(class_ref):
    rows = class_ref.shape[0]
    across = jnp.broadcast_to(class_ref[...][None, :], (rows, rows))
    row = lax.broadcasted_iota(jnp.int32, (rows, rows), 0)
    column = lax.broadcasted_iota(jnp.int32, (rows, rows), 1)
    lane = lax.broadcasted_iota(jnp.int32, (rows, LANES), 1)
    digits = jnp.zeros((rows, LANES), jnp.float32)
    for k in range(DIGITS):
        byte = (lax.shift_right_logical(across, 8 * k) & 255).astype(jnp.float32)
        down = jnp.sum(jnp.where(row == column, byte, 0.0), axis=1, keepdims=True)
        digits = jnp.where(lane == k, down, digits)
    return digits.astype(jnp.bfloat16)


def pack_kernel(rows_ref, class_ref, out_ref):
    depth = rows_ref.shape[1]
    out_ref[:, :depth] = unit_rows(rows_ref[...])[0].astype(jnp.bfloat16)
    out_ref[:, depth:] = class_digits(class_ref)


def put_blocks(out_ref, refs):
    start = 0
    for ref in refs:
        out_ref[start : start + ref.shape[0], :] = ref[...]
        start += ref.shape[0]


def join_kernel(*refs):
    put_blocks(refs[-1], refs[:-1])


def join_with_pair_kernel(scale_ref, shift_ref, *refs):
    put_blocks(refs[-2], refs[:-2])
    row = lax.broadcasted_iota(jnp.int32, refs[-1].shape, 0)
    refs[-1][...] = jnp.where(row == 0, scale_ref[0], shift_ref[0])


def power_above(size):
    return jnp.ceil(jnp.log2(jnp.maximum(size, 1e-30)) + 0.01)


def code(values, power):
    steps = jnp.clip(jnp.round(values * (TOP / jnp.exp2(power))), -TOP, TOP)
    return steps.astype(jnp.int32).astype(jnp.int16)


def decode(steps, power):
    return steps.astype(jnp.int32).astype(jnp.float32) * (jnp.exp2(power) * (1.0 / TOP))


def put_rows(outs, pull, loss):
    blocks, (rows, width) = len(outs), outs[0].shape
    depth = width - LANES
    power = power_above(jnp.max(jnp.abs(pull), axis=1, keepdims=True))
    steps = code(pull, power)
    lane = lax.broadcasted_iota(jnp.int32, (blocks * rows, LANES), 1)
    loss_power = power_above(loss)
    tail = jnp.where(lane == 0, power, 0.0)
    tail = jnp.where(lane == 1, loss_power, tail)
    tail = jnp.where(lane == 2, jnp.round(loss * (TOP / jnp.exp2(loss_power))), tail)
    tail = tail.astype(jnp.int32).astype(jnp.int16)
    for k, out in enumerate(outs):
        out[:, :depth] = steps[k * rows : (k + 1) * rows]
        out[:, depth:] = tail[k * rows : (k + 1) * rows]


def partial_pull(lines, columns, scale, shift):
    depth = lines.shape[1] - LANES
    logits = (
        scale
        * lax.dot_general(
            lines[:, :depth],
            columns[:, :depth],
            (((1,), (1,)), ((), ())),
            preferred_element_type=jnp.float32,
        )
        + shift
    )
    pick = (
        lax.broadcasted_iota(jnp.int32, (8, LANES), 0)
        == lax.broadcasted_iota(jnp.int32, (8, LANES), 1)
    )
    column_digits = lax.dot_general(
        pick.astype(jnp.bfloat16),
        columns[:, depth:],
        (((1,), (1,)), ((), ())),
        preferred_element_type=jnp.float32,
    )
    line_digits = lines[:, depth:].astype(jnp.float32)
    same = None
    for k in range(DIGITS):
        equal = line_digits[:, k : k + 1] == column_digits[k : k + 1, :]
        same = equal if same is None else same & equal
    sign = jnp.where(same, 1.0, -1.0).astype(jnp.float32)
    margin = sign * logits
    small = jnp.exp(-jnp.abs(margin))
    over = 1.0 / (1.0 + small)
    coef = -sign * jnp.where(margin >= 0, small * over, over) * scale
    pull = jnp.dot(
        coef.astype(jnp.bfloat16), columns[:, :depth], preferred_element_type=jnp.float32
    )
    loss = jnp.sum(jnp.log1p(small) - jnp.minimum(margin, 0.0), axis=1, keepdims=True)
    return pull, loss


def lines_kernel(pair_ref, lines_ref, columns_ref, other_columns_ref, out_ref):
    scale, shift = pair_ref[0:1, 0:1], pair_ref[1:2, 0:1]
    columns = jnp.concatenate([columns_ref[...], other_columns_ref[...]], axis=0)
    pull, loss = partial_pull(lines_ref[...], columns, scale, shift)
    put_rows([out_ref], pull, loss)


def final_kernel(a, b, image_ref, text_ref, *refs):
    image_parts, text_parts = refs[:a], refs[a : a + b]
    loss_ref, grad_image_ref, grad_text_ref = refs[a + b :]
    rows, depth = image_ref.shape
    pairs = 2 * rows * a * b
    for source, parts, out in (
        (image_ref, image_parts, grad_image_ref),
        (text_ref, text_parts, grad_text_ref),
    ):
        unit, inverse = unit_rows(source[...])
        pull = jnp.zeros((rows, depth), jnp.float32)
        loss = jnp.zeros((rows, 1), jnp.float32)
        for part in parts:
            tail = part[:, depth:].astype(jnp.int32).astype(jnp.float32)
            pull = pull + decode(part[:, :depth], tail[:, 0:1])
            loss = loss + tail[:, 2:3] * (jnp.exp2(tail[:, 1:2]) * (1.0 / TOP))
        out[...] = project_back(unit, inverse, pull)
        if out is grad_image_ref:
            row = lax.broadcasted_iota(jnp.int32, (rows, rows), 0)
            column = lax.broadcasted_iota(jnp.int32, (rows, rows), 1)
            across = jnp.where(row == column, loss / pairs, 0.0)
            loss_ref[...] = jnp.sum(across, axis=0, keepdims=True)


def partner(place, k, size):
    return place ^ k if size & (size - 1) == 0 else (place + k) % size


def local(image_emb, text_emb, pair_class, scale, shift):
    rows, depth = image_emb.shape
    width = depth + LANES
    lanes = lax.axis_size("txt")
    n = lax.axis_size("img") * lanes
    chips = n // 2
    b = min(d for d in range(1, chips + 1) if chips % d == 0 and d * d >= chips)
    a = chips // b
    vmem = pl.BlockSpec(memory_space=pltpu.VMEM)
    smem = pl.BlockSpec(memory_space=pltpu.SMEM)
    params = pltpu.CompilerParams(vmem_limit_bytes=32 << 20)

    def split(i):
        return i // (2 * lanes) * lanes + i % lanes, i // lanes % 2

    def place(chip, core):
        return (chip // lanes * 2 + core) * lanes + chip % lanes

    def along_a(i, k):
        chip, core = split(i)
        return place(partner(chip // b, k, a) * b + chip % b, core)

    def along_b(i, k):
        chip, core = split(i)
        return place(chip // b * b + partner(chip % b, k, b), core)

    def move(x, pairs):
        return lax.ppermute(x, AXES, pairs)

    def call(kernel, shapes, operands, name, scalars=0, after=()):
        def body(*refs):
            kernel(*refs[len(after) :])

        return pl.pallas_call(
            body,
            out_shape=shapes,
            in_specs=[pl.BlockSpec(memory_space=pl.ANY)] * len(after)
            + [smem] * scalars
            + [vmem] * (len(operands) - scalars),
            out_specs=jax.tree.map(lambda _: vmem, shapes),
            compiler_params=params,
            name=name,
        )(*after, *operands)

    def block(count, dtype=jnp.bfloat16):
        return jax.ShapeDtypeStruct((count * rows, width), dtype)

    def wide(*shape):
        return jax.ShapeDtypeStruct(shape, jnp.float32)

    def fetch(x, k, along):
        return move(x, [(along(i, k), i) for i in range(n)])

    def give(x, k, along):
        return move(x, [(i, along(i, k)) for i in range(n)])

    def swap(x):
        return move(x, [(i, place(split(i)[0], 1 - split(i)[1])) for i in range(n)])

    far_a, far_b = range(a - 1, 0, -1), range(b - 1, 0, -1)
    own_texts = call(pack_kernel, block(1), [text_emb, pair_class], "pack_texts")
    own_images = call(
        pack_kernel, block(1), [image_emb, pair_class], "pack_images", after=[own_texts]
    )
    texts = [own_texts] + [fetch(own_texts, k, along_b) for k in far_b]
    got_texts = dict(zip([0, *far_b], texts))
    images = [own_images] + [fetch(own_images, k, along_a) for k in far_a]
    texts, pair = call(
        join_with_pair_kernel,
        (block(b), wide(8, LANES)),
        [scale[None], shift[None], *texts[::-1]],
        "join_texts",
        2,
        after=images[2:0:-1],
    )
    other_texts = swap(texts)
    image_parts = [
        call(
            lines_kernel,
            block(1, jnp.int16),
            [pair, x, texts, other_texts],
            "image_lines",
        )
        for x in images
    ]
    given = [give(x, k, along_a) for x, k in zip(image_parts[1:], far_a)]
    images = call(join_kernel, block(a), images, "join_images", after=image_parts[1:-1])
    other_images = swap(images)
    text_parts = []
    for position, k in enumerate([*far_b, 0]):
        after = given[position - 1 : position] if position else []
        part = call(
            lines_kernel,
            block(1, jnp.int16),
            [pair, got_texts[k], images, other_images],
            "text_lines",
            after=after,
        )
        text_parts.append(give(part, k, along_b) if k else part)
    image_parts = [image_parts[0]] + given
    loss, grad_image, grad_text = call(
        functools.partial(final_kernel, a, b),
        (wide(1, rows), wide(rows, depth), wide(rows, depth)),
        [image_emb, text_emb, *image_parts, *text_parts],
        "final",
    )
    return (loss[0], grad_image, grad_text)


def solution(mesh):
    in_specs = (P(AXES, None), P(AXES, None), P(AXES), P(), P())
    out_specs = (P(AXES), P(AXES, None), P(AXES, None))
    return jax.shard_map(local, mesh=mesh, in_specs=in_specs, out_specs=out_specs, check_vma=False)
```

```python
import functools

import jax
import jax.numpy as jnp
from jax import lax
from jax.experimental import pallas as pl
from jax.experimental.pallas import tpu as pltpu
from jax.sharding import PartitionSpec as P

AXES = ("img", "txt")
DIGITS = 4
LANES = 128
TOP = 32767.0


def unit_rows(rows):
    wide = rows.astype(jnp.float32)
    inverse = 1.0 / jnp.sqrt(jnp.sum(wide * wide, axis=1, keepdims=True) + 1e-06)
    return (wide * inverse, inverse)


def project_back(unit, inverse, pull):
    inner = jnp.sum(unit * pull, axis=1, keepdims=True)
    return (pull - unit * inner) * inverse


def tile_terms(rows_half, row_class, cols_half, col_class, scale, shift):
    logits = (
        scale
        * lax.dot_general(
            rows_half, cols_half, (((1,), (1,)), ((), ())), preferred_element_type=jnp.float32
        )
        + shift
    )
    sign = jnp.where(row_class[:, None] == col_class[None, :], 1.0, -1.0).astype(jnp.float32)
    margin = sign * logits
    loss_part = -jnp.sum(jax.nn.log_sigmoid(margin), axis=1)
    coef = (-sign * jax.nn.sigmoid(-margin) * scale).astype(jnp.bfloat16)
    return (coef, loss_part)


def tile_plan(image_emb, text_emb, pair_class, scale, shift):
    image_unit, image_inv = unit_rows(image_emb)
    text_unit, text_inv = unit_rows(text_emb)
    own_rows = text_emb.shape[0]
    pairs = own_rows * lax.axis_size("img") * lax.axis_size("txt")
    text_half = text_unit.astype(jnp.bfloat16)
    rows_half, row_class = (
        lax.all_gather(image_unit.astype(jnp.bfloat16), "txt", axis=0, tiled=True),
        lax.all_gather(pair_class, "txt", axis=0, tiled=True),
    )
    cols_half, col_class = (
        lax.all_gather(text_half, "img", axis=0, tiled=True),
        lax.all_gather(pair_class, "img", axis=0, tiled=True),
    )
    coef, loss_part = tile_terms(rows_half, row_class, cols_half, col_class, scale, shift)
    image_pull = jnp.dot(coef, cols_half, preferred_element_type=jnp.float32)
    text_pull = lax.psum_scatter(
        lax.dot_general(
            coef, rows_half, (((0,), (0,)), ((), ())), preferred_element_type=jnp.float32
        ),
        "img",
        scatter_dimension=0,
        tiled=True,
    )
    image_sum, loss_sum = (
        lax.psum_scatter(image_pull, "txt", scatter_dimension=0, tiled=True),
        lax.psum_scatter(loss_part, "txt", scatter_dimension=0, tiled=True),
    )
    row_loss = loss_sum / pairs
    grad_image = project_back(image_unit, image_inv, image_sum)
    grad_text = project_back(text_unit, text_inv, text_pull)
    return (row_loss, grad_image, grad_text)


def on_first_core():
    return lax.rem(lax.axis_index("img"), 2) == 0


def class_digits(class_ref):
    rows = class_ref.shape[0]
    across = jnp.broadcast_to(class_ref[...][None, :], (rows, rows))
    row = lax.broadcasted_iota(jnp.int32, (rows, rows), 0)
    column = lax.broadcasted_iota(jnp.int32, (rows, rows), 1)
    lane = lax.broadcasted_iota(jnp.int32, (rows, LANES), 1)
    digits = jnp.zeros((rows, LANES), jnp.float32)
    for k in range(DIGITS):
        byte = (lax.shift_right_logical(across, 8 * k) & 255).astype(jnp.float32)
        down = jnp.sum(jnp.where(row == column, byte, 0.0), axis=1, keepdims=True)
        digits = jnp.where(lane == k, down, digits)
    return digits.astype(jnp.bfloat16)


def digits_kernel(class_ref, digits_ref):
    digits_ref[...] = class_digits(class_ref)


def pack_kernel(image_ref, text_ref, digits_ref, out_ref):
    rows, depth = image_ref.shape
    for start, source in ((0, image_ref), (rows, text_ref)):
        out_ref[start : start + rows, :depth] = unit_rows(source[...])[0].astype(jnp.bfloat16)
        out_ref[start : start + rows, depth:] = digits_ref[...]


def join_kernel(scale_ref, shift_ref, own_ref, got_ref, *refs):
    first = on_first_core()
    rows = own_ref.shape[0] // 2
    own, got = own_ref[...].astype(jnp.float32), got_ref[...].astype(jnp.float32)
    low, high = jnp.where(first, own, got), jnp.where(first, got, own)
    images = jnp.concatenate([low[:rows], high[:rows]], axis=0)
    texts = jnp.concatenate([low[rows:], high[rows:]], axis=0)
    mine = jnp.where(first, images, texts).astype(jnp.bfloat16)
    other = jnp.where(first, texts, images).astype(jnp.bfloat16)
    for ref, block in zip(refs[:-1], (mine, other, mine, mine, other)):
        ref[...] = block
    pair_ref = refs[-1]
    row = lax.broadcasted_iota(jnp.int32, pair_ref.shape, 0)
    pair_ref[...] = jnp.where(row == 0, scale_ref[0], shift_ref[0])


def gather_kernel(*refs):
    rows = refs[0].shape[0]
    for k, ref in enumerate(refs[:-1]):
        refs[-1][k * rows : (k + 1) * rows, :] = ref[...]


def power_above(size):
    return jnp.ceil(jnp.log2(jnp.maximum(size, 1e-30)) + 0.01)


def code(values, power):
    steps = jnp.clip(jnp.round(values * (TOP / jnp.exp2(power))), -TOP, TOP)
    return steps.astype(jnp.int32).astype(jnp.int16)


def decode(steps, power):
    return steps.astype(jnp.int32).astype(jnp.float32) * (jnp.exp2(power) * (1.0 / TOP))


def put_rows(outs, pull, loss):
    blocks, (rows, width) = len(outs), outs[0].shape
    depth = width - LANES
    power = power_above(jnp.max(jnp.abs(pull), axis=1, keepdims=True))
    steps = code(pull, power)
    lane = lax.broadcasted_iota(jnp.int32, (blocks * rows, LANES), 1)
    loss_power = power_above(loss)
    tail = jnp.where(lane == 0, power, 0.0)
    tail = jnp.where(lane == 1, loss_power, tail)
    tail = jnp.where(lane == 2, jnp.round(loss * (TOP / jnp.exp2(loss_power))), tail)
    tail = tail.astype(jnp.int32).astype(jnp.int16)
    for k, out in enumerate(outs):
        out[:, :depth] = steps[k * rows : (k + 1) * rows]
        out[:, depth:] = tail[k * rows : (k + 1) * rows]


def partial_pull(lines, columns, scale, shift):
    depth = lines.shape[1] - LANES
    logits = (
        scale
        * lax.dot_general(
            lines[:, :depth],
            columns[:, :depth],
            (((1,), (1,)), ((), ())),
            preferred_element_type=jnp.float32,
        )
        + shift
    )
    pick = (
        lax.broadcasted_iota(jnp.int32, (8, LANES), 0)
        == lax.broadcasted_iota(jnp.int32, (8, LANES), 1)
    )
    column_digits = lax.dot_general(
        pick.astype(jnp.bfloat16),
        columns[:, depth:],
        (((1,), (1,)), ((), ())),
        preferred_element_type=jnp.float32,
    )
    line_digits = lines[:, depth:].astype(jnp.float32)
    same = None
    for k in range(DIGITS):
        equal = line_digits[:, k : k + 1] == column_digits[k : k + 1, :]
        same = equal if same is None else same & equal
    sign = jnp.where(same, 1.0, -1.0).astype(jnp.float32)
    margin = sign * logits
    small = jnp.exp(-jnp.abs(margin))
    over = 1.0 / (1.0 + small)
    coef = -sign * jnp.where(margin >= 0, small * over, over) * scale
    pull = jnp.dot(
        coef.astype(jnp.bfloat16), columns[:, :depth], preferred_element_type=jnp.float32
    )
    loss = jnp.sum(jnp.log1p(small) - jnp.minimum(margin, 0.0), axis=1, keepdims=True)
    return pull, loss


def tile_kernel(pair_ref, mine_ref, other_ref, got_ref, swapped_ref, *outs):
    rows = mine_ref.shape[0]
    scale, shift = pair_ref[0:1, 0:1], pair_ref[1:2, 0:1]
    got = [got_ref[k * rows : (k + 1) * rows, :] for k in range(3)]
    swapped = [swapped_ref[k * rows : (k + 1) * rows, :] for k in range(3)]
    mine_side = jnp.concatenate([mine_ref[...], got[0], swapped[1], got[2]], axis=0)
    other_side = jnp.concatenate([other_ref[...], swapped[0], got[1], swapped[2]], axis=0)
    lines = jnp.concatenate([got[0], got[2], mine_ref[...]], axis=0)
    put_rows([outs[0], outs[2], outs[3]], *partial_pull(lines, other_side, scale, shift))
    put_rows([outs[1]], *partial_pull(got[1], mine_side, scale, shift))


def total(parts, rows, depth):
    pull = jnp.zeros((rows, depth), jnp.float32)
    loss = jnp.zeros((rows, 1), jnp.float32)
    for part in parts:
        tail = part[:, depth:].astype(jnp.int32).astype(jnp.float32)
        pull = pull + decode(part[:, :depth], tail[:, 0:1])
        loss = loss + tail[:, 2:3] * (jnp.exp2(tail[:, 1:2]) * (1.0 / TOP))
    return pull, loss


def place_of(first, rows):
    own = pl.multiple_of(jnp.where(first, 0, rows), rows)
    return pl.ds(own, rows), pl.ds(pl.multiple_of(rows - own, rows), rows)


def add_kernel(own_ref, back_0, back_1, back_2, keep_ref, loss_ref, give_ref):
    rows, depth = keep_ref.shape[1:]
    own, other = place_of(on_first_core(), rows)
    for side, parts in enumerate(((own_ref, back_0, back_2), (back_1,))):
        keep_ref[side], loss = total([part[own, :] for part in parts], rows, depth)
        loss_ref[side] = jnp.broadcast_to(loss, loss_ref.shape[1:])
        pull, loss = total([part[other, :] for part in parts], rows, depth)
        put_rows([give_ref.at[side * rows : (side + 1) * rows, :]], pull, loss)


def final_kernel(pairs, image_ref, text_ref, keep_ref, kept_loss_ref, got_ref, loss_ref, grad_image_ref, grad_text_ref):
    first = on_first_core()
    rows, depth = image_ref.shape
    pulls, losses = [], []
    for side in (0, 1):
        pull, loss = total([got_ref[(1 - side) * rows : (2 - side) * rows, :]], rows, depth)
        pulls.append(keep_ref[side] + pull)
        losses.append(kept_loss_ref[side][:, 0:1] + loss)
    for source, pull, out in (
        (image_ref, jnp.where(first, pulls[0], pulls[1]), grad_image_ref),
        (text_ref, jnp.where(first, pulls[1], pulls[0]), grad_text_ref),
    ):
        unit, inverse = unit_rows(source[...])
        out[...] = project_back(unit, inverse, pull)
    row = lax.broadcasted_iota(jnp.int32, (rows, rows), 0)
    column = lax.broadcasted_iota(jnp.int32, (rows, rows), 1)
    loss = jnp.where(first, losses[0], losses[1])
    across = jnp.where(row == column, loss / pairs, 0.0)
    loss_ref[...] = jnp.sum(across, axis=0, keepdims=True)


def chip_plan(image_emb, text_emb, pair_class, scale, shift):
    rows, depth = image_emb.shape
    width = depth + LANES
    lanes = lax.axis_size("txt")
    n = lax.axis_size("img") * lanes
    vmem = pl.BlockSpec(memory_space=pltpu.VMEM)
    smem = pl.BlockSpec(memory_space=pltpu.SMEM)

    def call(kernel, shapes, operands, name, scalars=0, cost=None):
        return pl.pallas_call(
            kernel,
            cost_estimate=cost,
            out_shape=shapes,
            in_specs=[smem] * scalars + [vmem] * (len(operands) - scalars),
            out_specs=jax.tree.map(lambda _: vmem, shapes),
            compiler_params=pltpu.CompilerParams(vmem_limit_bytes=32 << 20),
            name=name,
        )(*operands)

    def block(count, dtype=jnp.bfloat16):
        return jax.ShapeDtypeStruct((count * rows, width), dtype)

    def wide(*shape):
        return jax.ShapeDtypeStruct(shape, jnp.float32)

    def core(i):
        return i // lanes % 2

    def visit(x, masks):
        pairs = []
        for i in range(n):
            chip = (i // (2 * lanes) * lanes + i % lanes) ^ masks[core(i)]
            pairs.append((i, (chip // lanes * 2 + core(i)) * lanes + chip % lanes))
        return lax.ppermute(x, AXES, pairs)

    def swap(x):
        return lax.ppermute(x, AXES, [(i, i ^ lanes) for i in range(n)])

    visits = ((12, 3), (2, 8), (4, 1))
    digits = call(
        digits_kernel, jax.ShapeDtypeStruct((rows, LANES), jnp.bfloat16), [pair_class], "digits", cost=pl.CostEstimate(flops=10**9, bytes_accessed=10**7, transcendentals=0)
    )
    own = call(pack_kernel, block(2), [image_emb, text_emb, digits], "pack")
    *sent, mine, other, pair = call(
        join_kernel,
        (block(2),) * 5 + (wide(8, LANES),),
        [scale[None], shift[None], own, swap(own)],
        "join",
        2,
    )
    got = [visit(x, masks) for x, masks in zip(sent, visits)]
    got = call(gather_kernel, block(6), got, "gather")
    parts = call(
        tile_kernel, (block(2, jnp.int16),) * 4, [pair, mine, other, got, swap(got)], "tile"
    )
    back = [visit(x, masks) for x, masks in zip(parts, visits)]
    keep, kept_loss, give = call(
        add_kernel,
        (wide(2, rows, depth), wide(2, rows, LANES), block(2, jnp.int16)),
        [parts[3], *back],
        "add",
    )
    loss, grad_image, grad_text = call(
        functools.partial(final_kernel, n * rows),
        (wide(1, rows), wide(rows, depth), wide(rows, depth)),
        [image_emb, text_emb, keep, kept_loss, swap(give)],
        "final",
    )
    return (loss[0], grad_image, grad_text)


def local(image_emb, text_emb, pair_class, scale, shift):
    if lax.axis_size("img") * lax.axis_size("txt") == 2 * 4 * 4 and lax.axis_size("txt") in (1, 2, 4):
        return chip_plan(image_emb, text_emb, pair_class, scale, shift)
    return tile_plan(image_emb, text_emb, pair_class, scale, shift)


def solution(mesh):
    in_specs = (P(AXES, None), P(AXES, None), P(AXES), P(), P())
    out_specs = (P(AXES), P(AXES, None), P(AXES, None))
    return jax.shard_map(local, mesh=mesh, in_specs=in_specs, out_specs=out_specs, check_vma=False)
```

```python
import functools

import jax
import jax.numpy as jnp
from jax import lax
from jax.experimental import pallas as pl
from jax.experimental.pallas import tpu as pltpu
from jax.sharding import PartitionSpec as P

AXES = ("img", "txt")
DIGITS = 4
LANES = 128
TOP = 32767.0


def unit_rows(rows):
    wide = rows.astype(jnp.float32)
    inverse = 1.0 / jnp.sqrt(jnp.sum(wide * wide, axis=1, keepdims=True) + 1e-06)
    return (wide * inverse, inverse)


def project_back(unit, inverse, pull):
    inner = jnp.sum(unit * pull, axis=1, keepdims=True)
    return (pull - unit * inner) * inverse


def tile_terms(rows_half, row_class, cols_half, col_class, scale, shift):
    logits = (
        scale
        * lax.dot_general(
            rows_half, cols_half, (((1,), (1,)), ((), ())), preferred_element_type=jnp.float32
        )
        + shift
    )
    sign = jnp.where(row_class[:, None] == col_class[None, :], 1.0, -1.0).astype(jnp.float32)
    margin = sign * logits
    loss_part = -jnp.sum(jax.nn.log_sigmoid(margin), axis=1)
    coef = (-sign * jax.nn.sigmoid(-margin) * scale).astype(jnp.bfloat16)
    return (coef, loss_part)


def tile_plan(image_emb, text_emb, pair_class, scale, shift):
    image_unit, image_inv = unit_rows(image_emb)
    text_unit, text_inv = unit_rows(text_emb)
    own_rows = text_emb.shape[0]
    pairs = own_rows * lax.axis_size("img") * lax.axis_size("txt")
    text_half = text_unit.astype(jnp.bfloat16)
    rows_half, row_class = (
        lax.all_gather(image_unit.astype(jnp.bfloat16), "txt", axis=0, tiled=True),
        lax.all_gather(pair_class, "txt", axis=0, tiled=True),
    )
    cols_half, col_class = (
        lax.all_gather(text_half, "img", axis=0, tiled=True),
        lax.all_gather(pair_class, "img", axis=0, tiled=True),
    )
    coef, loss_part = tile_terms(rows_half, row_class, cols_half, col_class, scale, shift)
    image_pull = jnp.dot(coef, cols_half, preferred_element_type=jnp.float32)
    text_pull = lax.psum_scatter(
        lax.dot_general(
            coef, rows_half, (((0,), (0,)), ((), ())), preferred_element_type=jnp.float32
        ),
        "img",
        scatter_dimension=0,
        tiled=True,
    )
    image_sum, loss_sum = (
        lax.psum_scatter(image_pull, "txt", scatter_dimension=0, tiled=True),
        lax.psum_scatter(loss_part, "txt", scatter_dimension=0, tiled=True),
    )
    row_loss = loss_sum / pairs
    grad_image = project_back(image_unit, image_inv, image_sum)
    grad_text = project_back(text_unit, text_inv, text_pull)
    return (row_loss, grad_image, grad_text)


def on_first_core():
    return lax.rem(lax.axis_index("img"), 2) == 0


def class_digits(class_ref):
    rows = class_ref.shape[0]
    across = jnp.broadcast_to(class_ref[...][None, :], (rows, rows))
    row = lax.broadcasted_iota(jnp.int32, (rows, rows), 0)
    column = lax.broadcasted_iota(jnp.int32, (rows, rows), 1)
    lane = lax.broadcasted_iota(jnp.int32, (rows, LANES), 1)
    digits = jnp.zeros((rows, LANES), jnp.float32)
    for k in range(DIGITS):
        byte = (lax.shift_right_logical(across, 8 * k) & 255).astype(jnp.float32)
        down = jnp.sum(jnp.where(row == column, byte, 0.0), axis=1, keepdims=True)
        digits = jnp.where(lane == k, down, digits)
    return digits.astype(jnp.bfloat16)


def digits_kernel(class_ref, digits_ref):
    digits_ref[...] = class_digits(class_ref)


def pack_kernel(image_ref, text_ref, digits_ref, out_ref):
    rows, depth = image_ref.shape
    for start, source in ((0, image_ref), (rows, text_ref)):
        out_ref[start : start + rows, :depth] = unit_rows(source[...])[0].astype(jnp.bfloat16)
        out_ref[start : start + rows, depth:] = digits_ref[...]


def join_kernel(scale_ref, shift_ref, own_ref, got_ref, *refs):
    first = on_first_core()
    rows = own_ref.shape[0] // 2
    own, got = own_ref[...].astype(jnp.float32), got_ref[...].astype(jnp.float32)
    low, high = jnp.where(first, own, got), jnp.where(first, got, own)
    images = jnp.concatenate([low[:rows], high[:rows]], axis=0)
    texts = jnp.concatenate([low[rows:], high[rows:]], axis=0)
    mine = jnp.where(first, images, texts).astype(jnp.bfloat16)
    other = jnp.where(first, texts, images).astype(jnp.bfloat16)
    for ref, block in zip(refs[:-1], (mine, other, mine, mine, other)):
        ref[...] = block
    pair_ref = refs[-1]
    row = lax.broadcasted_iota(jnp.int32, pair_ref.shape, 0)
    pair_ref[...] = jnp.where(row == 0, scale_ref[0], shift_ref[0])


def gather_kernel(*refs):
    rows = refs[0].shape[0]
    for k, ref in enumerate(refs[:-1]):
        refs[-1][k * rows : (k + 1) * rows, :] = ref[...]


def power_above(size):
    return jnp.ceil(jnp.log2(jnp.maximum(size, 1e-30)) + 0.01)


def nearest(values):
    return jnp.floor(values + 0.5).astype(jnp.int32)


def code(values, power):
    return nearest(values * (TOP / jnp.exp2(power))).astype(jnp.int16)


def decode(steps, power):
    return steps.astype(jnp.int32).astype(jnp.float32) * (jnp.exp2(power) * (1.0 / TOP))


def put_rows(outs, pull, loss):
    blocks, (rows, width) = len(outs), outs[0].shape
    depth = width - LANES
    power = power_above(jnp.max(jnp.abs(pull), axis=1, keepdims=True))
    steps = code(pull, power)
    lane = lax.broadcasted_iota(jnp.int32, (blocks * rows, LANES), 1)
    loss_power = power_above(loss)
    tail = jnp.where(lane == 0, power, 0.0)
    tail = jnp.where(lane == 1, loss_power, tail)
    tail = jnp.where(lane == 2, loss * (TOP / jnp.exp2(loss_power)), tail)
    tail = nearest(tail).astype(jnp.int16)
    for k, out in enumerate(outs):
        out[:, :depth] = steps[k * rows : (k + 1) * rows]
        out[:, depth:] = tail[k * rows : (k + 1) * rows]


def partial_pull(lines, columns, scale, shift):
    depth = lines.shape[1] - LANES
    logits = (
        scale
        * lax.dot_general(
            lines[:, :depth],
            columns[:, :depth],
            (((1,), (1,)), ((), ())),
            preferred_element_type=jnp.float32,
        )
        + shift
    )
    pick = (
        lax.broadcasted_iota(jnp.int32, (8, LANES), 0)
        == lax.broadcasted_iota(jnp.int32, (8, LANES), 1)
    )
    column_digits = lax.dot_general(
        pick.astype(jnp.bfloat16),
        columns[:, depth:],
        (((1,), (1,)), ((), ())),
        preferred_element_type=jnp.float32,
    )
    line_digits = lines[:, depth:].astype(jnp.float32)
    same = None
    for k in range(DIGITS):
        equal = line_digits[:, k : k + 1] == column_digits[k : k + 1, :]
        same = equal if same is None else same & equal
    sign = jnp.where(same, 1.0, -1.0).astype(jnp.float32)
    margin = sign * logits
    small = jnp.exp(-jnp.abs(margin))
    over = 1.0 / (1.0 + small)
    coef = -sign * jnp.where(margin >= 0, small * over, over) * scale
    pull = jnp.dot(
        coef.astype(jnp.bfloat16), columns[:, :depth], preferred_element_type=jnp.float32
    )
    loss = jnp.sum(jnp.log1p(small) - jnp.minimum(margin, 0.0), axis=1, keepdims=True)
    return pull, loss


def tile_kernel(pair_ref, mine_ref, other_ref, got_ref, swapped_ref, *outs):
    rows = mine_ref.shape[0]
    scale, shift = pair_ref[0:1, 0:1], pair_ref[1:2, 0:1]
    got = [got_ref[k * rows : (k + 1) * rows, :] for k in range(3)]
    swapped = [swapped_ref[k * rows : (k + 1) * rows, :] for k in range(3)]
    mine_side = jnp.concatenate([mine_ref[...], got[0], swapped[1], got[2]], axis=0)
    other_side = jnp.concatenate([other_ref[...], swapped[0], got[1], swapped[2]], axis=0)
    lines = jnp.concatenate([got[0], mine_ref[...], got[2]], axis=0)
    pull, loss = partial_pull(lines, other_side, scale, shift)
    put_rows([outs[0], outs[4]], pull[: 2 * rows], loss[: 2 * rows])
    half = rows // 2
    first = on_first_core()
    last = []
    for part in (pull, loss):
        low, high = part[2 * rows : 2 * rows + half], part[2 * rows + half :]
        last.append((jnp.where(first, low, high), jnp.where(first, high, low)))
    for out, part, part_loss in zip(outs[2:4], *last):
        put_rows([out], part, part_loss)
    put_rows([outs[1]], *partial_pull(got[1], mine_side, scale, shift))


def total(parts, rows, depth):
    pull = jnp.zeros((rows, depth), jnp.float32)
    loss = jnp.zeros((rows, 1), jnp.float32)
    for part in parts:
        tail = part[:, depth:].astype(jnp.int32).astype(jnp.float32)
        pull = pull + decode(part[:, :depth], tail[:, 0:1])
        loss = loss + tail[:, 2:3] * (jnp.exp2(tail[:, 1:2]) * (1.0 / TOP))
    return pull, loss


def place_of(first, rows):
    own = pl.multiple_of(jnp.where(first, 0, rows), rows)
    return pl.ds(own, rows), pl.ds(pl.multiple_of(rows - own, rows), rows)


def add_kernel(own_ref, back_0, back_1, keep_ref, loss_ref, give_ref):
    rows, depth = keep_ref.shape[1:]
    own, other = place_of(on_first_core(), rows)
    for side, parts in enumerate(((own_ref, back_0), (back_1,))):
        keep_ref[side], loss = total([part[own, :] for part in parts], rows, depth)
        loss_ref[side] = jnp.broadcast_to(loss, loss_ref.shape[1:])
        pull, loss = total([part[other, :] for part in parts], rows, depth)
        put_rows([give_ref.at[side * rows : (side + 1) * rows, :]], pull, loss)


def more_kernel(keep_ref, kept_loss_ref, same_ref, cross_ref, sum_ref, sum_loss_ref):
    rows, depth = keep_ref.shape[1:]
    for side, ref in enumerate((same_ref, cross_ref)):
        pull, loss = total([ref[...]], rows, depth)
        sum_ref[side] = keep_ref[side] + pull
        sum_loss_ref[side] = kept_loss_ref[side] + loss


def final_kernel(pairs, image_ref, text_ref, keep_ref, kept_loss_ref, got_ref, loss_ref, grad_image_ref, grad_text_ref):
    first = on_first_core()
    rows, depth = image_ref.shape
    pulls, losses = [], []
    for side in (0, 1):
        pull, loss = total([got_ref[(1 - side) * rows : (2 - side) * rows, :]], rows, depth)
        pulls.append(keep_ref[side] + pull)
        losses.append(kept_loss_ref[side][:, 0:1] + loss)
    for source, pull, out in (
        (image_ref, jnp.where(first, pulls[0], pulls[1]), grad_image_ref),
        (text_ref, jnp.where(first, pulls[1], pulls[0]), grad_text_ref),
    ):
        unit, inverse = unit_rows(source[...])
        out[...] = project_back(unit, inverse, pull)
    row = lax.broadcasted_iota(jnp.int32, (rows, rows), 0)
    column = lax.broadcasted_iota(jnp.int32, (rows, rows), 1)
    loss = jnp.where(first, losses[0], losses[1])
    across = jnp.where(row == column, loss / pairs, 0.0)
    loss_ref[...] = jnp.sum(across, axis=0, keepdims=True)


def chip_plan(image_emb, text_emb, pair_class, scale, shift):
    rows, depth = image_emb.shape
    width = depth + LANES
    lanes = lax.axis_size("txt")
    n = lax.axis_size("img") * lanes
    vmem = pl.BlockSpec(memory_space=pltpu.VMEM)
    smem = pl.BlockSpec(memory_space=pltpu.SMEM)

    def call(kernel, shapes, operands, name, scalars=0, cost=None):
        return pl.pallas_call(
            kernel,
            cost_estimate=cost,
            out_shape=shapes,
            in_specs=[smem] * scalars + [vmem] * (len(operands) - scalars),
            out_specs=jax.tree.map(lambda _: vmem, shapes),
            compiler_params=pltpu.CompilerParams(vmem_limit_bytes=32 << 20),
            name=name,
        )(*operands)

    def block(count, dtype=jnp.bfloat16):
        return jax.ShapeDtypeStruct((count * rows, width), dtype)

    def wide(*shape):
        return jax.ShapeDtypeStruct(shape, jnp.float32)

    def core(i):
        return i // lanes % 2

    def visit(x, masks, cross=0):
        pairs = []
        for i in range(n):
            chip = (i // (2 * lanes) * lanes + i % lanes) ^ masks[core(i)]
            pairs.append((i, (chip // lanes * 2 + (core(i) ^ cross)) * lanes + chip % lanes))
        return lax.ppermute(x, AXES, pairs)

    def swap(x):
        return lax.ppermute(x, AXES, [(i, i ^ lanes) for i in range(n)])

    visits = ((12, 3), (2, 8), (4, 1))
    digits = call(
        digits_kernel, jax.ShapeDtypeStruct((rows, LANES), jnp.bfloat16), [pair_class], "digits", cost=pl.CostEstimate(flops=10**9, bytes_accessed=10**7, transcendentals=0)
    )
    own = call(pack_kernel, block(2), [image_emb, text_emb, digits], "pack")
    *sent, mine, other, pair = call(
        join_kernel,
        (block(2),) * 5 + (wide(8, LANES),),
        [scale[None], shift[None], own, swap(own)],
        "join",
        2,
    )
    got = [visit(x, masks) for x, masks in zip(sent, visits)]
    got = call(gather_kernel, block(6), got, "gather")
    one, two = block(1, jnp.int16), block(2, jnp.int16)
    parts = call(
        tile_kernel, (two, two, one, one, two), [pair, mine, other, got, swap(got)], "tile"
    )
    back = [visit(x, masks) for x, masks in zip(parts, visits)]
    cross = visit(parts[3], visits[2], 1)
    keep, kept_loss, give = call(
        add_kernel,
        (wide(2, rows, depth), wide(2, rows, LANES), two),
        [parts[4], *back[:2]],
        "add",
    )
    keep, kept_loss = call(
        more_kernel,
        (wide(2, rows, depth), wide(2, rows, LANES)),
        [keep, kept_loss, back[2], cross],
        "more",
        cost=pl.CostEstimate(flops=10**9, bytes_accessed=10**7, transcendentals=0),
    )
    loss, grad_image, grad_text = call(
        functools.partial(final_kernel, n * rows),
        (wide(1, rows), wide(rows, depth), wide(rows, depth)),
        [image_emb, text_emb, keep, kept_loss, swap(give)],
        "final",
    )
    return (loss[0], grad_image, grad_text)


def local(image_emb, text_emb, pair_class, scale, shift):
    if lax.axis_size("img") * lax.axis_size("txt") == 2 * 4 * 4 and lax.axis_size("txt") in (1, 2, 4):
        return chip_plan(image_emb, text_emb, pair_class, scale, shift)
    return tile_plan(image_emb, text_emb, pair_class, scale, shift)


def solution(mesh):
    in_specs = (P(AXES, None), P(AXES, None), P(AXES), P(), P())
    out_specs = (P(AXES), P(AXES, None), P(AXES, None))
    return jax.shard_map(local, mesh=mesh, in_specs=in_specs, out_specs=out_specs, check_vma=False)
```

```python
import functools

import jax
import jax.numpy as jnp
from jax import lax
from jax.experimental import pallas as pl
from jax.experimental.pallas import tpu as pltpu
from jax.sharding import PartitionSpec as P

AXES = ("img", "txt")
DIGITS = 4
LANES = 128
TOP = 32767.0


def unit_rows(rows):
    wide = rows.astype(jnp.float32)
    inverse = 1.0 / jnp.sqrt(jnp.sum(wide * wide, axis=1, keepdims=True) + 1e-06)
    return (wide * inverse, inverse)


def project_back(unit, inverse, pull):
    inner = jnp.sum(unit * pull, axis=1, keepdims=True)
    return (pull - unit * inner) * inverse


def tile_terms(rows_half, row_class, cols_half, col_class, scale, shift):
    logits = (
        scale
        * lax.dot_general(
            rows_half, cols_half, (((1,), (1,)), ((), ())), preferred_element_type=jnp.float32
        )
        + shift
    )
    sign = jnp.where(row_class[:, None] == col_class[None, :], 1.0, -1.0).astype(jnp.float32)
    margin = sign * logits
    loss_part = -jnp.sum(jax.nn.log_sigmoid(margin), axis=1)
    coef = (-sign * jax.nn.sigmoid(-margin) * scale).astype(jnp.bfloat16)
    return (coef, loss_part)


def tile_plan(image_emb, text_emb, pair_class, scale, shift):
    image_unit, image_inv = unit_rows(image_emb)
    text_unit, text_inv = unit_rows(text_emb)
    own_rows = text_emb.shape[0]
    pairs = own_rows * lax.axis_size("img") * lax.axis_size("txt")
    text_half = text_unit.astype(jnp.bfloat16)
    rows_half, row_class = (
        lax.all_gather(image_unit.astype(jnp.bfloat16), "txt", axis=0, tiled=True),
        lax.all_gather(pair_class, "txt", axis=0, tiled=True),
    )
    cols_half, col_class = (
        lax.all_gather(text_half, "img", axis=0, tiled=True),
        lax.all_gather(pair_class, "img", axis=0, tiled=True),
    )
    coef, loss_part = tile_terms(rows_half, row_class, cols_half, col_class, scale, shift)
    image_pull = jnp.dot(coef, cols_half, preferred_element_type=jnp.float32)
    text_pull = lax.psum_scatter(
        lax.dot_general(
            coef, rows_half, (((0,), (0,)), ((), ())), preferred_element_type=jnp.float32
        ),
        "img",
        scatter_dimension=0,
        tiled=True,
    )
    image_sum, loss_sum = (
        lax.psum_scatter(image_pull, "txt", scatter_dimension=0, tiled=True),
        lax.psum_scatter(loss_part, "txt", scatter_dimension=0, tiled=True),
    )
    row_loss = loss_sum / pairs
    grad_image = project_back(image_unit, image_inv, image_sum)
    grad_text = project_back(text_unit, text_inv, text_pull)
    return (row_loss, grad_image, grad_text)


def on_first_core():
    return lax.rem(lax.axis_index("img"), 2) == 0


def class_digits(class_ref):
    rows = class_ref.shape[0]
    across = jnp.broadcast_to(class_ref[...][None, :], (rows, rows))
    row = lax.broadcasted_iota(jnp.int32, (rows, rows), 0)
    column = lax.broadcasted_iota(jnp.int32, (rows, rows), 1)
    lane = lax.broadcasted_iota(jnp.int32, (rows, LANES), 1)
    digits = jnp.zeros((rows, LANES), jnp.float32)
    for k in range(DIGITS):
        byte = (lax.shift_right_logical(across, 8 * k) & 255).astype(jnp.float32)
        down = jnp.sum(jnp.where(row == column, byte, 0.0), axis=1, keepdims=True)
        digits = jnp.where(lane == k, down, digits)
    return digits.astype(jnp.bfloat16)


def digits_kernel(class_ref, digits_ref):
    digits_ref[...] = class_digits(class_ref)


def pack_kernel(image_ref, text_ref, digits_ref, out_ref):
    rows, depth = image_ref.shape
    for start, source in ((0, image_ref), (rows, text_ref)):
        out_ref[start : start + rows, :depth] = unit_rows(source[...])[0].astype(jnp.bfloat16)
        out_ref[start : start + rows, depth:] = digits_ref[...]


def join_kernel(own_ref, got_ref, *refs):
    first = on_first_core()
    rows = own_ref.shape[0] // 2
    own, got = own_ref[...].astype(jnp.float32), got_ref[...].astype(jnp.float32)
    low, high = jnp.where(first, own, got), jnp.where(first, got, own)
    images = jnp.concatenate([low[:rows], high[:rows]], axis=0)
    texts = jnp.concatenate([low[rows:], high[rows:]], axis=0)
    mine = jnp.where(first, images, texts).astype(jnp.bfloat16)
    other = jnp.where(first, texts, images).astype(jnp.bfloat16)
    for ref, block in zip(refs, (mine, other, mine, mine, mine, other)):
        ref[...] = block


def put_pair(upper_ref, lower_ref, out_ref):
    rows = upper_ref.shape[0]
    out_ref[:rows, :] = upper_ref[...]
    out_ref[rows:, :] = lower_ref[...]


def far_kernel(scale_ref, shift_ref, upper_ref, lower_ref, out_ref, pair_ref):
    put_pair(upper_ref, lower_ref, out_ref)
    row = lax.broadcasted_iota(jnp.int32, pair_ref.shape, 0)
    pair_ref[...] = jnp.where(row == 0, scale_ref[0], shift_ref[0])


def power_above(size):
    return jnp.ceil(jnp.log2(jnp.maximum(size, 1e-30)) + 0.01)


def nearest(values):
    return jnp.floor(values + 0.5).astype(jnp.int32)


def code(values, power):
    return nearest(values * (TOP / jnp.exp2(power))).astype(jnp.int16)


def decode(steps, power):
    return steps.astype(jnp.int32).astype(jnp.float32) * (jnp.exp2(power) * (1.0 / TOP))


def put_rows(outs, pull, loss):
    blocks, (rows, width) = len(outs), outs[0].shape
    depth = width - LANES
    power = power_above(jnp.max(jnp.abs(pull), axis=1, keepdims=True))
    steps = code(pull, power)
    lane = lax.broadcasted_iota(jnp.int32, (blocks * rows, LANES), 1)
    loss_power = power_above(loss)
    tail = jnp.where(lane == 0, power, 0.0)
    tail = jnp.where(lane == 1, loss_power, tail)
    tail = jnp.where(lane == 2, loss * (TOP / jnp.exp2(loss_power)), tail)
    tail = nearest(tail).astype(jnp.int16)
    for k, out in enumerate(outs):
        out[:, :depth] = steps[k * rows : (k + 1) * rows]
        out[:, depth:] = tail[k * rows : (k + 1) * rows]


def partial_pull(lines, columns, scale, shift):
    depth = lines.shape[1] - LANES
    logits = (
        scale
        * lax.dot_general(
            lines[:, :depth],
            columns[:, :depth],
            (((1,), (1,)), ((), ())),
            preferred_element_type=jnp.float32,
        )
        + shift
    )
    pick = (
        lax.broadcasted_iota(jnp.int32, (8, LANES), 0)
        == lax.broadcasted_iota(jnp.int32, (8, LANES), 1)
    )
    column_digits = lax.dot_general(
        pick.astype(jnp.bfloat16),
        columns[:, depth:],
        (((1,), (1,)), ((), ())),
        preferred_element_type=jnp.float32,
    )
    line_digits = lines[:, depth:].astype(jnp.float32)
    same = None
    for k in range(DIGITS):
        equal = line_digits[:, k : k + 1] == column_digits[k : k + 1, :]
        same = equal if same is None else same & equal
    sign = jnp.where(same, 1.0, -1.0).astype(jnp.float32)
    margin = sign * logits
    small = jnp.exp(-jnp.abs(margin))
    over = 1.0 / (1.0 + small)
    coef = -sign * jnp.where(margin >= 0, small * over, over) * scale
    pull = jnp.dot(
        coef.astype(jnp.bfloat16), columns[:, :depth], preferred_element_type=jnp.float32
    )
    loss = jnp.sum(jnp.log1p(small) - jnp.minimum(margin, 0.0), axis=1, keepdims=True)
    return pull, loss


def tile_kernel(pair_ref, mine_ref, other_ref, far_ref, swapped_ref, near_ref, *outs):
    rows = mine_ref.shape[0]
    scale, shift = pair_ref[0:1, 0:1], pair_ref[1:2, 0:1]
    got = [far_ref[:rows, :], far_ref[rows:, :], near_ref[:rows, :]]
    swapped = [swapped_ref[:rows, :], swapped_ref[rows:, :], near_ref[rows:, :]]
    mine_side = jnp.concatenate([mine_ref[...], got[0], swapped[1], got[2]], axis=0)
    other_side = jnp.concatenate([other_ref[...], swapped[0], got[1], swapped[2]], axis=0)
    lines = jnp.concatenate([got[0], mine_ref[...], got[2]], axis=0)
    pull, loss = partial_pull(lines, other_side, scale, shift)
    put_rows([outs[0], outs[4]], pull[: 2 * rows], loss[: 2 * rows])
    half = rows // 2
    first = on_first_core()
    last = []
    for part in (pull, loss):
        low, high = part[2 * rows : 2 * rows + half], part[2 * rows + half :]
        last.append((jnp.where(first, low, high), jnp.where(first, high, low)))
    for out, part, part_loss in zip(outs[2:4], *last):
        put_rows([out], part, part_loss)
    put_rows([outs[1]], *partial_pull(got[1], mine_side, scale, shift))


def total(parts, rows, depth):
    pull = jnp.zeros((rows, depth), jnp.float32)
    loss = jnp.zeros((rows, 1), jnp.float32)
    for part in parts:
        tail = part[:, depth:].astype(jnp.int32).astype(jnp.float32)
        pull = pull + decode(part[:, :depth], tail[:, 0:1])
        loss = loss + tail[:, 2:3] * (jnp.exp2(tail[:, 1:2]) * (1.0 / TOP))
    return pull, loss


def place_of(first, rows):
    own = pl.multiple_of(jnp.where(first, 0, rows), rows)
    return pl.ds(own, rows), pl.ds(pl.multiple_of(rows - own, rows), rows)


def add_kernel(own_ref, back_0, back_1, keep_ref, loss_ref, give_ref):
    rows, depth = keep_ref.shape[1:]
    own, other = place_of(on_first_core(), rows)
    for side, parts in enumerate(((own_ref, back_0), (back_1,))):
        keep_ref[side], loss = total([part[own, :] for part in parts], rows, depth)
        loss_ref[side] = jnp.broadcast_to(loss, loss_ref.shape[1:])
        pull, loss = total([part[other, :] for part in parts], rows, depth)
        put_rows([give_ref.at[side * rows : (side + 1) * rows, :]], pull, loss)


def more_kernel(keep_ref, kept_loss_ref, same_ref, cross_ref, image_ref, text_ref, sum_ref, sum_loss_ref, *units):
    rows, depth = keep_ref.shape[1:]
    for side, ref in enumerate((same_ref, cross_ref)):
        pull, loss = total([ref[...]], rows, depth)
        sum_ref[side] = keep_ref[side] + pull
        sum_loss_ref[side] = kept_loss_ref[side] + loss
    for side, ref in enumerate((image_ref, text_ref)):
        unit, inverse = unit_rows(ref[...])
        units[0][side] = unit
        units[1][side] = jnp.broadcast_to(inverse, units[1].shape[1:])


def final_kernel(pairs, keep_ref, kept_loss_ref, unit_ref, inverse_ref, got_ref, loss_ref, grad_image_ref, grad_text_ref):
    first = on_first_core()
    rows, depth = keep_ref.shape[1:]
    pulls, losses = [], []
    for side in (0, 1):
        pull, loss = total([got_ref[(1 - side) * rows : (2 - side) * rows, :]], rows, depth)
        pulls.append(keep_ref[side] + pull)
        losses.append(kept_loss_ref[side][:, 0:1] + loss)
    for side, (pull, out) in enumerate(
        (
            (jnp.where(first, pulls[0], pulls[1]), grad_image_ref),
            (jnp.where(first, pulls[1], pulls[0]), grad_text_ref),
        )
    ):
        out[...] = project_back(unit_ref[side], inverse_ref[side][:, 0:1], pull)
    row = lax.broadcasted_iota(jnp.int32, (rows, rows), 0)
    column = lax.broadcasted_iota(jnp.int32, (rows, rows), 1)
    loss = jnp.where(first, losses[0], losses[1])
    across = jnp.where(row == column, loss / pairs, 0.0)
    loss_ref[...] = jnp.sum(across, axis=0, keepdims=True)


def chip_plan(image_emb, text_emb, pair_class, scale, shift):
    rows, depth = image_emb.shape
    width = depth + LANES
    lanes = lax.axis_size("txt")
    n = lax.axis_size("img") * lanes
    vmem = pl.BlockSpec(memory_space=pltpu.VMEM)
    smem = pl.BlockSpec(memory_space=pltpu.SMEM)

    def call(kernel, shapes, operands, name, scalars=0, cost=None):
        return pl.pallas_call(
            kernel,
            cost_estimate=cost,
            out_shape=shapes,
            in_specs=[smem] * scalars + [vmem] * (len(operands) - scalars),
            out_specs=jax.tree.map(lambda _: vmem, shapes),
            compiler_params=pltpu.CompilerParams(vmem_limit_bytes=32 << 20),
            name=name,
        )(*operands)

    def block(count, dtype=jnp.bfloat16):
        return jax.ShapeDtypeStruct((count * rows, width), dtype)

    def wide(*shape):
        return jax.ShapeDtypeStruct(shape, jnp.float32)

    def core(i):
        return i // lanes % 2

    def visit(x, masks, cross=0):
        pairs = []
        for i in range(n):
            chip = (i // (2 * lanes) * lanes + i % lanes) ^ masks[core(i)]
            pairs.append((i, (chip // lanes * 2 + (core(i) ^ cross)) * lanes + chip % lanes))
        return lax.ppermute(x, AXES, pairs)

    def swap(x):
        return lax.ppermute(x, AXES, [(i, i ^ lanes) for i in range(n)])

    visits = ((12, 3), (2, 8), (4, 1), (4, 1))
    crosses = (0, 0, 0, 1)
    late = pl.CostEstimate(flops=10**9, bytes_accessed=10**7, transcendentals=0)
    digits = call(
        digits_kernel,
        jax.ShapeDtypeStruct((rows, LANES), jnp.bfloat16),
        [pair_class],
        "digits",
        cost=late,
    )
    own = call(pack_kernel, block(2), [image_emb, text_emb, digits], "pack")
    *sent, mine, other = call(join_kernel, (block(2),) * 6, [own, swap(own)], "join")
    got = [visit(*three) for three in zip(sent, visits, crosses)]
    far, pair = call(
        far_kernel,
        (block(4), wide(8, LANES)),
        [scale[None], shift[None], *got[:2]],
        "far",
        2,
    )
    near = call(put_pair, block(4), got[2:], "near", cost=late)
    one, two = block(1, jnp.int16), block(2, jnp.int16)
    parts = call(
        tile_kernel,
        (two, two, one, one, two),
        [pair, mine, other, far, swap(far), near],
        "tile",
    )
    back = [visit(*three) for three in zip(parts, visits, crosses)]
    keep, kept_loss, give = call(
        add_kernel,
        (wide(2, rows, depth), wide(2, rows, LANES), two),
        [parts[4], *back[:2]],
        "add",
    )
    sums = call(
        more_kernel,
        (wide(2, rows, depth), wide(2, rows, LANES)) * 2,
        [keep, kept_loss, *back[2:], image_emb, text_emb],
        "more",
        cost=late,
    )
    loss, grad_image, grad_text = call(
        functools.partial(final_kernel, n * rows),
        (wide(1, rows), wide(rows, depth), wide(rows, depth)),
        [*sums, swap(give)],
        "final",
    )
    return (loss[0], grad_image, grad_text)


def local(image_emb, text_emb, pair_class, scale, shift):
    if lax.axis_size("img") * lax.axis_size("txt") == 2 * 4 * 4 and lax.axis_size("txt") in (1, 2, 4):
        return chip_plan(image_emb, text_emb, pair_class, scale, shift)
    return tile_plan(image_emb, text_emb, pair_class, scale, shift)


def solution(mesh):
    in_specs = (P(AXES, None), P(AXES, None), P(AXES), P(), P())
    out_specs = (P(AXES), P(AXES, None), P(AXES, None))
    return jax.shard_map(local, mesh=mesh, in_specs=in_specs, out_specs=out_specs, check_vma=False)
```

```python
import functools

import jax
import jax.numpy as jnp
from jax import lax
from jax.experimental import pallas as pl
from jax.experimental.pallas import tpu as pltpu
from jax.sharding import PartitionSpec as P

AXES = ("img", "txt")
DIGITS = 4
LANES = 128
TOP = 32767.0


def unit_rows(rows):
    wide = rows.astype(jnp.float32)
    inverse = 1.0 / jnp.sqrt(jnp.sum(wide * wide, axis=1, keepdims=True) + 1e-06)
    return (wide * inverse, inverse)


def project_back(unit, inverse, pull):
    inner = jnp.sum(unit * pull, axis=1, keepdims=True)
    return (pull - unit * inner) * inverse


def tile_terms(rows_half, row_class, cols_half, col_class, scale, shift):
    logits = (
        scale
        * lax.dot_general(
            rows_half, cols_half, (((1,), (1,)), ((), ())), preferred_element_type=jnp.float32
        )
        + shift
    )
    sign = jnp.where(row_class[:, None] == col_class[None, :], 1.0, -1.0).astype(jnp.float32)
    margin = sign * logits
    loss_part = -jnp.sum(jax.nn.log_sigmoid(margin), axis=1)
    coef = (-sign * jax.nn.sigmoid(-margin) * scale).astype(jnp.bfloat16)
    return (coef, loss_part)


def tile_plan(image_emb, text_emb, pair_class, scale, shift):
    image_unit, image_inv = unit_rows(image_emb)
    text_unit, text_inv = unit_rows(text_emb)
    own_rows = text_emb.shape[0]
    pairs = own_rows * lax.axis_size("img") * lax.axis_size("txt")
    text_half = text_unit.astype(jnp.bfloat16)
    rows_half, row_class = (
        lax.all_gather(image_unit.astype(jnp.bfloat16), "txt", axis=0, tiled=True),
        lax.all_gather(pair_class, "txt", axis=0, tiled=True),
    )
    cols_half, col_class = (
        lax.all_gather(text_half, "img", axis=0, tiled=True),
        lax.all_gather(pair_class, "img", axis=0, tiled=True),
    )
    coef, loss_part = tile_terms(rows_half, row_class, cols_half, col_class, scale, shift)
    image_pull = jnp.dot(coef, cols_half, preferred_element_type=jnp.float32)
    text_pull = lax.psum_scatter(
        lax.dot_general(
            coef, rows_half, (((0,), (0,)), ((), ())), preferred_element_type=jnp.float32
        ),
        "img",
        scatter_dimension=0,
        tiled=True,
    )
    image_sum, loss_sum = (
        lax.psum_scatter(image_pull, "txt", scatter_dimension=0, tiled=True),
        lax.psum_scatter(loss_part, "txt", scatter_dimension=0, tiled=True),
    )
    row_loss = loss_sum / pairs
    grad_image = project_back(image_unit, image_inv, image_sum)
    grad_text = project_back(text_unit, text_inv, text_pull)
    return (row_loss, grad_image, grad_text)


def on_first_core():
    return lax.rem(lax.axis_index("img"), 2) == 0


def class_digits(class_ref):
    rows = class_ref.shape[0]
    across = jnp.broadcast_to(class_ref[...][None, :], (rows, rows))
    row = lax.broadcasted_iota(jnp.int32, (rows, rows), 0)
    column = lax.broadcasted_iota(jnp.int32, (rows, rows), 1)
    lane = lax.broadcasted_iota(jnp.int32, (rows, LANES), 1)
    digits = jnp.zeros((rows, LANES), jnp.float32)
    for k in range(DIGITS):
        byte = (lax.shift_right_logical(across, 8 * k) & 255).astype(jnp.float32)
        down = jnp.sum(jnp.where(row == column, byte, 0.0), axis=1, keepdims=True)
        digits = jnp.where(lane == k, down, digits)
    return digits.astype(jnp.bfloat16)


def digits_kernel(class_ref, digits_ref):
    digits_ref[...] = class_digits(class_ref)


def pack_kernel(image_ref, text_ref, digits_ref, out_ref):
    rows, depth = image_ref.shape
    for start, source in ((0, image_ref), (rows, text_ref)):
        out_ref[start : start + rows, :depth] = unit_rows(source[...])[0].astype(jnp.bfloat16)
        out_ref[start : start + rows, depth:] = digits_ref[...]


def join_kernel(own_ref, got_ref, *refs):
    first = on_first_core()
    rows = own_ref.shape[0] // 2
    own, got = own_ref[...].astype(jnp.float32), got_ref[...].astype(jnp.float32)
    low, high = jnp.where(first, own, got), jnp.where(first, got, own)
    images = jnp.concatenate([low[:rows], high[:rows]], axis=0)
    texts = jnp.concatenate([low[rows:], high[rows:]], axis=0)
    mine = jnp.where(first, images, texts).astype(jnp.bfloat16)
    other = jnp.where(first, texts, images).astype(jnp.bfloat16)
    for ref, block in zip(refs, (mine, other, mine, mine, mine, other)):
        ref[...] = block


def put_pair(upper_ref, lower_ref, out_ref):
    rows = upper_ref.shape[0]
    out_ref[:rows, :] = upper_ref[...]
    out_ref[rows:, :] = lower_ref[...]


def far_kernel(scale_ref, shift_ref, upper_ref, lower_ref, out_ref, pair_ref):
    put_pair(upper_ref, lower_ref, out_ref)
    row = lax.broadcasted_iota(jnp.int32, pair_ref.shape, 0)
    pair_ref[...] = jnp.where(row == 0, scale_ref[0], shift_ref[0])


def power_above(size):
    return jnp.ceil(jnp.log2(jnp.maximum(size, 1e-30)) + 0.01)


def nearest(values):
    return jnp.floor(values + 0.5).astype(jnp.int32)


def code(values, power):
    return nearest(values * (TOP / jnp.exp2(power))).astype(jnp.int16)


def decode(steps, power):
    return steps.astype(jnp.int32).astype(jnp.float32) * (jnp.exp2(power) * (1.0 / TOP))


def put_rows(outs, pull, loss):
    blocks, (rows, width) = len(outs), outs[0].shape
    depth = width - LANES
    power = power_above(jnp.max(jnp.abs(pull), axis=1, keepdims=True))
    steps = code(pull, power)
    lane = lax.broadcasted_iota(jnp.int32, (blocks * rows, LANES), 1)
    loss_power = power_above(loss)
    tail = jnp.where(lane == 0, power, 0.0)
    tail = jnp.where(lane == 1, loss_power, tail)
    tail = jnp.where(lane == 2, loss * (TOP / jnp.exp2(loss_power)), tail)
    tail = nearest(tail).astype(jnp.int16)
    for k, out in enumerate(outs):
        out[:, :depth] = steps[k * rows : (k + 1) * rows]
        out[:, depth:] = tail[k * rows : (k + 1) * rows]


def tile_terms_of(lines, columns, scale, shift):
    depth = lines.shape[1] - LANES
    logits = (
        scale
        * lax.dot_general(
            lines[:, :depth],
            columns[:, :depth],
            (((1,), (1,)), ((), ())),
            preferred_element_type=jnp.float32,
        )
        + shift
    )
    pick = (
        lax.broadcasted_iota(jnp.int32, (8, LANES), 0)
        == lax.broadcasted_iota(jnp.int32, (8, LANES), 1)
    )
    column_digits = lax.dot_general(
        pick.astype(jnp.bfloat16),
        columns[:, depth:],
        (((1,), (1,)), ((), ())),
        preferred_element_type=jnp.float32,
    )
    line_digits = lines[:, depth:].astype(jnp.float32)
    same = None
    for k in range(DIGITS):
        equal = line_digits[:, k : k + 1] == column_digits[k : k + 1, :]
        same = equal if same is None else same & equal
    sign = jnp.where(same, 1.0, -1.0).astype(jnp.float32)
    margin = sign * logits
    small = jnp.exp(-jnp.abs(margin))
    over = 1.0 / (1.0 + small)
    coef = -sign * jnp.where(margin >= 0, small * over, over) * scale
    return jnp.log1p(small) - jnp.minimum(margin, 0.0), coef


def pulls_of(loss, coef, columns):
    depth = columns.shape[1] - LANES
    pull = jnp.dot(
        coef.astype(jnp.bfloat16), columns[:, :depth], preferred_element_type=jnp.float32
    )
    return pull, jnp.sum(loss, axis=1, keepdims=True)


def tile_kernel(pair_ref, mine_ref, other_ref, far_ref, swapped_ref, near_ref, *outs):
    rows = mine_ref.shape[0]
    scale, shift = pair_ref[0:1, 0:1], pair_ref[1:2, 0:1]
    lines = jnp.concatenate(
        [far_ref[:rows, :], near_ref[:rows, :], mine_ref[...], swapped_ref[rows:, :]], axis=0
    )
    columns = jnp.concatenate(
        [far_ref[rows:, :], swapped_ref[:rows, :], near_ref[rows:, :], other_ref[...]], axis=0
    )
    loss, coef = tile_terms_of(lines, columns, scale, shift)
    put_rows([outs[0], outs[1], outs[4]], *pulls_of(loss[: 3 * rows], coef[: 3 * rows], columns))
    first = on_first_core()
    half = rows // 2
    halves = []
    for part in pulls_of(loss.T[:rows], coef.T[:rows], lines):
        low, high = part[:half], part[half:]
        halves.append((jnp.where(first, low, high), jnp.where(first, high, low)))
    for out, pull, part_loss in zip(outs[2:4], *halves):
        put_rows([out], pull, part_loss)


def total(parts, rows, depth):
    pull = jnp.zeros((rows, depth), jnp.float32)
    loss = jnp.zeros((rows, 1), jnp.float32)
    for part in parts:
        tail = part[:, depth:].astype(jnp.int32).astype(jnp.float32)
        pull = pull + decode(part[:, :depth], tail[:, 0:1])
        loss = loss + tail[:, 2:3] * (jnp.exp2(tail[:, 1:2]) * (1.0 / TOP))
    return pull, loss


def place_of(first, rows):
    own = pl.multiple_of(jnp.where(first, 0, rows), rows)
    return pl.ds(own, rows), pl.ds(pl.multiple_of(rows - own, rows), rows)


def add_kernel(own_ref, back_0, back_1, keep_ref, loss_ref, give_ref):
    rows, depth = keep_ref.shape
    own, other = place_of(on_first_core(), rows)
    parts = (own_ref, back_0, back_1)
    pull, loss = total([part[other, :] for part in parts], rows, depth)
    put_rows([give_ref], pull, loss)
    keep_ref[...], loss = total([part[own, :] for part in parts], rows, depth)
    loss_ref[...] = jnp.broadcast_to(loss, loss_ref.shape)


def more_kernel(keep_ref, kept_loss_ref, same_ref, cross_ref, image_ref, text_ref, sum_ref, sum_loss_ref, *units):
    rows, depth = keep_ref.shape
    pull, loss = total([cross_ref], rows, depth)
    sum_ref[0] = keep_ref[...] + pull
    sum_loss_ref[0] = kept_loss_ref[...] + loss
    sum_ref[1], loss = total([same_ref], rows, depth)
    sum_loss_ref[1] = jnp.broadcast_to(loss, sum_loss_ref.shape[1:])
    for side, ref in enumerate((image_ref, text_ref)):
        unit, inverse = unit_rows(ref[...])
        units[0][side] = unit
        units[1][side] = jnp.broadcast_to(inverse, units[1].shape[1:])


def final_kernel(pairs, sum_ref, sum_loss_ref, unit_ref, inverse_ref, got_ref, loss_ref, grad_image_ref, grad_text_ref):
    first = on_first_core()
    rows, depth = sum_ref.shape[1:]
    pull, loss = total([got_ref], rows, depth)
    pulls = (sum_ref[0], sum_ref[1] + pull)
    losses = (sum_loss_ref[0][:, 0:1], sum_loss_ref[1][:, 0:1] + loss)
    for side, (pull, out) in enumerate(
        (
            (jnp.where(first, pulls[0], pulls[1]), grad_image_ref),
            (jnp.where(first, pulls[1], pulls[0]), grad_text_ref),
        )
    ):
        out[...] = project_back(unit_ref[side], inverse_ref[side][:, 0:1], pull)
    row = lax.broadcasted_iota(jnp.int32, (rows, rows), 0)
    column = lax.broadcasted_iota(jnp.int32, (rows, rows), 1)
    loss = jnp.where(first, losses[0], losses[1])
    across = jnp.where(row == column, loss / pairs, 0.0)
    loss_ref[...] = jnp.sum(across, axis=0, keepdims=True)


def chip_plan(image_emb, text_emb, pair_class, scale, shift):
    rows, depth = image_emb.shape
    width = depth + LANES
    lanes = lax.axis_size("txt")
    n = lax.axis_size("img") * lanes
    vmem = pl.BlockSpec(memory_space=pltpu.VMEM)
    smem = pl.BlockSpec(memory_space=pltpu.SMEM)

    def call(kernel, shapes, operands, name, scalars=0, cost=None):
        return pl.pallas_call(
            kernel,
            cost_estimate=cost,
            out_shape=shapes,
            in_specs=[smem] * scalars + [vmem] * (len(operands) - scalars),
            out_specs=jax.tree.map(lambda _: vmem, shapes),
            compiler_params=pltpu.CompilerParams(vmem_limit_bytes=32 << 20),
            name=name,
        )(*operands)

    def block(count, dtype=jnp.bfloat16):
        return jax.ShapeDtypeStruct((count * rows, width), dtype)

    def wide(*shape):
        return jax.ShapeDtypeStruct(shape, jnp.float32)

    def core(i):
        return i // lanes % 2

    def visit(x, masks, cross):
        pairs = []
        for i in range(n):
            chip = (i // (2 * lanes) * lanes + i % lanes) ^ masks[core(i)]
            pairs.append((i, (chip // lanes * 2 + (core(i) ^ cross)) * lanes + chip % lanes))
        return lax.ppermute(x, AXES, pairs)

    def swap(x):
        return lax.ppermute(x, AXES, [(i, i ^ lanes) for i in range(n)])

    out_visits = (((12, 3), 0), ((2, 8), 0), ((4, 1), 0), ((4, 1), 1))
    back_visits = (((12, 3), 0), ((4, 1), 0), ((2, 8), 0), ((2, 8), 1))
    late = pl.CostEstimate(flops=10**9, bytes_accessed=10**7, transcendentals=0)
    digits = call(
        digits_kernel,
        jax.ShapeDtypeStruct((rows, LANES), jnp.bfloat16),
        [pair_class],
        "digits",
        cost=late,
    )
    own = call(pack_kernel, block(2), [image_emb, text_emb, digits], "pack")
    *sent, mine, other = call(join_kernel, (block(2),) * 6, [own, swap(own)], "join")
    got = [visit(x, *way) for x, way in zip(sent, out_visits)]
    far, pair = call(
        far_kernel,
        (block(4), wide(8, LANES)),
        [scale[None], shift[None], *got[:2]],
        "far",
        2,
    )
    near = call(put_pair, block(4), got[2:], "near", cost=late)
    one, two = block(1, jnp.int16), block(2, jnp.int16)
    parts = call(
        tile_kernel,
        (two, two, one, one, two),
        [pair, mine, other, far, swap(far), near],
        "tile",
    )
    back = [visit(x, *way) for x, way in zip(parts, back_visits)]
    keep, kept_loss, give = call(
        add_kernel,
        (wide(rows, depth), wide(rows, LANES), one),
        [parts[4], *back[:2]],
        "add",
    )
    sums = call(
        more_kernel,
        (wide(2, rows, depth), wide(2, rows, LANES)) * 2,
        [keep, kept_loss, *back[2:], image_emb, text_emb],
        "more",
        cost=late,
    )
    loss, grad_image, grad_text = call(
        functools.partial(final_kernel, n * rows),
        (wide(1, rows), wide(rows, depth), wide(rows, depth)),
        [*sums, swap(give)],
        "final",
    )
    return (loss[0], grad_image, grad_text)


def local(image_emb, text_emb, pair_class, scale, shift):
    if lax.axis_size("img") * lax.axis_size("txt") == 2 * 4 * 4 and lax.axis_size("txt") in (1, 2, 4):
        return chip_plan(image_emb, text_emb, pair_class, scale, shift)
    return tile_plan(image_emb, text_emb, pair_class, scale, shift)


def solution(mesh):
    in_specs = (P(AXES, None), P(AXES, None), P(AXES), P(), P())
    out_specs = (P(AXES), P(AXES, None), P(AXES, None))
    return jax.shard_map(local, mesh=mesh, in_specs=in_specs, out_specs=out_specs, check_vma=False)
```

```python
import functools

import jax
import jax.numpy as jnp
from jax import lax
from jax.experimental import pallas as pl
from jax.experimental.pallas import tpu as pltpu
from jax.sharding import PartitionSpec as P

AXES = ("img", "txt")
DIGITS = 4
LANES = 128
TOP = 32767.0


def unit_rows(rows):
    wide = rows.astype(jnp.float32)
    inverse = 1.0 / jnp.sqrt(jnp.sum(wide * wide, axis=1, keepdims=True) + 1e-06)
    return (wide * inverse, inverse)


def project_back(unit, inverse, pull):
    inner = jnp.sum(unit * pull, axis=1, keepdims=True)
    return (pull - unit * inner) * inverse


def tile_terms(rows_half, row_class, cols_half, col_class, scale, shift):
    logits = (
        scale
        * lax.dot_general(
            rows_half, cols_half, (((1,), (1,)), ((), ())), preferred_element_type=jnp.float32
        )
        + shift
    )
    sign = jnp.where(row_class[:, None] == col_class[None, :], 1.0, -1.0).astype(jnp.float32)
    margin = sign * logits
    loss_part = -jnp.sum(jax.nn.log_sigmoid(margin), axis=1)
    coef = (-sign * jax.nn.sigmoid(-margin) * scale).astype(jnp.bfloat16)
    return (coef, loss_part)


def tile_plan(image_emb, text_emb, pair_class, scale, shift):
    image_unit, image_inv = unit_rows(image_emb)
    text_unit, text_inv = unit_rows(text_emb)
    own_rows = text_emb.shape[0]
    pairs = own_rows * lax.axis_size("img") * lax.axis_size("txt")
    text_half = text_unit.astype(jnp.bfloat16)
    rows_half, row_class = (
        lax.all_gather(image_unit.astype(jnp.bfloat16), "txt", axis=0, tiled=True),
        lax.all_gather(pair_class, "txt", axis=0, tiled=True),
    )
    cols_half, col_class = (
        lax.all_gather(text_half, "img", axis=0, tiled=True),
        lax.all_gather(pair_class, "img", axis=0, tiled=True),
    )
    coef, loss_part = tile_terms(rows_half, row_class, cols_half, col_class, scale, shift)
    image_pull = jnp.dot(coef, cols_half, preferred_element_type=jnp.float32)
    text_pull = lax.psum_scatter(
        lax.dot_general(
            coef, rows_half, (((0,), (0,)), ((), ())), preferred_element_type=jnp.float32
        ),
        "img",
        scatter_dimension=0,
        tiled=True,
    )
    image_sum, loss_sum = (
        lax.psum_scatter(image_pull, "txt", scatter_dimension=0, tiled=True),
        lax.psum_scatter(loss_part, "txt", scatter_dimension=0, tiled=True),
    )
    row_loss = loss_sum / pairs
    grad_image = project_back(image_unit, image_inv, image_sum)
    grad_text = project_back(text_unit, text_inv, text_pull)
    return (row_loss, grad_image, grad_text)


def on_first_core():
    return lax.rem(lax.axis_index("img"), 2) == 0


def class_digits(class_ref):
    rows = class_ref.shape[0]
    across = jnp.broadcast_to(class_ref[...][None, :], (rows, rows))
    row = lax.broadcasted_iota(jnp.int32, (rows, rows), 0)
    column = lax.broadcasted_iota(jnp.int32, (rows, rows), 1)
    lane = lax.broadcasted_iota(jnp.int32, (rows, LANES), 1)
    digits = jnp.zeros((rows, LANES), jnp.float32)
    for k in range(DIGITS):
        byte = (lax.shift_right_logical(across, 8 * k) & 255).astype(jnp.float32)
        down = jnp.sum(jnp.where(row == column, byte, 0.0), axis=1, keepdims=True)
        digits = jnp.where(lane == k, down, digits)
    return digits.astype(jnp.bfloat16)


def digits_kernel(class_ref, digits_ref):
    digits_ref[...] = class_digits(class_ref)


def pack_kernel(image_ref, text_ref, digits_ref, both_ref, image_out, text_out):
    rows, depth = image_ref.shape
    for start, source, out in ((0, image_ref, image_out), (rows, text_ref, text_out)):
        half = unit_rows(source[...])[0].astype(jnp.bfloat16)
        for ref in (both_ref.at[start : start + rows, :], out):
            ref[:, :depth] = half
            ref[:, depth:] = digits_ref[...]


def join_kernel(own_ref, got_ref, *refs):
    first = on_first_core()
    rows = own_ref.shape[0] // 2
    own, got = own_ref[...].astype(jnp.float32), got_ref[...].astype(jnp.float32)
    low, high = jnp.where(first, own, got), jnp.where(first, got, own)
    images = jnp.concatenate([low[:rows], high[:rows]], axis=0)
    texts = jnp.concatenate([low[rows:], high[rows:]], axis=0)
    mine = jnp.where(first, images, texts).astype(jnp.bfloat16)
    other = jnp.where(first, texts, images).astype(jnp.bfloat16)
    for ref, block in zip(refs, (mine, mine, mine, mine, other)):
        ref[...] = block


def stack(refs, out_ref):
    start = 0
    for ref in refs:
        out_ref[start : start + ref.shape[0], :] = ref[...]
        start += ref.shape[0]


def near_kernel(scale_ref, shift_ref, *refs):
    stack(refs[:-2], refs[-2])
    row = lax.broadcasted_iota(jnp.int32, refs[-1].shape, 0)
    refs[-1][...] = jnp.where(row == 0, scale_ref[0], shift_ref[0])


def stack_kernel(*refs):
    stack(refs[:-1], refs[-1])


def power_above(size):
    return jnp.ceil(jnp.log2(jnp.maximum(size, 1e-30)) + 0.01)


def nearest(values):
    return jnp.floor(values + 0.5).astype(jnp.int32)


def code(values, power):
    return nearest(values * (TOP / jnp.exp2(power))).astype(jnp.int16)


def decode(steps, power):
    return steps.astype(jnp.int32).astype(jnp.float32) * (jnp.exp2(power) * (1.0 / TOP))


def put_rows(outs, pull, loss):
    blocks, (rows, width) = len(outs), outs[0].shape
    depth = width - LANES
    power = power_above(jnp.max(jnp.abs(pull), axis=1, keepdims=True))
    steps = code(pull, power)
    lane = lax.broadcasted_iota(jnp.int32, (blocks * rows, LANES), 1)
    loss_power = power_above(loss)
    tail = jnp.where(lane == 0, power, 0.0)
    tail = jnp.where(lane == 1, loss_power, tail)
    tail = jnp.where(lane == 2, loss * (TOP / jnp.exp2(loss_power)), tail)
    tail = nearest(tail).astype(jnp.int16)
    for k, out in enumerate(outs):
        out[:, :depth] = steps[k * rows : (k + 1) * rows]
        out[:, depth:] = tail[k * rows : (k + 1) * rows]


def tile_terms_of(lines, columns, scale, shift):
    depth = lines.shape[1] - LANES
    logits = (
        scale
        * lax.dot_general(
            lines[:, :depth],
            columns[:, :depth],
            (((1,), (1,)), ((), ())),
            preferred_element_type=jnp.float32,
        )
        + shift
    )
    pick = (
        lax.broadcasted_iota(jnp.int32, (8, LANES), 0)
        == lax.broadcasted_iota(jnp.int32, (8, LANES), 1)
    )
    column_digits = lax.dot_general(
        pick.astype(jnp.bfloat16),
        columns[:, depth:],
        (((1,), (1,)), ((), ())),
        preferred_element_type=jnp.float32,
    )
    line_digits = lines[:, depth:].astype(jnp.float32)
    same = None
    for k in range(DIGITS):
        equal = line_digits[:, k : k + 1] == column_digits[k : k + 1, :]
        same = equal if same is None else same & equal
    sign = jnp.where(same, 1.0, -1.0).astype(jnp.float32)
    margin = sign * logits
    small = jnp.exp(-jnp.abs(margin))
    over = 1.0 / (1.0 + small)
    coef = -sign * jnp.where(margin >= 0, small * over, over) * scale
    return jnp.log1p(small) - jnp.minimum(margin, 0.0), coef


def pulls_of(loss, coef, columns):
    depth = columns.shape[1] - LANES
    pull = jnp.dot(
        coef.astype(jnp.bfloat16), columns[:, :depth], preferred_element_type=jnp.float32
    )
    return pull, jnp.sum(loss, axis=1, keepdims=True)


def tile_kernel(pair_ref, mine_ref, other_ref, far_ref, swapped_ref, near_ref, *outs):
    rows = mine_ref.shape[0]
    half = rows // 2
    first = on_first_core()
    scale, shift = pair_ref[0:1, 0:1], pair_ref[1:2, 0:1]

    def pick(one, two):
        return jnp.where(first, one.astype(jnp.float32), two.astype(jnp.float32))

    def parted(ref):
        image, text = ref[:half, :], ref[half:rows, :]
        return pick(image, text).astype(jnp.bfloat16), pick(text, image).astype(jnp.bfloat16)

    (line_half, column_half), (line_rest, column_rest) = parted(far_ref), parted(swapped_ref)
    lines = jnp.concatenate(
        [far_ref[rows:, :], near_ref[:rows, :], line_half, mine_ref[...], line_rest], axis=0
    )
    columns = jnp.concatenate(
        [column_half, column_rest, swapped_ref[rows:, :], near_ref[rows:, :], other_ref[...]], axis=0
    )
    loss, coef = tile_terms_of(lines, columns, scale, shift)
    used = 3 * rows + half
    pull, loss_sum = pulls_of(loss[:used], coef[:used], columns)
    column_pull, column_loss = pulls_of(loss.T[:half], coef.T[:half], lines)
    put_rows([outs[0]], pull[:rows], loss_sum[:rows])
    line_pull, line_loss = pull[2 * rows : 2 * rows + half], loss_sum[2 * rows : 2 * rows + half]
    put_rows([outs[1]], pick(line_pull, column_pull), pick(line_loss, column_loss))
    put_rows([outs[2]], pick(column_pull, line_pull), pick(column_loss, line_loss))
    low, high = pull[rows : rows + half], pull[rows + half : 2 * rows]
    low_loss, high_loss = loss_sum[rows : rows + half], loss_sum[rows + half : 2 * rows]
    put_rows([outs[3]], pick(low, high), pick(low_loss, high_loss))
    put_rows([outs[4]], pick(high, low), pick(high_loss, low_loss))
    put_rows([outs[5]], pull[2 * rows + half : used], loss_sum[2 * rows + half : used])


def total(parts, rows, depth):
    pull = jnp.zeros((rows, depth), jnp.float32)
    loss = jnp.zeros((rows, 1), jnp.float32)
    for part in parts:
        tail = part[:, depth:].astype(jnp.int32).astype(jnp.float32)
        pull = pull + decode(part[:, :depth], tail[:, 0:1])
        loss = loss + tail[:, 2:3] * (jnp.exp2(tail[:, 1:2]) * (1.0 / TOP))
    return pull, loss


def place_of(first, rows):
    own = pl.multiple_of(jnp.where(first, 0, rows), rows)
    return pl.ds(own, rows), pl.ds(pl.multiple_of(rows - own, rows), rows)


def add_kernel(own_ref, back_ref, keep_ref, loss_ref, give_ref):
    rows, depth = keep_ref.shape
    own, other = place_of(on_first_core(), rows)
    pull, loss = total([own_ref[other, :], back_ref[other, :]], rows, depth)
    put_rows([give_ref], pull, loss)
    keep_ref[...], loss = total([own_ref[own, :], back_ref[own, :]], rows, depth)
    loss_ref[...] = jnp.broadcast_to(loss, loss_ref.shape)


def more_kernel(keep_ref, kept_loss_ref, image_back, text_back, same_ref, cross_ref, image_ref, text_ref, *outs):
    sum_ref, sum_loss_ref, unit_ref, inverse_ref = outs
    first = on_first_core()
    rows, depth = keep_ref.shape
    pull, loss = total([same_ref], rows, depth)
    mine = (keep_ref[...] + pull, kept_loss_ref[:, 0:1] + loss)
    other = total([cross_ref], rows, depth)
    for side, (back, source) in enumerate(((image_back, image_ref), (text_back, text_ref))):
        pull, loss = total([back], rows, depth)
        here, there = (mine, other) if side == 0 else (other, mine)
        sum_ref[side] = pull + jnp.where(first, here[0], there[0])
        loss = loss + jnp.where(first, here[1], there[1])
        sum_loss_ref[side] = jnp.broadcast_to(loss, sum_loss_ref.shape[1:])
        unit, inverse = unit_rows(source[...])
        unit_ref[side] = unit
        inverse_ref[side] = jnp.broadcast_to(inverse, inverse_ref.shape[1:])


def final_kernel(pairs, sum_ref, sum_loss_ref, unit_ref, inverse_ref, got_ref, loss_ref, grad_image_ref, grad_text_ref):
    first = on_first_core()
    rows, depth = sum_ref.shape[1:]
    pull, loss = total([got_ref], rows, depth)
    image_pull = sum_ref[0] + jnp.where(first, 0.0, pull)
    text_pull = sum_ref[1] + jnp.where(first, pull, 0.0)
    grad_image_ref[...] = project_back(unit_ref[0], inverse_ref[0][:, 0:1], image_pull)
    grad_text_ref[...] = project_back(unit_ref[1], inverse_ref[1][:, 0:1], text_pull)
    row = lax.broadcasted_iota(jnp.int32, (rows, rows), 0)
    column = lax.broadcasted_iota(jnp.int32, (rows, rows), 1)
    loss = sum_loss_ref[0][:, 0:1] + jnp.where(first, 0.0, loss)
    across = jnp.where(row == column, loss / pairs, 0.0)
    loss_ref[...] = jnp.sum(across, axis=0, keepdims=True)


def chip_plan(image_emb, text_emb, pair_class, scale, shift):
    rows, depth = image_emb.shape
    width = depth + LANES
    lanes = lax.axis_size("txt")
    n = lax.axis_size("img") * lanes
    vmem = pl.BlockSpec(memory_space=pltpu.VMEM)
    smem = pl.BlockSpec(memory_space=pltpu.SMEM)

    def call(kernel, shapes, operands, name, scalars=0, cost=None):
        return pl.pallas_call(
            kernel,
            cost_estimate=cost,
            out_shape=shapes,
            in_specs=[smem] * scalars + [vmem] * (len(operands) - scalars),
            out_specs=jax.tree.map(lambda _: vmem, shapes),
            compiler_params=pltpu.CompilerParams(vmem_limit_bytes=32 << 20),
            name=name,
        )(*operands)

    def block(count, dtype=jnp.bfloat16):
        return jax.ShapeDtypeStruct((count * rows, width), dtype)

    def wide(*shape):
        return jax.ShapeDtypeStruct(shape, jnp.float32)

    def core(i):
        return i // lanes % 2

    def visit(x, masks, cross):
        pairs = []
        for i in range(n):
            chip = (i // (2 * lanes) * lanes + i % lanes) ^ masks[core(i)]
            pairs.append((i, (chip // lanes * 2 + (core(i) ^ cross)) * lanes + chip % lanes))
        return lax.ppermute(x, AXES, pairs)

    def swap(x):
        return lax.ppermute(x, AXES, [(i, i ^ lanes) for i in range(n)])

    across, beside = ((12, 12), 0), ((3, 3), 0)
    second, near_same, near_cross = ((8, 2), 0), ((4, 1), 0), ((4, 1), 1)
    late = pl.CostEstimate(flops=10**9, bytes_accessed=10**7, transcendentals=0)
    digits = call(
        digits_kernel,
        jax.ShapeDtypeStruct((rows, LANES), jnp.bfloat16),
        [pair_class],
        "digits",
        cost=late,
    )
    own, own_images, own_texts = call(
        pack_kernel, (block(2), block(1), block(1)), [image_emb, text_emb, digits], "pack"
    )
    halves = [visit(own_images, *across), visit(own_texts, *beside)]
    *sent, mine, other = call(join_kernel, (block(2),) * 5, [own, swap(own)], "join")
    got = [visit(x, *way) for x, way in zip(sent, (second, near_same, near_cross))]
    halves = call(stack_kernel, block(2), halves, "halves", cost=late)
    far = call(stack_kernel, block(4), [halves, got[0]], "far", cost=late)
    near, pair = call(
        near_kernel,
        (block(4), wide(8, LANES)),
        [scale[None], shift[None], *got[1:]],
        "near",
        2,
        late,
    )
    one, two = block(1, jnp.int16), block(2, jnp.int16)
    parts = call(
        tile_kernel,
        (two, one, one, one, one, two),
        [pair, mine, other, far, swap(far), near],
        "tile",
    )
    ways = (second, across, beside, near_same, near_cross)
    back = [visit(x, *way) for x, way in zip(parts, ways)]
    keep, kept_loss, give = call(
        add_kernel, (wide(rows, depth), wide(rows, LANES), one), [parts[5], back[0]], "add"
    )
    sums = call(
        more_kernel,
        (wide(2, rows, depth), wide(2, rows, LANES)) * 2,
        [keep, kept_loss, *back[1:], image_emb, text_emb],
        "more",
        cost=late,
    )
    loss, grad_image, grad_text = call(
        functools.partial(final_kernel, n * rows),
        (wide(1, rows), wide(rows, depth), wide(rows, depth)),
        [*sums, swap(give)],
        "final",
    )
    return (loss[0], grad_image, grad_text)


def local(image_emb, text_emb, pair_class, scale, shift):
    if lax.axis_size("img") * lax.axis_size("txt") == 2 * 4 * 4 and lax.axis_size("txt") in (1, 2, 4):
        return chip_plan(image_emb, text_emb, pair_class, scale, shift)
    return tile_plan(image_emb, text_emb, pair_class, scale, shift)


def solution(mesh):
    in_specs = (P(AXES, None), P(AXES, None), P(AXES), P(), P())
    out_specs = (P(AXES), P(AXES, None), P(AXES, None))
    return jax.shard_map(local, mesh=mesh, in_specs=in_specs, out_specs=out_specs, check_vma=False)
```

```python
import functools

import jax
import jax.numpy as jnp
from jax import lax
from jax.experimental import pallas as pl
from jax.experimental.pallas import tpu as pltpu
from jax.sharding import PartitionSpec as P

AXES = ("img", "txt")
DIGITS = 4
LANES = 128
TOP = 32767.0


def unit_rows(rows):
    wide = rows.astype(jnp.float32)
    inverse = 1.0 / jnp.sqrt(jnp.sum(wide * wide, axis=1, keepdims=True) + 1e-06)
    return (wide * inverse, inverse)


def project_back(unit, inverse, pull):
    inner = jnp.sum(unit * pull, axis=1, keepdims=True)
    return (pull - unit * inner) * inverse


def tile_terms(rows_half, row_class, cols_half, col_class, scale, shift):
    logits = (
        scale
        * lax.dot_general(
            rows_half, cols_half, (((1,), (1,)), ((), ())), preferred_element_type=jnp.float32
        )
        + shift
    )
    sign = jnp.where(row_class[:, None] == col_class[None, :], 1.0, -1.0).astype(jnp.float32)
    margin = sign * logits
    loss_part = -jnp.sum(jax.nn.log_sigmoid(margin), axis=1)
    coef = (-sign * jax.nn.sigmoid(-margin) * scale).astype(jnp.bfloat16)
    return (coef, loss_part)


def tile_plan(image_emb, text_emb, pair_class, scale, shift):
    image_unit, image_inv = unit_rows(image_emb)
    text_unit, text_inv = unit_rows(text_emb)
    own_rows = text_emb.shape[0]
    pairs = own_rows * lax.axis_size("img") * lax.axis_size("txt")
    text_half = text_unit.astype(jnp.bfloat16)
    rows_half, row_class = (
        lax.all_gather(image_unit.astype(jnp.bfloat16), "txt", axis=0, tiled=True),
        lax.all_gather(pair_class, "txt", axis=0, tiled=True),
    )
    cols_half, col_class = (
        lax.all_gather(text_half, "img", axis=0, tiled=True),
        lax.all_gather(pair_class, "img", axis=0, tiled=True),
    )
    coef, loss_part = tile_terms(rows_half, row_class, cols_half, col_class, scale, shift)
    image_pull = jnp.dot(coef, cols_half, preferred_element_type=jnp.float32)
    text_pull = lax.psum_scatter(
        lax.dot_general(
            coef, rows_half, (((0,), (0,)), ((), ())), preferred_element_type=jnp.float32
        ),
        "img",
        scatter_dimension=0,
        tiled=True,
    )
    image_sum, loss_sum = (
        lax.psum_scatter(image_pull, "txt", scatter_dimension=0, tiled=True),
        lax.psum_scatter(loss_part, "txt", scatter_dimension=0, tiled=True),
    )
    row_loss = loss_sum / pairs
    grad_image = project_back(image_unit, image_inv, image_sum)
    grad_text = project_back(text_unit, text_inv, text_pull)
    return (row_loss, grad_image, grad_text)


def on_first_core():
    return lax.rem(lax.axis_index("img"), 2) == 0


def class_digits(class_ref):
    rows = class_ref.shape[0]
    across = jnp.broadcast_to(class_ref[...][None, :], (rows, rows))
    row = lax.broadcasted_iota(jnp.int32, (rows, rows), 0)
    column = lax.broadcasted_iota(jnp.int32, (rows, rows), 1)
    lane = lax.broadcasted_iota(jnp.int32, (rows, LANES), 1)
    digits = jnp.zeros((rows, LANES), jnp.float32)
    for k in range(DIGITS):
        byte = (lax.shift_right_logical(across, 8 * k) & 255).astype(jnp.float32)
        down = jnp.sum(jnp.where(row == column, byte, 0.0), axis=1, keepdims=True)
        digits = jnp.where(lane == k, down, digits)
    return digits.astype(jnp.bfloat16)


def digits_kernel(class_ref, digits_ref):
    digits_ref[...] = class_digits(class_ref)


def pack_kernel(image_ref, text_ref, digits_ref, out_ref):
    rows, depth = image_ref.shape
    for start, source in ((0, image_ref), (rows, text_ref)):
        out_ref[start : start + rows, :depth] = unit_rows(source[...])[0].astype(jnp.bfloat16)
        out_ref[start : start + rows, depth:] = digits_ref[...]


def join_kernel(own_ref, got_ref, *refs):
    first = on_first_core()
    rows = own_ref.shape[0] // 2
    own, got = own_ref[...].astype(jnp.float32), got_ref[...].astype(jnp.float32)
    low, high = jnp.where(first, own, got), jnp.where(first, got, own)
    images = jnp.concatenate([low[:rows], high[:rows]], axis=0)
    texts = jnp.concatenate([low[rows:], high[rows:]], axis=0)
    mine = jnp.where(first, images, texts).astype(jnp.bfloat16)
    other = jnp.where(first, texts, images).astype(jnp.bfloat16)
    for ref, block in zip(refs, (mine, other, mine, mine, mine, other)):
        ref[...] = block


def near_kernel(scale_ref, shift_ref, upper_ref, lower_ref, out_ref, pair_ref):
    rows = upper_ref.shape[0]
    out_ref[:rows, :] = upper_ref[...]
    out_ref[rows:, :] = lower_ref[...]
    row = lax.broadcasted_iota(jnp.int32, pair_ref.shape, 0)
    pair_ref[...] = jnp.where(row == 0, scale_ref[0], shift_ref[0])


def power_above(size):
    return jnp.ceil(jnp.log2(jnp.maximum(size, 1e-30)) + 0.01)


def nearest(values):
    return jnp.floor(values + 0.5).astype(jnp.int32)


def code(values, power):
    return nearest(values * (TOP / jnp.exp2(power))).astype(jnp.int16)


def decode(steps, power):
    return steps.astype(jnp.int32).astype(jnp.float32) * (jnp.exp2(power) * (1.0 / TOP))


def put_rows(outs, pull, loss):
    blocks, (rows, width) = len(outs), outs[0].shape
    depth = width - LANES
    power = power_above(jnp.max(jnp.abs(pull), axis=1, keepdims=True))
    steps = code(pull, power)
    lane = lax.broadcasted_iota(jnp.int32, (blocks * rows, LANES), 1)
    loss_power = power_above(loss)
    tail = jnp.where(lane == 0, power, 0.0)
    tail = jnp.where(lane == 1, loss_power, tail)
    tail = jnp.where(lane == 2, loss * (TOP / jnp.exp2(loss_power)), tail)
    tail = nearest(tail).astype(jnp.int16)
    for k, out in enumerate(outs):
        out[:, :depth] = steps[k * rows : (k + 1) * rows]
        out[:, depth:] = tail[k * rows : (k + 1) * rows]


def tile_terms_of(lines, columns, scale, shift):
    depth = lines.shape[1] - LANES
    logits = (
        scale
        * lax.dot_general(
            lines[:, :depth],
            columns[:, :depth],
            (((1,), (1,)), ((), ())),
            preferred_element_type=jnp.float32,
        )
        + shift
    )
    pick = (
        lax.broadcasted_iota(jnp.int32, (8, LANES), 0)
        == lax.broadcasted_iota(jnp.int32, (8, LANES), 1)
    )
    column_digits = lax.dot_general(
        pick.astype(jnp.bfloat16),
        columns[:, depth:],
        (((1,), (1,)), ((), ())),
        preferred_element_type=jnp.float32,
    )
    line_digits = lines[:, depth:].astype(jnp.float32)
    same = None
    for k in range(DIGITS):
        equal = line_digits[:, k : k + 1] == column_digits[k : k + 1, :]
        same = equal if same is None else same & equal
    sign = jnp.where(same, 1.0, -1.0).astype(jnp.float32)
    margin = sign * logits
    small = jnp.exp(-jnp.abs(margin))
    over = 1.0 / (1.0 + small)
    coef = -sign * jnp.where(margin >= 0, small * over, over) * scale
    return jnp.log1p(small) - jnp.minimum(margin, 0.0), coef


def pulls_of(loss, coef, columns):
    depth = columns.shape[1] - LANES
    pull = jnp.dot(
        coef.astype(jnp.bfloat16), columns[:, :depth], preferred_element_type=jnp.float32
    )
    return pull, jnp.sum(loss, axis=1, keepdims=True)


def tile_kernel(pair_ref, mine_ref, other_ref, got_0, got_1, swapped_0, swapped_1, near_ref, *outs):
    rows = mine_ref.shape[0]
    scale, shift = pair_ref[0:1, 0:1], pair_ref[1:2, 0:1]
    lines = jnp.concatenate(
        [got_0[...], near_ref[:rows, :], mine_ref[...], swapped_1[...]], axis=0
    )
    columns = jnp.concatenate(
        [got_1[...], swapped_0[...], near_ref[rows:, :], other_ref[...]], axis=0
    )
    loss, coef = tile_terms_of(lines, columns, scale, shift)
    pull, loss_sum = pulls_of(loss[: 3 * rows], coef[: 3 * rows], columns)
    put_rows([outs[0]], pull[:rows], loss_sum[:rows])
    put_rows([outs[1]], *pulls_of(loss.T[:rows], coef.T[:rows], lines))
    first = on_first_core()
    half = rows // 2
    halves = []
    for part in (pull, loss_sum):
        low, high = part[rows : rows + half], part[rows + half : 2 * rows]
        halves.append((jnp.where(first, low, high), jnp.where(first, high, low)))
    for out, part, part_loss in zip(outs[2:4], *halves):
        put_rows([out], part, part_loss)
    put_rows([outs[4]], pull[2 * rows :], loss_sum[2 * rows :])


def total(parts, rows, depth):
    pull = jnp.zeros((rows, depth), jnp.float32)
    loss = jnp.zeros((rows, 1), jnp.float32)
    for part in parts:
        tail = part[:, depth:].astype(jnp.int32).astype(jnp.float32)
        pull = pull + decode(part[:, :depth], tail[:, 0:1])
        loss = loss + tail[:, 2:3] * (jnp.exp2(tail[:, 1:2]) * (1.0 / TOP))
    return pull, loss


def place_of(first, rows):
    own = pl.multiple_of(jnp.where(first, 0, rows), rows)
    return pl.ds(own, rows), pl.ds(pl.multiple_of(rows - own, rows), rows)


def add_kernel(own_ref, back_ref, keep_ref, loss_ref, give_ref):
    rows, depth = keep_ref.shape
    own, other = place_of(on_first_core(), rows)
    pull, loss = total([own_ref[other, :], back_ref[other, :]], rows, depth)
    put_rows([give_ref], pull, loss)
    keep_ref[...], loss = total([own_ref[own, :], back_ref[own, :]], rows, depth)
    loss_ref[...] = jnp.broadcast_to(loss, loss_ref.shape)


def more_kernel(keep_ref, kept_loss_ref, back_ref, got_ref, same_ref, cross_ref, image_ref, text_ref, *outs):
    sum_ref, sum_loss_ref, unit_ref, inverse_ref = outs
    rows, depth = keep_ref.shape
    own, _ = place_of(on_first_core(), rows)
    pull, loss = total([same_ref], rows, depth)
    sum_ref[0] = keep_ref[...] + pull
    sum_loss_ref[0] = kept_loss_ref[...] + loss
    sum_ref[1], loss = total([back_ref[own, :], got_ref, cross_ref], rows, depth)
    sum_loss_ref[1] = jnp.broadcast_to(loss, sum_loss_ref.shape[1:])
    for side, ref in enumerate((image_ref, text_ref)):
        unit, inverse = unit_rows(ref[...])
        unit_ref[side] = unit
        inverse_ref[side] = jnp.broadcast_to(inverse, inverse_ref.shape[1:])


def final_kernel(pairs, sum_ref, sum_loss_ref, unit_ref, inverse_ref, got_ref, loss_ref, grad_image_ref, grad_text_ref):
    first = on_first_core()
    rows, depth = sum_ref.shape[1:]
    own, _ = place_of(first, rows)
    pull, loss = total([got_ref[own, :]], rows, depth)
    pulls = (sum_ref[0] + pull, sum_ref[1])
    losses = (sum_loss_ref[0][:, 0:1] + loss, sum_loss_ref[1][:, 0:1])
    for side, (pull, out) in enumerate(
        (
            (jnp.where(first, pulls[0], pulls[1]), grad_image_ref),
            (jnp.where(first, pulls[1], pulls[0]), grad_text_ref),
        )
    ):
        out[...] = project_back(unit_ref[side], inverse_ref[side][:, 0:1], pull)
    row = lax.broadcasted_iota(jnp.int32, (rows, rows), 0)
    column = lax.broadcasted_iota(jnp.int32, (rows, rows), 1)
    loss = jnp.where(first, losses[0], losses[1])
    across = jnp.where(row == column, loss / pairs, 0.0)
    loss_ref[...] = jnp.sum(across, axis=0, keepdims=True)


def chip_plan(image_emb, text_emb, pair_class, scale, shift):
    rows, depth = image_emb.shape
    width = depth + LANES
    lanes = lax.axis_size("txt")
    n = lax.axis_size("img") * lanes
    vmem = pl.BlockSpec(memory_space=pltpu.VMEM)
    smem = pl.BlockSpec(memory_space=pltpu.SMEM)

    def call(kernel, shapes, operands, name, scalars=0, cost=None):
        return pl.pallas_call(
            kernel,
            cost_estimate=cost,
            out_shape=shapes,
            in_specs=[smem] * scalars + [vmem] * (len(operands) - scalars),
            out_specs=jax.tree.map(lambda _: vmem, shapes),
            compiler_params=pltpu.CompilerParams(vmem_limit_bytes=32 << 20),
            name=name,
        )(*operands)

    def block(count, dtype=jnp.bfloat16):
        return jax.ShapeDtypeStruct((count * rows, width), dtype)

    def wide(*shape):
        return jax.ShapeDtypeStruct(shape, jnp.float32)

    def core(i):
        return i // lanes % 2

    def visit(x, masks, cross):
        pairs = []
        for i in range(n):
            chip = (i // (2 * lanes) * lanes + i % lanes) ^ masks[core(i)]
            pairs.append((i, (chip // lanes * 2 + (core(i) ^ cross)) * lanes + chip % lanes))
        return lax.ppermute(x, AXES, pairs)

    def swap(x):
        return lax.ppermute(x, AXES, [(i, i ^ lanes) for i in range(n)])

    visits = (((12, 3), 0), ((2, 8), 0), ((4, 1), 0), ((4, 1), 1))
    late = pl.CostEstimate(flops=10**9, bytes_accessed=10**7, transcendentals=0)
    digits = call(
        digits_kernel,
        jax.ShapeDtypeStruct((rows, LANES), jnp.bfloat16),
        [pair_class],
        "digits",
        cost=late,
    )
    own = call(pack_kernel, block(2), [image_emb, text_emb, digits], "pack")
    *sent, mine, other = call(join_kernel, (block(2),) * 6, [own, swap(own)], "join")
    got = [visit(x, *way) for x, way in zip(sent, visits)]
    near, pair = call(
        near_kernel,
        (block(4), wide(8, LANES)),
        [scale[None], shift[None], *got[2:]],
        "near",
        2,
        late,
    )
    one, two = block(1, jnp.int16), block(2, jnp.int16)
    parts = call(
        tile_kernel,
        (two, two, one, one, two),
        [pair, mine, other, *got[:2], swap(got[0]), swap(got[1]), near],
        "tile",
    )
    back = [visit(x, *way) for x, way in zip(parts, visits)]
    keep, kept_loss, give = call(
        add_kernel, (wide(rows, depth), wide(rows, LANES), one), [parts[4], back[0]], "add"
    )
    sums = call(
        more_kernel,
        (wide(2, rows, depth), wide(2, rows, LANES)) * 2,
        [keep, kept_loss, back[1], swap(give), *back[2:], image_emb, text_emb],
        "more",
        cost=late,
    )
    loss, grad_image, grad_text = call(
        functools.partial(final_kernel, n * rows),
        (wide(1, rows), wide(rows, depth), wide(rows, depth)),
        [*sums, swap(back[1])],
        "final",
    )
    return (loss[0], grad_image, grad_text)


def local(image_emb, text_emb, pair_class, scale, shift):
    if lax.axis_size("img") * lax.axis_size("txt") == 2 * 4 * 4 and lax.axis_size("txt") in (1, 2, 4):
        return chip_plan(image_emb, text_emb, pair_class, scale, shift)
    return tile_plan(image_emb, text_emb, pair_class, scale, shift)


def solution(mesh):
    in_specs = (P(AXES, None), P(AXES, None), P(AXES), P(), P())
    out_specs = (P(AXES), P(AXES, None), P(AXES, None))
    return jax.shard_map(local, mesh=mesh, in_specs=in_specs, out_specs=out_specs, check_vma=False)
```

```python
import functools

import jax
import jax.numpy as jnp
from jax import lax
from jax.experimental import pallas as pl
from jax.experimental.pallas import tpu as pltpu
from jax.sharding import PartitionSpec as P

AXES = ("img", "txt")
DIGITS = 4
LANES = 128
TOP = 32767.0


def unit_rows(rows):
    wide = rows.astype(jnp.float32)
    inverse = 1.0 / jnp.sqrt(jnp.sum(wide * wide, axis=1, keepdims=True) + 1e-06)
    return (wide * inverse, inverse)


def project_back(unit, inverse, pull):
    inner = jnp.sum(unit * pull, axis=1, keepdims=True)
    return (pull - unit * inner) * inverse


def tile_terms(rows_half, row_class, cols_half, col_class, scale, shift):
    logits = (
        scale
        * lax.dot_general(
            rows_half, cols_half, (((1,), (1,)), ((), ())), preferred_element_type=jnp.float32
        )
        + shift
    )
    sign = jnp.where(row_class[:, None] == col_class[None, :], 1.0, -1.0).astype(jnp.float32)
    margin = sign * logits
    loss_part = -jnp.sum(jax.nn.log_sigmoid(margin), axis=1)
    coef = (-sign * jax.nn.sigmoid(-margin) * scale).astype(jnp.bfloat16)
    return (coef, loss_part)


def tile_plan(image_emb, text_emb, pair_class, scale, shift):
    image_unit, image_inv = unit_rows(image_emb)
    text_unit, text_inv = unit_rows(text_emb)
    own_rows = text_emb.shape[0]
    pairs = own_rows * lax.axis_size("img") * lax.axis_size("txt")
    text_half = text_unit.astype(jnp.bfloat16)
    rows_half, row_class = (
        lax.all_gather(image_unit.astype(jnp.bfloat16), "txt", axis=0, tiled=True),
        lax.all_gather(pair_class, "txt", axis=0, tiled=True),
    )
    cols_half, col_class = (
        lax.all_gather(text_half, "img", axis=0, tiled=True),
        lax.all_gather(pair_class, "img", axis=0, tiled=True),
    )
    coef, loss_part = tile_terms(rows_half, row_class, cols_half, col_class, scale, shift)
    image_pull = jnp.dot(coef, cols_half, preferred_element_type=jnp.float32)
    text_pull = lax.psum_scatter(
        lax.dot_general(
            coef, rows_half, (((0,), (0,)), ((), ())), preferred_element_type=jnp.float32
        ),
        "img",
        scatter_dimension=0,
        tiled=True,
    )
    image_sum, loss_sum = (
        lax.psum_scatter(image_pull, "txt", scatter_dimension=0, tiled=True),
        lax.psum_scatter(loss_part, "txt", scatter_dimension=0, tiled=True),
    )
    row_loss = loss_sum / pairs
    grad_image = project_back(image_unit, image_inv, image_sum)
    grad_text = project_back(text_unit, text_inv, text_pull)
    return (row_loss, grad_image, grad_text)


def on_first_core():
    return lax.rem(lax.axis_index("img"), 2) == 0


def class_digits(classes):
    rows = classes.shape[1]
    across = jnp.broadcast_to(classes, (rows, rows))
    row = lax.broadcasted_iota(jnp.int32, (rows, rows), 0)
    column = lax.broadcasted_iota(jnp.int32, (rows, rows), 1)
    lane = lax.broadcasted_iota(jnp.int32, (rows, LANES), 1)
    digits = jnp.zeros((rows, LANES), jnp.float32)
    for k in range(DIGITS):
        byte = (lax.shift_right_logical(across, 8 * k) & 255).astype(jnp.float32)
        down = jnp.sum(jnp.where(row == column, byte, 0.0), axis=1, keepdims=True)
        digits = jnp.where(lane == k, down, digits)
    return digits.astype(jnp.bfloat16)


def digits_kernel(class_ref, digits_ref):
    digits_ref[...] = class_digits(class_ref[...][None, :])


def put_rows_of(image_ref, text_ref, digits, out_ref):
    rows, depth = image_ref.shape
    for start, source in ((0, image_ref), (rows, text_ref)):
        out_ref[start : start + rows, :depth] = unit_rows(source[...])[0].astype(jnp.bfloat16)
        out_ref[start : start + rows, depth:] = digits


def pack_kernel(image_ref, text_ref, digits_ref, out_ref):
    put_rows_of(image_ref, text_ref, digits_ref[...], out_ref)


def join_kernel(own_ref, got_image, got_text, got_class, *refs):
    *refs, got_ref = refs
    put_rows_of(got_image, got_text, class_digits(got_class[...][None, :]), got_ref)
    first = on_first_core()
    rows = own_ref.shape[0] // 2
    own, got = own_ref[...].astype(jnp.float32), got_ref[...].astype(jnp.float32)
    low, high = jnp.where(first, own, got), jnp.where(first, got, own)
    images = jnp.concatenate([low[:rows], high[:rows]], axis=0)
    texts = jnp.concatenate([low[rows:], high[rows:]], axis=0)
    mine = jnp.where(first, images, texts).astype(jnp.bfloat16)
    other = jnp.where(first, texts, images).astype(jnp.bfloat16)
    for ref, block in zip(refs, (mine, other, mine, mine, mine, other)):
        ref[...] = block


def near_kernel(scale_ref, shift_ref, upper_ref, lower_ref, out_ref, pair_ref):
    rows = upper_ref.shape[0]
    out_ref[:rows, :] = upper_ref[...]
    out_ref[rows:, :] = lower_ref[...]
    row = lax.broadcasted_iota(jnp.int32, pair_ref.shape, 0)
    pair_ref[...] = jnp.where(row == 0, scale_ref[0], shift_ref[0])


def power_above(size):
    return jnp.ceil(jnp.log2(jnp.maximum(size, 1e-30)) + 0.01)


def nearest(values):
    return jnp.floor(values + 0.5).astype(jnp.int32)


def code(values, power):
    return nearest(values * (TOP / jnp.exp2(power))).astype(jnp.int16)


def decode(steps, power):
    return steps.astype(jnp.int32).astype(jnp.float32) * (jnp.exp2(power) * (1.0 / TOP))


def put_rows(outs, pull, loss):
    blocks, (rows, width) = len(outs), outs[0].shape
    depth = width - LANES
    power = power_above(jnp.max(jnp.abs(pull), axis=1, keepdims=True))
    steps = code(pull, power)
    lane = lax.broadcasted_iota(jnp.int32, (blocks * rows, LANES), 1)
    loss_power = power_above(loss)
    tail = jnp.where(lane == 0, power, 0.0)
    tail = jnp.where(lane == 1, loss_power, tail)
    tail = jnp.where(lane == 2, loss * (TOP / jnp.exp2(loss_power)), tail)
    tail = nearest(tail).astype(jnp.int16)
    for k, out in enumerate(outs):
        out[:, :depth] = steps[k * rows : (k + 1) * rows]
        out[:, depth:] = tail[k * rows : (k + 1) * rows]


def tile_terms_of(lines, columns, scale, shift):
    depth = lines.shape[1] - LANES
    logits = (
        scale
        * lax.dot_general(
            lines[:, :depth],
            columns[:, :depth],
            (((1,), (1,)), ((), ())),
            preferred_element_type=jnp.float32,
        )
        + shift
    )
    pick = (
        lax.broadcasted_iota(jnp.int32, (8, LANES), 0)
        == lax.broadcasted_iota(jnp.int32, (8, LANES), 1)
    )
    column_digits = lax.dot_general(
        pick.astype(jnp.bfloat16),
        columns[:, depth:],
        (((1,), (1,)), ((), ())),
        preferred_element_type=jnp.float32,
    )
    line_digits = lines[:, depth:].astype(jnp.float32)
    same = None
    for k in range(DIGITS):
        equal = line_digits[:, k : k + 1] == column_digits[k : k + 1, :]
        same = equal if same is None else same & equal
    sign = jnp.where(same, 1.0, -1.0).astype(jnp.float32)
    margin = sign * logits
    small = jnp.exp(-jnp.abs(margin))
    over = 1.0 / (1.0 + small)
    coef = -sign * jnp.where(margin >= 0, small * over, over) * scale
    return jnp.log1p(small) - jnp.minimum(margin, 0.0), coef


def pulls_of(loss, coef, columns):
    depth = columns.shape[1] - LANES
    pull = jnp.dot(
        coef.astype(jnp.bfloat16), columns[:, :depth], preferred_element_type=jnp.float32
    )
    return pull, jnp.sum(loss, axis=1, keepdims=True)


def tile_kernel(pair_ref, mine_ref, other_ref, got_0, got_1, swapped_0, swapped_1, near_ref, *outs):
    rows = mine_ref.shape[0]
    scale, shift = pair_ref[0:1, 0:1], pair_ref[1:2, 0:1]
    lines = jnp.concatenate(
        [got_0[...], near_ref[:rows, :], mine_ref[...], swapped_1[...]], axis=0
    )
    columns = jnp.concatenate(
        [got_1[...], swapped_0[...], near_ref[rows:, :], other_ref[...]], axis=0
    )
    loss, coef = tile_terms_of(lines, columns, scale, shift)
    pull, loss_sum = pulls_of(loss[: 3 * rows], coef[: 3 * rows], columns)
    put_rows([outs[0]], pull[:rows], loss_sum[:rows])
    put_rows([outs[1]], *pulls_of(loss.T[:rows], coef.T[:rows], lines))
    first = on_first_core()
    half = rows // 2
    halves = []
    for part in (pull, loss_sum):
        low, high = part[rows : rows + half], part[rows + half : 2 * rows]
        halves.append((jnp.where(first, low, high), jnp.where(first, high, low)))
    for out, part, part_loss in zip(outs[2:4], *halves):
        put_rows([out], part, part_loss)
    put_rows([outs[4]], pull[2 * rows :], loss_sum[2 * rows :])


def total(parts, rows, depth):
    pull = jnp.zeros((rows, depth), jnp.float32)
    loss = jnp.zeros((rows, 1), jnp.float32)
    for part in parts:
        tail = part[:, depth:].astype(jnp.int32).astype(jnp.float32)
        pull = pull + decode(part[:, :depth], tail[:, 0:1])
        loss = loss + tail[:, 2:3] * (jnp.exp2(tail[:, 1:2]) * (1.0 / TOP))
    return pull, loss


def place_of(first, rows):
    own = pl.multiple_of(jnp.where(first, 0, rows), rows)
    return pl.ds(own, rows), pl.ds(pl.multiple_of(rows - own, rows), rows)


def add_kernel(own_ref, back_ref, keep_ref, loss_ref, give_ref):
    rows, depth = keep_ref.shape
    own, other = place_of(on_first_core(), rows)
    pull, loss = total([own_ref[other, :], back_ref[other, :]], rows, depth)
    put_rows([give_ref], pull, loss)
    keep_ref[...], loss = total([own_ref[own, :], back_ref[own, :]], rows, depth)
    loss_ref[...] = jnp.broadcast_to(loss, loss_ref.shape)


def more_kernel(keep_ref, kept_loss_ref, back_ref, got_ref, same_ref, cross_ref, image_ref, text_ref, *outs):
    sum_ref, sum_loss_ref, unit_ref, inverse_ref = outs
    rows, depth = keep_ref.shape
    own, _ = place_of(on_first_core(), rows)
    pull, loss = total([same_ref], rows, depth)
    sum_ref[0] = keep_ref[...] + pull
    sum_loss_ref[0] = kept_loss_ref[...] + loss
    sum_ref[1], loss = total([back_ref[own, :], got_ref, cross_ref], rows, depth)
    sum_loss_ref[1] = jnp.broadcast_to(loss, sum_loss_ref.shape[1:])
    for side, ref in enumerate((image_ref, text_ref)):
        unit, inverse = unit_rows(ref[...])
        unit_ref[side] = unit
        inverse_ref[side] = jnp.broadcast_to(inverse, inverse_ref.shape[1:])


def final_kernel(pairs, sum_ref, sum_loss_ref, unit_ref, inverse_ref, got_ref, loss_ref, grad_image_ref, grad_text_ref):
    first = on_first_core()
    rows, depth = sum_ref.shape[1:]
    own, _ = place_of(first, rows)
    pull, loss = total([got_ref[own, :]], rows, depth)
    pulls = (sum_ref[0] + pull, sum_ref[1])
    losses = (sum_loss_ref[0][:, 0:1] + loss, sum_loss_ref[1][:, 0:1])
    for side, (pull, out) in enumerate(
        (
            (jnp.where(first, pulls[0], pulls[1]), grad_image_ref),
            (jnp.where(first, pulls[1], pulls[0]), grad_text_ref),
        )
    ):
        out[...] = project_back(unit_ref[side], inverse_ref[side][:, 0:1], pull)
    row = lax.broadcasted_iota(jnp.int32, (rows, rows), 0)
    column = lax.broadcasted_iota(jnp.int32, (rows, rows), 1)
    loss = jnp.where(first, losses[0], losses[1])
    across = jnp.where(row == column, loss / pairs, 0.0)
    loss_ref[...] = jnp.sum(across, axis=0, keepdims=True)


def chip_plan(image_emb, text_emb, pair_class, scale, shift):
    rows, depth = image_emb.shape
    width = depth + LANES
    lanes = lax.axis_size("txt")
    n = lax.axis_size("img") * lanes
    vmem = pl.BlockSpec(memory_space=pltpu.VMEM)
    smem = pl.BlockSpec(memory_space=pltpu.SMEM)

    def call(kernel, shapes, operands, name, scalars=0, cost=None):
        return pl.pallas_call(
            kernel,
            cost_estimate=cost,
            out_shape=shapes,
            in_specs=[smem] * scalars + [vmem] * (len(operands) - scalars),
            out_specs=jax.tree.map(lambda _: vmem, shapes),
            compiler_params=pltpu.CompilerParams(vmem_limit_bytes=32 << 20),
            name=name,
        )(*operands)

    def block(count, dtype=jnp.bfloat16):
        return jax.ShapeDtypeStruct((count * rows, width), dtype)

    def wide(*shape):
        return jax.ShapeDtypeStruct(shape, jnp.float32)

    def core(i):
        return i // lanes % 2

    def visit(x, masks, cross):
        pairs = []
        for i in range(n):
            chip = (i // (2 * lanes) * lanes + i % lanes) ^ masks[core(i)]
            pairs.append((i, (chip // lanes * 2 + (core(i) ^ cross)) * lanes + chip % lanes))
        return lax.ppermute(x, AXES, pairs)

    def swap(x):
        return lax.ppermute(x, AXES, [(i, i ^ lanes) for i in range(n)])

    visits = (((12, 3), 0), ((2, 8), 0), ((4, 1), 0), ((4, 1), 1))
    late = pl.CostEstimate(flops=10**9, bytes_accessed=10**7, transcendentals=0)
    digits = call(
        digits_kernel,
        jax.ShapeDtypeStruct((rows, LANES), jnp.bfloat16),
        [pair_class],
        "digits",
        cost=late,
    )
    own = call(pack_kernel, block(2), [image_emb, text_emb, digits], "pack")
    swapped = [swap(x) for x in (image_emb, text_emb, pair_class)]
    *sent, mine, other, _ = call(join_kernel, (block(2),) * 7, [own, *swapped], "join")
    got = [visit(x, *way) for x, way in zip(sent, visits)]
    near, pair = call(
        near_kernel,
        (block(4), wide(8, LANES)),
        [scale[None], shift[None], *got[2:]],
        "near",
        2,
        late,
    )
    one, two = block(1, jnp.int16), block(2, jnp.int16)
    parts = call(
        tile_kernel,
        (two, two, one, one, two),
        [pair, mine, other, *got[:2], swap(got[0]), swap(got[1]), near],
        "tile",
    )
    back = [visit(x, *way) for x, way in zip(parts, visits)]
    keep, kept_loss, give = call(
        add_kernel, (wide(rows, depth), wide(rows, LANES), one), [parts[4], back[0]], "add"
    )
    sums = call(
        more_kernel,
        (wide(2, rows, depth), wide(2, rows, LANES)) * 2,
        [keep, kept_loss, back[1], swap(give), *back[2:], image_emb, text_emb],
        "more",
        cost=late,
    )
    loss, grad_image, grad_text = call(
        functools.partial(final_kernel, n * rows),
        (wide(1, rows), wide(rows, depth), wide(rows, depth)),
        [*sums, swap(back[1])],
        "final",
    )
    return (loss[0], grad_image, grad_text)


def local(image_emb, text_emb, pair_class, scale, shift):
    if lax.axis_size("img") * lax.axis_size("txt") == 2 * 4 * 4 and lax.axis_size("txt") in (1, 2, 4):
        return chip_plan(image_emb, text_emb, pair_class, scale, shift)
    return tile_plan(image_emb, text_emb, pair_class, scale, shift)


def solution(mesh):
    in_specs = (P(AXES, None), P(AXES, None), P(AXES), P(), P())
    out_specs = (P(AXES), P(AXES, None), P(AXES, None))
    return jax.shard_map(local, mesh=mesh, in_specs=in_specs, out_specs=out_specs, check_vma=False)
```

```python
import functools

import jax
import jax.numpy as jnp
from jax import lax
from jax.experimental import pallas as pl
from jax.experimental.pallas import tpu as pltpu
from jax.sharding import PartitionSpec as P

AXES = ("img", "txt")
DIGITS = 4
LANES = 128
TOP = 32767.0


def unit_rows(rows):
    wide = rows.astype(jnp.float32)
    inverse = 1.0 / jnp.sqrt(jnp.sum(wide * wide, axis=1, keepdims=True) + 1e-06)
    return (wide * inverse, inverse)


def project_back(unit, inverse, pull):
    inner = jnp.sum(unit * pull, axis=1, keepdims=True)
    return (pull - unit * inner) * inverse


def tile_terms(rows_half, row_class, cols_half, col_class, scale, shift):
    logits = (
        scale
        * lax.dot_general(
            rows_half, cols_half, (((1,), (1,)), ((), ())), preferred_element_type=jnp.float32
        )
        + shift
    )
    sign = jnp.where(row_class[:, None] == col_class[None, :], 1.0, -1.0).astype(jnp.float32)
    margin = sign * logits
    loss_part = -jnp.sum(jax.nn.log_sigmoid(margin), axis=1)
    coef = (-sign * jax.nn.sigmoid(-margin) * scale).astype(jnp.bfloat16)
    return (coef, loss_part)


def tile_plan(image_emb, text_emb, pair_class, scale, shift):
    image_unit, image_inv = unit_rows(image_emb)
    text_unit, text_inv = unit_rows(text_emb)
    own_rows = text_emb.shape[0]
    pairs = own_rows * lax.axis_size("img") * lax.axis_size("txt")
    text_half = text_unit.astype(jnp.bfloat16)
    rows_half, row_class = (
        lax.all_gather(image_unit.astype(jnp.bfloat16), "txt", axis=0, tiled=True),
        lax.all_gather(pair_class, "txt", axis=0, tiled=True),
    )
    cols_half, col_class = (
        lax.all_gather(text_half, "img", axis=0, tiled=True),
        lax.all_gather(pair_class, "img", axis=0, tiled=True),
    )
    coef, loss_part = tile_terms(rows_half, row_class, cols_half, col_class, scale, shift)
    image_pull = jnp.dot(coef, cols_half, preferred_element_type=jnp.float32)
    text_pull = lax.psum_scatter(
        lax.dot_general(
            coef, rows_half, (((0,), (0,)), ((), ())), preferred_element_type=jnp.float32
        ),
        "img",
        scatter_dimension=0,
        tiled=True,
    )
    image_sum, loss_sum = (
        lax.psum_scatter(image_pull, "txt", scatter_dimension=0, tiled=True),
        lax.psum_scatter(loss_part, "txt", scatter_dimension=0, tiled=True),
    )
    row_loss = loss_sum / pairs
    grad_image = project_back(image_unit, image_inv, image_sum)
    grad_text = project_back(text_unit, text_inv, text_pull)
    return (row_loss, grad_image, grad_text)


def on_first_core():
    return lax.rem(lax.axis_index("img"), 2) == 0


def class_digits(classes):
    rows = classes.shape[1]
    across = jnp.broadcast_to(classes, (rows, rows))
    row = lax.broadcasted_iota(jnp.int32, (rows, rows), 0)
    column = lax.broadcasted_iota(jnp.int32, (rows, rows), 1)
    lane = lax.broadcasted_iota(jnp.int32, (rows, LANES), 1)
    digits = jnp.zeros((rows, LANES), jnp.float32)
    for k in range(DIGITS):
        byte = (lax.shift_right_logical(across, 8 * k) & 255).astype(jnp.float32)
        down = jnp.sum(jnp.where(row == column, byte, 0.0), axis=1, keepdims=True)
        digits = jnp.where(lane == k, down, digits)
    return digits.astype(jnp.bfloat16)


def digits_kernel(class_ref, digits_ref):
    digits_ref[...] = class_digits(class_ref[...][None, :])


def put_rows_of(image_ref, text_ref, digits, out_ref):
    rows, depth = image_ref.shape
    for start, source in ((0, image_ref), (rows, text_ref)):
        out_ref[start : start + rows, :depth] = unit_rows(source[...])[0].astype(jnp.bfloat16)
        out_ref[start : start + rows, depth:] = digits


def pack_kernel(image_ref, text_ref, digits_ref, out_ref):
    put_rows_of(image_ref, text_ref, digits_ref[...], out_ref)


def join_kernel(own_ref, got_image, got_text, got_class, *refs):
    *refs, got_ref = refs
    put_rows_of(got_image, got_text, class_digits(got_class[...][None, :]), got_ref)
    first = on_first_core()
    rows = own_ref.shape[0] // 2
    own, got = own_ref[...].astype(jnp.float32), got_ref[...].astype(jnp.float32)
    low, high = jnp.where(first, own, got), jnp.where(first, got, own)
    images = jnp.concatenate([low[:rows], high[:rows]], axis=0)
    texts = jnp.concatenate([low[rows:], high[rows:]], axis=0)
    mine, other = jnp.where(first, images, texts), jnp.where(first, texts, images)
    for ref, block in zip(refs, (images, texts, mine, mine, mine, other)):
        ref[...] = block.astype(jnp.bfloat16)


def near_kernel(scale_ref, shift_ref, upper_ref, lower_ref, out_ref, pair_ref):
    rows = upper_ref.shape[0]
    out_ref[:rows, :] = upper_ref[...]
    out_ref[rows:, :] = lower_ref[...]
    row = lax.broadcasted_iota(jnp.int32, pair_ref.shape, 0)
    pair_ref[...] = jnp.where(row == 0, scale_ref[0], shift_ref[0])


def power_above(size):
    return jnp.ceil(jnp.log2(jnp.maximum(size, 1e-30)) + 0.01)


def nearest(values):
    return jnp.floor(values + 0.5).astype(jnp.int32)


def code(values, power):
    return nearest(values * (TOP / jnp.exp2(power))).astype(jnp.int16)


def decode(steps, power):
    return steps.astype(jnp.int32).astype(jnp.float32) * (jnp.exp2(power) * (1.0 / TOP))


def put_rows(outs, pull, loss):
    blocks, (rows, width) = len(outs), outs[0].shape
    depth = width - LANES
    power = power_above(jnp.max(jnp.abs(pull), axis=1, keepdims=True))
    steps = code(pull, power)
    lane = lax.broadcasted_iota(jnp.int32, (blocks * rows, LANES), 1)
    loss_power = power_above(loss)
    tail = jnp.where(lane == 0, power, 0.0)
    tail = jnp.where(lane == 1, loss_power, tail)
    tail = jnp.where(lane == 2, loss * (TOP / jnp.exp2(loss_power)), tail)
    tail = nearest(tail).astype(jnp.int16)
    for k, out in enumerate(outs):
        out[:, :depth] = steps[k * rows : (k + 1) * rows]
        out[:, depth:] = tail[k * rows : (k + 1) * rows]


def tile_terms_of(lines, columns, scale, shift):
    depth = lines.shape[1] - LANES
    logits = (
        scale
        * lax.dot_general(
            lines[:, :depth],
            columns[:, :depth],
            (((1,), (1,)), ((), ())),
            preferred_element_type=jnp.float32,
        )
        + shift
    )
    pick = (
        lax.broadcasted_iota(jnp.int32, (8, LANES), 0)
        == lax.broadcasted_iota(jnp.int32, (8, LANES), 1)
    )
    column_digits = lax.dot_general(
        pick.astype(jnp.bfloat16),
        columns[:, depth:],
        (((1,), (1,)), ((), ())),
        preferred_element_type=jnp.float32,
    )
    line_digits = lines[:, depth:].astype(jnp.float32)
    same = None
    for k in range(DIGITS):
        equal = line_digits[:, k : k + 1] == column_digits[k : k + 1, :]
        same = equal if same is None else same & equal
    sign = jnp.where(same, 1.0, -1.0).astype(jnp.float32)
    margin = sign * logits
    small = jnp.exp(-jnp.abs(margin))
    over = 1.0 / (1.0 + small)
    coef = -sign * jnp.where(margin >= 0, small * over, over) * scale
    return jnp.log1p(small) - jnp.minimum(margin, 0.0), coef


def pulls_of(loss, coef, columns):
    depth = columns.shape[1] - LANES
    pull = jnp.dot(
        coef.astype(jnp.bfloat16), columns[:, :depth], preferred_element_type=jnp.float32
    )
    return pull, jnp.sum(loss, axis=1, keepdims=True)


def tile_kernel(pair_ref, mine_ref, other_ref, images, texts, other_images, other_texts, near_ref, *outs):
    rows = mine_ref.shape[0]
    first = on_first_core()
    scale, shift = pair_ref[0:1, 0:1], pair_ref[1:2, 0:1]

    def pick(one, two):
        return jnp.where(first, one, two)

    def parted(image_ref, text_ref):
        image, text = image_ref[...].astype(jnp.float32), text_ref[...].astype(jnp.float32)
        return pick(image, text).astype(jnp.bfloat16), pick(text, image).astype(jnp.bfloat16)

    (line, column), (other_line, other_column) = parted(images, texts), parted(other_images, other_texts)
    lines = jnp.concatenate([line, near_ref[:rows, :], mine_ref[...], other_line], axis=0)
    columns = jnp.concatenate([column, other_column, near_ref[rows:, :], other_ref[...]], axis=0)
    loss, coef = tile_terms_of(lines, columns, scale, shift)
    pull, loss_sum = pulls_of(loss[: 3 * rows], coef[: 3 * rows], columns)
    column_pull, column_loss = pulls_of(loss.T[:rows], coef.T[:rows], lines)
    line_pull, line_loss = pull[:rows], loss_sum[:rows]
    put_rows([outs[0]], pick(line_pull, column_pull), pick(line_loss, column_loss))
    put_rows([outs[1]], pick(column_pull, line_pull), pick(column_loss, line_loss))
    half = rows // 2
    halves = [], []
    for start in (rows, 2 * rows):
        for part, listing in zip((pull, loss_sum), halves):
            low, high = part[start : start + half], part[start + half : start + rows]
            listing.extend((pick(low, high), pick(high, low)))
    for out, part, part_loss in zip(outs[2:], *halves):
        put_rows([out], part, part_loss)


def total(parts, rows, depth):
    pull = jnp.zeros((rows, depth), jnp.float32)
    loss = jnp.zeros((rows, 1), jnp.float32)
    for part in parts:
        tail = part[:, depth:].astype(jnp.int32).astype(jnp.float32)
        pull = pull + decode(part[:, :depth], tail[:, 0:1])
        loss = loss + tail[:, 2:3] * (jnp.exp2(tail[:, 1:2]) * (1.0 / TOP))
    return pull, loss


def place_of(first, rows):
    own = pl.multiple_of(jnp.where(first, 0, rows), rows)
    return pl.ds(own, rows), pl.ds(pl.multiple_of(rows - own, rows), rows)


def give_kernel(back_ref, give_ref):
    _, other = place_of(on_first_core(), give_ref.shape[0])
    give_ref[...] = back_ref[other, :]


def more_kernel(own_ref, text_back, got_own, got_text, same_ref, cross_ref, image_ref, text_ref, *outs):
    sum_ref, sum_loss_ref, unit_ref, inverse_ref = outs
    first = on_first_core()
    rows, depth = sum_ref.shape[1:]
    own, _ = place_of(first, rows)
    mine = total([own_ref, same_ref], rows, depth)
    other = total([got_own, cross_ref], rows, depth)
    texts = total([text_back[own, :], got_text], rows, depth)
    for side, (one, two, back) in enumerate(((mine, other, None), (other, mine, texts))):
        pull, loss = (jnp.where(first, x, y) for x, y in zip(one, two))
        sum_ref[side] = pull if back is None else pull + back[0]
        loss = loss if back is None else loss + back[1]
        sum_loss_ref[side] = jnp.broadcast_to(loss, sum_loss_ref.shape[1:])
    for side, ref in enumerate((image_ref, text_ref)):
        unit, inverse = unit_rows(ref[...])
        unit_ref[side] = unit
        inverse_ref[side] = jnp.broadcast_to(inverse, inverse_ref.shape[1:])


def final_kernel(pairs, sum_ref, sum_loss_ref, unit_ref, inverse_ref, back_ref, got_ref, *outs):
    loss_ref, grad_image_ref, grad_text_ref = outs
    rows, depth = sum_ref.shape[1:]
    own, _ = place_of(on_first_core(), rows)
    pull, loss = total([back_ref[own, :], got_ref[own, :]], rows, depth)
    for side, (side_pull, out) in enumerate(((sum_ref[0] + pull, grad_image_ref), (sum_ref[1], grad_text_ref))):
        out[...] = project_back(unit_ref[side], inverse_ref[side][:, 0:1], side_pull)
    row = lax.broadcasted_iota(jnp.int32, (rows, rows), 0)
    column = lax.broadcasted_iota(jnp.int32, (rows, rows), 1)
    across = jnp.where(row == column, (sum_loss_ref[0][:, 0:1] + loss) / pairs, 0.0)
    loss_ref[...] = jnp.sum(across, axis=0, keepdims=True)


def chip_plan(image_emb, text_emb, pair_class, scale, shift):
    rows, depth = image_emb.shape
    width = depth + LANES
    lanes = lax.axis_size("txt")
    n = lax.axis_size("img") * lanes
    vmem = pl.BlockSpec(memory_space=pltpu.VMEM)
    smem = pl.BlockSpec(memory_space=pltpu.SMEM)

    def call(kernel, shapes, operands, name, scalars=0, cost=None, scratch=()):
        return pl.pallas_call(
            kernel,
            scratch_shapes=scratch,
            cost_estimate=cost,
            out_shape=shapes,
            in_specs=[smem] * scalars + [vmem] * (len(operands) - scalars),
            out_specs=jax.tree.map(lambda _: vmem, shapes),
            compiler_params=pltpu.CompilerParams(vmem_limit_bytes=32 << 20),
            name=name,
        )(*operands)

    def block(count, dtype=jnp.bfloat16):
        return jax.ShapeDtypeStruct((count * rows, width), dtype)

    def wide(*shape):
        return jax.ShapeDtypeStruct(shape, jnp.float32)

    def core(i):
        return i // lanes % 2

    def visit(x, masks, cross):
        pairs = []
        for i in range(n):
            chip = (i // (2 * lanes) * lanes + i % lanes) ^ masks[core(i)]
            pairs.append((i, (chip // lanes * 2 + (core(i) ^ cross)) * lanes + chip % lanes))
        return lax.ppermute(x, AXES, pairs)

    def swap(x):
        return lax.ppermute(x, AXES, [(i, i ^ lanes) for i in range(n)])

    visits = (((12, 8), 0), ((2, 3), 0), ((4, 1), 0), ((4, 1), 1))
    late = pl.CostEstimate(flops=10**9, bytes_accessed=10**7, transcendentals=0)
    digits = call(
        digits_kernel,
        jax.ShapeDtypeStruct((rows, LANES), jnp.bfloat16),
        [pair_class],
        "digits",
        cost=late,
    )
    own = call(pack_kernel, block(2), [image_emb, text_emb, digits], "pack")
    swapped = [swap(x) for x in (image_emb, text_emb, pair_class)]
    *sent, mine, other = call(
        join_kernel,
        (block(2),) * 6,
        [own, *swapped],
        "join",
        scratch=[pltpu.VMEM((2 * rows, width), jnp.bfloat16)],
    )
    got = [visit(x, *way) for x, way in zip(sent, visits)]
    near, pair = call(
        near_kernel,
        (block(4), wide(8, LANES)),
        [scale[None], shift[None], *got[2:]],
        "near",
        2,
        late,
    )
    one, two = block(1, jnp.int16), block(2, jnp.int16)
    parts = call(
        tile_kernel,
        (two, two, one, one, one, one),
        [pair, mine, other, *got[:2], swap(got[0]), swap(got[1]), near],
        "tile",
    )
    back = [visit(x, *way) for x, way in zip(parts, visits)]
    give = call(give_kernel, one, [back[1]], "give")
    sums = call(
        more_kernel,
        (wide(2, rows, depth), wide(2, rows, LANES)) * 2,
        [parts[4], back[1], swap(parts[5]), swap(give), *back[2:], image_emb, text_emb],
        "more",
        cost=late,
    )
    loss, grad_image, grad_text = call(
        functools.partial(final_kernel, n * rows),
        (wide(1, rows), wide(rows, depth), wide(rows, depth)),
        [*sums, back[0], swap(back[0])],
        "final",
    )
    return (loss[0], grad_image, grad_text)


def local(image_emb, text_emb, pair_class, scale, shift):
    if lax.axis_size("img") * lax.axis_size("txt") == 2 * 4 * 4 and lax.axis_size("txt") in (1, 2, 4):
        return chip_plan(image_emb, text_emb, pair_class, scale, shift)
    return tile_plan(image_emb, text_emb, pair_class, scale, shift)


def solution(mesh):
    in_specs = (P(AXES, None), P(AXES, None), P(AXES), P(), P())
    out_specs = (P(AXES), P(AXES, None), P(AXES, None))
    return jax.shard_map(local, mesh=mesh, in_specs=in_specs, out_specs=out_specs, check_vma=False)
```

```python
import functools

import jax
import jax.numpy as jnp
from jax import lax
from jax.experimental import pallas as pl
from jax.experimental.pallas import tpu as pltpu
from jax.sharding import PartitionSpec as P

AXES = ("img", "txt")
DIGITS = 4
LANES = 128
TOP = 32767.0


def unit_rows(rows):
    wide = rows.astype(jnp.float32)
    inverse = 1.0 / jnp.sqrt(jnp.sum(wide * wide, axis=1, keepdims=True) + 1e-06)
    return (wide * inverse, inverse)


def project_back(unit, inverse, pull):
    inner = jnp.sum(unit * pull, axis=1, keepdims=True)
    return (pull - unit * inner) * inverse


def tile_terms(rows_half, row_class, cols_half, col_class, scale, shift):
    logits = (
        scale
        * lax.dot_general(
            rows_half, cols_half, (((1,), (1,)), ((), ())), preferred_element_type=jnp.float32
        )
        + shift
    )
    sign = jnp.where(row_class[:, None] == col_class[None, :], 1.0, -1.0).astype(jnp.float32)
    margin = sign * logits
    loss_part = -jnp.sum(jax.nn.log_sigmoid(margin), axis=1)
    coef = (-sign * jax.nn.sigmoid(-margin) * scale).astype(jnp.bfloat16)
    return (coef, loss_part)


def tile_plan(image_emb, text_emb, pair_class, scale, shift):
    image_unit, image_inv = unit_rows(image_emb)
    text_unit, text_inv = unit_rows(text_emb)
    own_rows = text_emb.shape[0]
    pairs = own_rows * lax.axis_size("img") * lax.axis_size("txt")
    text_half = text_unit.astype(jnp.bfloat16)
    rows_half, row_class = (
        lax.all_gather(image_unit.astype(jnp.bfloat16), "txt", axis=0, tiled=True),
        lax.all_gather(pair_class, "txt", axis=0, tiled=True),
    )
    cols_half, col_class = (
        lax.all_gather(text_half, "img", axis=0, tiled=True),
        lax.all_gather(pair_class, "img", axis=0, tiled=True),
    )
    coef, loss_part = tile_terms(rows_half, row_class, cols_half, col_class, scale, shift)
    image_pull = jnp.dot(coef, cols_half, preferred_element_type=jnp.float32)
    text_pull = lax.psum_scatter(
        lax.dot_general(
            coef, rows_half, (((0,), (0,)), ((), ())), preferred_element_type=jnp.float32
        ),
        "img",
        scatter_dimension=0,
        tiled=True,
    )
    image_sum, loss_sum = (
        lax.psum_scatter(image_pull, "txt", scatter_dimension=0, tiled=True),
        lax.psum_scatter(loss_part, "txt", scatter_dimension=0, tiled=True),
    )
    row_loss = loss_sum / pairs
    grad_image = project_back(image_unit, image_inv, image_sum)
    grad_text = project_back(text_unit, text_inv, text_pull)
    return (row_loss, grad_image, grad_text)


def on_first_core():
    return lax.rem(lax.axis_index("img"), 2) == 0


def class_digits(classes):
    rows = classes.shape[1]
    across = jnp.broadcast_to(classes, (rows, rows))
    row = lax.broadcasted_iota(jnp.int32, (rows, rows), 0)
    column = lax.broadcasted_iota(jnp.int32, (rows, rows), 1)
    lane = lax.broadcasted_iota(jnp.int32, (rows, LANES), 1)
    digits = jnp.zeros((rows, LANES), jnp.float32)
    for k in range(DIGITS):
        byte = (lax.shift_right_logical(across, 8 * k) & 255).astype(jnp.float32)
        down = jnp.sum(jnp.where(row == column, byte, 0.0), axis=1, keepdims=True)
        digits = jnp.where(lane == k, down, digits)
    return digits.astype(jnp.bfloat16)


def digits_kernel(class_ref, digits_ref):
    digits_ref[...] = class_digits(class_ref[...][None, :])


def put_rows_of(image_ref, text_ref, digits, out_ref):
    rows, depth = image_ref.shape
    for start, source in ((0, image_ref), (rows, text_ref)):
        out_ref[start : start + rows, :depth] = unit_rows(source[...])[0].astype(jnp.bfloat16)
        out_ref[start : start + rows, depth:] = digits


def pack_kernel(image_ref, text_ref, digits_ref, out_ref):
    put_rows_of(image_ref, text_ref, digits_ref[...], out_ref)


def join_kernel(own_ref, got_image, got_text, got_class, *refs):
    *refs, got_ref = refs
    put_rows_of(got_image, got_text, class_digits(got_class[...][None, :]), got_ref)
    first = on_first_core()
    rows = own_ref.shape[0] // 2
    own, got = own_ref[...].astype(jnp.float32), got_ref[...].astype(jnp.float32)
    low, high = jnp.where(first, own, got), jnp.where(first, got, own)
    images = jnp.concatenate([low[:rows], high[:rows]], axis=0)
    texts = jnp.concatenate([low[rows:], high[rows:]], axis=0)
    mine, other = jnp.where(first, images, texts), jnp.where(first, texts, images)
    for ref, block in zip(refs, (images, texts, mine, mine, mine, other)):
        ref[...] = block.astype(jnp.bfloat16)


def near_kernel(scale_ref, shift_ref, upper_ref, lower_ref, out_ref, pair_ref):
    rows = upper_ref.shape[0]
    out_ref[:rows, :] = upper_ref[...]
    out_ref[rows:, :] = lower_ref[...]
    row = lax.broadcasted_iota(jnp.int32, pair_ref.shape, 0)
    pair_ref[...] = jnp.where(row == 0, scale_ref[0], shift_ref[0])


def power_above(size):
    return jnp.ceil(jnp.log2(jnp.maximum(size, 1e-30)) + 0.01)


def nearest(values):
    return jnp.floor(values + 0.5).astype(jnp.int32)


def code(values, power):
    return nearest(values * (TOP / jnp.exp2(power))).astype(jnp.int16)


def decode(steps, power):
    return steps.astype(jnp.int32).astype(jnp.float32) * (jnp.exp2(power) * (1.0 / TOP))


def put_rows(outs, pull, loss):
    blocks, (rows, width) = len(outs), outs[0].shape
    depth = width - LANES
    power = power_above(jnp.max(jnp.abs(pull), axis=1, keepdims=True))
    steps = code(pull, power)
    lane = lax.broadcasted_iota(jnp.int32, (blocks * rows, LANES), 1)
    loss_power = power_above(loss)
    tail = jnp.where(lane == 0, power, 0.0)
    tail = jnp.where(lane == 1, loss_power, tail)
    tail = jnp.where(lane == 2, loss * (TOP / jnp.exp2(loss_power)), tail)
    tail = nearest(tail).astype(jnp.int16)
    for k, out in enumerate(outs):
        out[:, :depth] = steps[k * rows : (k + 1) * rows]
        out[:, depth:] = tail[k * rows : (k + 1) * rows]


def tile_terms_of(lines, columns, scale, shift):
    depth = lines.shape[1] - LANES
    logits = (
        scale
        * lax.dot_general(
            lines[:, :depth],
            columns[:, :depth],
            (((1,), (1,)), ((), ())),
            preferred_element_type=jnp.float32,
        )
        + shift
    )
    pick = (
        lax.broadcasted_iota(jnp.int32, (8, LANES), 0)
        == lax.broadcasted_iota(jnp.int32, (8, LANES), 1)
    )
    column_digits = lax.dot_general(
        pick.astype(jnp.bfloat16),
        columns[:, depth:],
        (((1,), (1,)), ((), ())),
        preferred_element_type=jnp.float32,
    )
    line_digits = lines[:, depth:].astype(jnp.float32)
    same = None
    for k in range(DIGITS):
        equal = line_digits[:, k : k + 1] == column_digits[k : k + 1, :]
        same = equal if same is None else same & equal
    sign = jnp.where(same, 1.0, -1.0).astype(jnp.float32)
    margin = sign * logits
    small = jnp.exp(-jnp.abs(margin))
    over = 1.0 / (1.0 + small)
    coef = -sign * jnp.where(margin >= 0, small * over, over) * scale
    return jnp.log1p(small) - jnp.minimum(margin, 0.0), coef


def pulls_of(loss, coef, columns):
    depth = columns.shape[1] - LANES
    pull = jnp.dot(
        coef.astype(jnp.bfloat16), columns[:, :depth], preferred_element_type=jnp.float32
    )
    return pull, jnp.sum(loss, axis=1, keepdims=True)


def tile_kernel(pair_ref, mine_ref, other_ref, images, texts, other_images, other_texts, near_ref, *outs):
    rows = mine_ref.shape[0]
    first = on_first_core()
    scale, shift = pair_ref[0:1, 0:1], pair_ref[1:2, 0:1]

    def pick(one, two):
        return jnp.where(first, one, two)

    def parted(image_ref, text_ref):
        image, text = image_ref[...].astype(jnp.float32), text_ref[...].astype(jnp.float32)
        return pick(image, text).astype(jnp.bfloat16), pick(text, image).astype(jnp.bfloat16)

    (line, column), (other_line, other_column) = parted(images, texts), parted(other_images, other_texts)
    lines = jnp.concatenate([line, near_ref[:rows, :], mine_ref[...], other_line], axis=0)
    columns = jnp.concatenate([column, other_column, near_ref[rows:, :], other_ref[...]], axis=0)
    loss, coef = tile_terms_of(lines, columns, scale, shift)
    pull, loss_sum = pulls_of(loss[: 3 * rows], coef[: 3 * rows], columns)
    put_rows([outs[0]], pull[:rows], loss_sum[:rows])
    put_rows([outs[1]], *pulls_of(loss.T[:rows], coef.T[:rows], lines))
    half = rows // 2
    halves = []
    for part in (pull, loss_sum):
        low, high = part[rows : rows + half], part[rows + half : 2 * rows]
        halves.append((pick(low, high), pick(high, low)))
    for out, part, part_loss in zip(outs[2:4], *halves):
        put_rows([out], part, part_loss)
    put_rows([outs[4]], pull[2 * rows :], loss_sum[2 * rows :])


def total(parts, rows, depth):
    pull = jnp.zeros((rows, depth), jnp.float32)
    loss = jnp.zeros((rows, 1), jnp.float32)
    for part in parts:
        tail = part[:, depth:].astype(jnp.int32).astype(jnp.float32)
        pull = pull + decode(part[:, :depth], tail[:, 0:1])
        loss = loss + tail[:, 2:3] * (jnp.exp2(tail[:, 1:2]) * (1.0 / TOP))
    return pull, loss


def place_of(first, rows):
    own = pl.multiple_of(jnp.where(first, 0, rows), rows)
    return pl.ds(own, rows), pl.ds(pl.multiple_of(rows - own, rows), rows)


def add_kernel(own_ref, back_ref, keep_ref, loss_ref, give_ref):
    rows, depth = keep_ref.shape
    own, other = place_of(on_first_core(), rows)
    pull, loss = total([own_ref[other, :], back_ref[other, :]], rows, depth)
    put_rows([give_ref], pull, loss)
    keep_ref[...], loss = total([own_ref[own, :], back_ref[own, :]], rows, depth)
    loss_ref[...] = jnp.broadcast_to(loss, loss_ref.shape)


def more_kernel(keep_ref, kept_loss_ref, back_ref, got_ref, same_ref, cross_ref, image_ref, text_ref, *outs):
    sum_ref, sum_loss_ref, unit_ref, inverse_ref = outs
    rows, depth = keep_ref.shape
    own, _ = place_of(on_first_core(), rows)
    pull, loss = total([same_ref], rows, depth)
    sum_ref[0] = keep_ref[...] + pull
    sum_loss_ref[0] = kept_loss_ref[...] + loss
    sum_ref[1], loss = total([back_ref[own, :], got_ref, cross_ref], rows, depth)
    sum_loss_ref[1] = jnp.broadcast_to(loss, sum_loss_ref.shape[1:])
    for side, ref in enumerate((image_ref, text_ref)):
        unit, inverse = unit_rows(ref[...])
        unit_ref[side] = unit
        inverse_ref[side] = jnp.broadcast_to(inverse, inverse_ref.shape[1:])


def final_kernel(pairs, sum_ref, sum_loss_ref, unit_ref, inverse_ref, got_ref, loss_ref, grad_image_ref, grad_text_ref):
    first = on_first_core()
    rows, depth = sum_ref.shape[1:]
    own, _ = place_of(first, rows)
    pull, loss = total([got_ref[own, :]], rows, depth)
    pulls = (sum_ref[0] + pull, sum_ref[1])
    losses = (sum_loss_ref[0][:, 0:1] + loss, sum_loss_ref[1][:, 0:1])
    for side, (pull, out) in enumerate(
        (
            (jnp.where(first, pulls[0], pulls[1]), grad_image_ref),
            (jnp.where(first, pulls[1], pulls[0]), grad_text_ref),
        )
    ):
        out[...] = project_back(unit_ref[side], inverse_ref[side][:, 0:1], pull)
    row = lax.broadcasted_iota(jnp.int32, (rows, rows), 0)
    column = lax.broadcasted_iota(jnp.int32, (rows, rows), 1)
    loss = jnp.where(first, losses[0], losses[1])
    across = jnp.where(row == column, loss / pairs, 0.0)
    loss_ref[...] = jnp.sum(across, axis=0, keepdims=True)


def chip_plan(image_emb, text_emb, pair_class, scale, shift):
    rows, depth = image_emb.shape
    width = depth + LANES
    lanes = lax.axis_size("txt")
    n = lax.axis_size("img") * lanes
    vmem = pl.BlockSpec(memory_space=pltpu.VMEM)
    smem = pl.BlockSpec(memory_space=pltpu.SMEM)

    def call(kernel, shapes, operands, name, scalars=0, cost=None, scratch=()):
        return pl.pallas_call(
            kernel,
            scratch_shapes=scratch,
            cost_estimate=cost,
            out_shape=shapes,
            in_specs=[smem] * scalars + [vmem] * (len(operands) - scalars),
            out_specs=jax.tree.map(lambda _: vmem, shapes),
            compiler_params=pltpu.CompilerParams(vmem_limit_bytes=32 << 20),
            name=name,
        )(*operands)

    def block(count, dtype=jnp.bfloat16):
        return jax.ShapeDtypeStruct((count * rows, width), dtype)

    def wide(*shape):
        return jax.ShapeDtypeStruct(shape, jnp.float32)

    def core(i):
        return i // lanes % 2

    def visit(x, masks, cross):
        pairs = []
        for i in range(n):
            chip = (i // (2 * lanes) * lanes + i % lanes) ^ masks[core(i)]
            pairs.append((i, (chip // lanes * 2 + (core(i) ^ cross)) * lanes + chip % lanes))
        return lax.ppermute(x, AXES, pairs)

    def swap(x):
        return lax.ppermute(x, AXES, [(i, i ^ lanes) for i in range(n)])

    out_visits = (((12, 8), 0), ((2, 3), 0), ((4, 1), 0), ((4, 1), 1))
    back_visits = (((12, 3), 0), ((2, 8), 0), ((4, 1), 0), ((4, 1), 1))
    late = pl.CostEstimate(flops=10**9, bytes_accessed=10**7, transcendentals=0)
    digits = call(
        digits_kernel,
        jax.ShapeDtypeStruct((rows, LANES), jnp.bfloat16),
        [pair_class],
        "digits",
        cost=late,
    )
    own = call(pack_kernel, block(2), [image_emb, text_emb, digits], "pack")
    swapped = [swap(x) for x in (image_emb, text_emb, pair_class)]
    *sent, mine, other = call(
        join_kernel,
        (block(2),) * 6,
        [own, *swapped],
        "join",
        scratch=[pltpu.VMEM((2 * rows, width), jnp.bfloat16)],
    )
    got = [visit(x, *way) for x, way in zip(sent, out_visits)]
    near, pair = call(
        near_kernel,
        (block(4), wide(8, LANES)),
        [scale[None], shift[None], *got[2:]],
        "near",
        2,
        late,
    )
    one, two = block(1, jnp.int16), block(2, jnp.int16)
    parts = call(
        tile_kernel,
        (two, two, one, one, two),
        [pair, mine, other, *got[:2], swap(got[0]), swap(got[1]), near],
        "tile",
    )
    back = [visit(x, *way) for x, way in zip(parts, back_visits)]
    keep, kept_loss, give = call(
        add_kernel, (wide(rows, depth), wide(rows, LANES), one), [parts[4], back[0]], "add"
    )
    sums = call(
        more_kernel,
        (wide(2, rows, depth), wide(2, rows, LANES)) * 2,
        [keep, kept_loss, back[1], swap(give), *back[2:], image_emb, text_emb],
        "more",
        cost=late,
    )
    loss, grad_image, grad_text = call(
        functools.partial(final_kernel, n * rows),
        (wide(1, rows), wide(rows, depth), wide(rows, depth)),
        [*sums, swap(back[1])],
        "final",
    )
    return (loss[0], grad_image, grad_text)


def local(image_emb, text_emb, pair_class, scale, shift):
    if lax.axis_size("img") * lax.axis_size("txt") == 2 * 4 * 4 and lax.axis_size("txt") in (1, 2, 4):
        return chip_plan(image_emb, text_emb, pair_class, scale, shift)
    return tile_plan(image_emb, text_emb, pair_class, scale, shift)


def solution(mesh):
    in_specs = (P(AXES, None), P(AXES, None), P(AXES), P(), P())
    out_specs = (P(AXES), P(AXES, None), P(AXES, None))
    return jax.shard_map(local, mesh=mesh, in_specs=in_specs, out_specs=out_specs, check_vma=False)
```

```python
import functools

import jax
import jax.numpy as jnp
from jax import lax
from jax.experimental import pallas as pl
from jax.experimental.pallas import tpu as pltpu
from jax.sharding import PartitionSpec as P

AXES = ("img", "txt")
DIGITS = 4
LANES = 128
TOP = 32767.0


def unit_rows(rows):
    wide = rows.astype(jnp.float32)
    inverse = 1.0 / jnp.sqrt(jnp.sum(wide * wide, axis=1, keepdims=True) + 1e-06)
    return (wide * inverse, inverse)


def project_back(unit, inverse, pull):
    inner = jnp.sum(unit * pull, axis=1, keepdims=True)
    return (pull - unit * inner) * inverse


def tile_terms(rows_half, row_class, cols_half, col_class, scale, shift):
    logits = (
        scale
        * lax.dot_general(
            rows_half, cols_half, (((1,), (1,)), ((), ())), preferred_element_type=jnp.float32
        )
        + shift
    )
    sign = jnp.where(row_class[:, None] == col_class[None, :], 1.0, -1.0).astype(jnp.float32)
    margin = sign * logits
    loss_part = -jnp.sum(jax.nn.log_sigmoid(margin), axis=1)
    coef = (-sign * jax.nn.sigmoid(-margin) * scale).astype(jnp.bfloat16)
    return (coef, loss_part)


def tile_plan(image_emb, text_emb, pair_class, scale, shift):
    image_unit, image_inv = unit_rows(image_emb)
    text_unit, text_inv = unit_rows(text_emb)
    own_rows = text_emb.shape[0]
    pairs = own_rows * lax.axis_size("img") * lax.axis_size("txt")
    text_half = text_unit.astype(jnp.bfloat16)
    rows_half, row_class = (
        lax.all_gather(image_unit.astype(jnp.bfloat16), "txt", axis=0, tiled=True),
        lax.all_gather(pair_class, "txt", axis=0, tiled=True),
    )
    cols_half, col_class = (
        lax.all_gather(text_half, "img", axis=0, tiled=True),
        lax.all_gather(pair_class, "img", axis=0, tiled=True),
    )
    coef, loss_part = tile_terms(rows_half, row_class, cols_half, col_class, scale, shift)
    image_pull = jnp.dot(coef, cols_half, preferred_element_type=jnp.float32)
    text_pull = lax.psum_scatter(
        lax.dot_general(
            coef, rows_half, (((0,), (0,)), ((), ())), preferred_element_type=jnp.float32
        ),
        "img",
        scatter_dimension=0,
        tiled=True,
    )
    image_sum, loss_sum = (
        lax.psum_scatter(image_pull, "txt", scatter_dimension=0, tiled=True),
        lax.psum_scatter(loss_part, "txt", scatter_dimension=0, tiled=True),
    )
    row_loss = loss_sum / pairs
    grad_image = project_back(image_unit, image_inv, image_sum)
    grad_text = project_back(text_unit, text_inv, text_pull)
    return (row_loss, grad_image, grad_text)


def on_first_core():
    return lax.rem(lax.axis_index("img"), 2) == 0


def class_digits(classes):
    rows = classes.shape[1]
    across = jnp.broadcast_to(classes, (rows, rows))
    row = lax.broadcasted_iota(jnp.int32, (rows, rows), 0)
    column = lax.broadcasted_iota(jnp.int32, (rows, rows), 1)
    lane = lax.broadcasted_iota(jnp.int32, (rows, LANES), 1)
    digits = jnp.zeros((rows, LANES), jnp.float32)
    for k in range(DIGITS):
        byte = (lax.shift_right_logical(across, 8 * k) & 255).astype(jnp.float32)
        down = jnp.sum(jnp.where(row == column, byte, 0.0), axis=1, keepdims=True)
        digits = jnp.where(lane == k, down, digits)
    return digits.astype(jnp.bfloat16)


def digits_kernel(class_ref, digits_ref):
    digits_ref[...] = class_digits(class_ref[...][None, :])


def put_rows_of(image_ref, text_ref, digits, out_ref):
    rows, depth = image_ref.shape
    for start, source in ((0, image_ref), (rows, text_ref)):
        out_ref[start : start + rows, :depth] = unit_rows(source[...])[0].astype(jnp.bfloat16)
        out_ref[start : start + rows, depth:] = digits


def pack_kernel(image_ref, text_ref, digits_ref, both_ref, image_out, text_out):
    rows = image_ref.shape[0]
    put_rows_of(image_ref, text_ref, digits_ref[...], both_ref)
    image_out[...] = both_ref[:rows, :]
    text_out[...] = both_ref[rows:, :]


def join_kernel(own_ref, got_ref, *refs):
    first = on_first_core()
    rows = own_ref.shape[0] // 2
    own, got = own_ref[...].astype(jnp.float32), got_ref[...].astype(jnp.float32)
    low, high = jnp.where(first, own, got), jnp.where(first, got, own)
    images = jnp.concatenate([low[:rows], high[:rows]], axis=0)
    texts = jnp.concatenate([low[rows:], high[rows:]], axis=0)
    mine, other = jnp.where(first, images, texts), jnp.where(first, texts, images)
    for ref, block in zip(refs, (other, mine, mine, other)):
        ref[...] = block.astype(jnp.bfloat16)


def halves_kernel(image_ref, text_ref, out_ref):
    rows = image_ref.shape[0]
    out_ref[:rows, :] = image_ref[...]
    out_ref[rows:, :] = text_ref[...]


def pair_kernel(scale_ref, shift_ref, pair_ref):
    row = lax.broadcasted_iota(jnp.int32, pair_ref.shape, 0)
    pair_ref[...] = jnp.where(row == 0, scale_ref[0], shift_ref[0])


def power_above(size):
    return jnp.ceil(jnp.log2(jnp.maximum(size, 1e-30)) + 0.01)


def nearest(values):
    return jnp.floor(values + 0.5).astype(jnp.int32)


def code(values, power):
    return nearest(values * (TOP / jnp.exp2(power))).astype(jnp.int16)


def decode(steps, power):
    return steps.astype(jnp.int32).astype(jnp.float32) * (jnp.exp2(power) * (1.0 / TOP))


def put_rows(outs, pull, loss):
    blocks, (rows, width) = len(outs), outs[0].shape
    depth = width - LANES
    power = power_above(jnp.max(jnp.abs(pull), axis=1, keepdims=True))
    steps = code(pull, power)
    lane = lax.broadcasted_iota(jnp.int32, (blocks * rows, LANES), 1)
    loss_power = power_above(loss)
    tail = jnp.where(lane == 0, power, 0.0)
    tail = jnp.where(lane == 1, loss_power, tail)
    tail = jnp.where(lane == 2, loss * (TOP / jnp.exp2(loss_power)), tail)
    tail = nearest(tail).astype(jnp.int16)
    for k, out in enumerate(outs):
        out[:, :depth] = steps[k * rows : (k + 1) * rows]
        out[:, depth:] = tail[k * rows : (k + 1) * rows]


def tile_terms_of(lines, columns, scale, shift):
    depth = lines.shape[1] - LANES
    logits = (
        scale
        * lax.dot_general(
            lines[:, :depth],
            columns[:, :depth],
            (((1,), (1,)), ((), ())),
            preferred_element_type=jnp.float32,
        )
        + shift
    )
    pick = (
        lax.broadcasted_iota(jnp.int32, (8, LANES), 0)
        == lax.broadcasted_iota(jnp.int32, (8, LANES), 1)
    )
    column_digits = lax.dot_general(
        pick.astype(jnp.bfloat16),
        columns[:, depth:],
        (((1,), (1,)), ((), ())),
        preferred_element_type=jnp.float32,
    )
    line_digits = lines[:, depth:].astype(jnp.float32)
    same = None
    for k in range(DIGITS):
        equal = line_digits[:, k : k + 1] == column_digits[k : k + 1, :]
        same = equal if same is None else same & equal
    sign = jnp.where(same, 1.0, -1.0).astype(jnp.float32)
    margin = sign * logits
    small = jnp.exp(-jnp.abs(margin))
    over = 1.0 / (1.0 + small)
    coef = -sign * jnp.where(margin >= 0, small * over, over) * scale
    return jnp.log1p(small) - jnp.minimum(margin, 0.0), coef


def pulls_of(loss, coef, columns):
    depth = columns.shape[1] - LANES
    pull = jnp.dot(
        coef.astype(jnp.bfloat16), columns[:, :depth], preferred_element_type=jnp.float32
    )
    return pull, jnp.sum(loss, axis=1, keepdims=True)


def tile_kernel(pair_ref, mine_ref, other_ref, got_0, got_1, swapped_0, swapped_1, halves, other_halves, *outs):
    rows = mine_ref.shape[0]
    half = rows // 2
    first = on_first_core()
    scale, shift = pair_ref[0:1, 0:1], pair_ref[1:2, 0:1]

    def pick(one, two):
        return jnp.where(first, one, two)

    def parted(ref):
        image, text = ref[:half, :].astype(jnp.float32), ref[half:, :].astype(jnp.float32)
        return pick(image, text).astype(jnp.bfloat16), pick(text, image).astype(jnp.bfloat16)

    (line, column), (other_line, other_column) = parted(halves), parted(other_halves)
    lines = jnp.concatenate([got_1[...], mine_ref[...], line, other_line, swapped_0[...]], axis=0)
    columns = jnp.concatenate([got_0[...], column, other_column, swapped_1[...], other_ref[...]], axis=0)
    loss, coef = tile_terms_of(lines, columns, scale, shift)
    used = 2 * rows + half
    pull, loss_sum = pulls_of(loss[:used], coef[:used], columns)
    used = rows + half
    column_pull, column_loss = pulls_of(loss.T[:used], coef.T[:used], lines)
    put_rows([outs[0], outs[4]], pull[: 2 * rows], loss_sum[: 2 * rows])
    put_rows([outs[1]], column_pull[:rows], column_loss[:rows])
    line_half, column_half = (
        (x[start:], y[start:]) for x, y, start in ((pull, loss_sum, 2 * rows), (column_pull, column_loss, rows))
    )
    for out, (one, two) in zip(outs[2:4], ((line_half, column_half), (column_half, line_half))):
        put_rows([out], *(pick(x, y) for x, y in zip(one, two)))


def total(parts, rows, depth):
    pull = jnp.zeros((rows, depth), jnp.float32)
    loss = jnp.zeros((rows, 1), jnp.float32)
    for part in parts:
        tail = part[:, depth:].astype(jnp.int32).astype(jnp.float32)
        pull = pull + decode(part[:, :depth], tail[:, 0:1])
        loss = loss + tail[:, 2:3] * (jnp.exp2(tail[:, 1:2]) * (1.0 / TOP))
    return pull, loss


def place_of(first, rows):
    own = pl.multiple_of(jnp.where(first, 0, rows), rows)
    return pl.ds(own, rows), pl.ds(pl.multiple_of(rows - own, rows), rows)


def add_kernel(own_ref, back_ref, keep_ref, loss_ref, give_ref):
    rows, depth = keep_ref.shape
    own, other = place_of(on_first_core(), rows)
    pull, loss = total([own_ref[other, :], back_ref[other, :]], rows, depth)
    put_rows([give_ref], pull, loss)
    keep_ref[...], loss = total([own_ref[own, :], back_ref[own, :]], rows, depth)
    loss_ref[...] = jnp.broadcast_to(loss, loss_ref.shape)


def more_kernel(keep_ref, kept_loss_ref, back_ref, got_ref, image_back, text_back, image_ref, text_ref, *outs):
    sum_ref, sum_loss_ref, unit_ref, inverse_ref = outs
    first = on_first_core()
    rows, depth = keep_ref.shape
    own, _ = place_of(first, rows)
    mine = (keep_ref[...], kept_loss_ref[:, 0:1])
    other = total([back_ref[own, :], got_ref], rows, depth)
    for side, (one, two, back) in enumerate(((mine, other, image_back), (other, mine, text_back))):
        pull, loss = total([back], rows, depth)
        sum_ref[side] = pull + jnp.where(first, one[0], two[0])
        sum_loss_ref[side] = jnp.broadcast_to(
            loss + jnp.where(first, one[1], two[1]), sum_loss_ref.shape[1:]
        )
    for side, ref in enumerate((image_ref, text_ref)):
        unit, inverse = unit_rows(ref[...])
        unit_ref[side] = unit
        inverse_ref[side] = jnp.broadcast_to(inverse, inverse_ref.shape[1:])


def final_kernel(pairs, sum_ref, sum_loss_ref, unit_ref, inverse_ref, got_ref, *outs):
    loss_ref, grad_image_ref, grad_text_ref = outs
    first = on_first_core()
    rows, depth = sum_ref.shape[1:]
    own, _ = place_of(first, rows)
    pull, loss = total([got_ref[own, :]], rows, depth)
    image_pull = sum_ref[0] + jnp.where(first, pull, 0.0)
    text_pull = sum_ref[1] + jnp.where(first, 0.0, pull)
    grad_image_ref[...] = project_back(unit_ref[0], inverse_ref[0][:, 0:1], image_pull)
    grad_text_ref[...] = project_back(unit_ref[1], inverse_ref[1][:, 0:1], text_pull)
    row = lax.broadcasted_iota(jnp.int32, (rows, rows), 0)
    column = lax.broadcasted_iota(jnp.int32, (rows, rows), 1)
    loss = sum_loss_ref[0][:, 0:1] + jnp.where(first, loss, 0.0)
    across = jnp.where(row == column, loss / pairs, 0.0)
    loss_ref[...] = jnp.sum(across, axis=0, keepdims=True)


def chip_plan(image_emb, text_emb, pair_class, scale, shift):
    rows, depth = image_emb.shape
    width = depth + LANES
    lanes = lax.axis_size("txt")
    n = lax.axis_size("img") * lanes
    vmem = pl.BlockSpec(memory_space=pltpu.VMEM)
    smem = pl.BlockSpec(memory_space=pltpu.SMEM)

    def call(kernel, shapes, operands, name, scalars=0, cost=None, scratch=()):
        return pl.pallas_call(
            kernel,
            scratch_shapes=scratch,
            cost_estimate=cost,
            out_shape=shapes,
            in_specs=[smem] * scalars + [vmem] * (len(operands) - scalars),
            out_specs=jax.tree.map(lambda _: vmem, shapes),
            compiler_params=pltpu.CompilerParams(vmem_limit_bytes=32 << 20),
            name=name,
        )(*operands)

    def block(count, dtype=jnp.bfloat16):
        return jax.ShapeDtypeStruct((count * rows, width), dtype)

    def wide(*shape):
        return jax.ShapeDtypeStruct(shape, jnp.float32)

    def core(i):
        return i // lanes % 2

    def visit(x, masks):
        pairs = []
        for i in range(n):
            chip = (i // (2 * lanes) * lanes + i % lanes) ^ masks[core(i)]
            pairs.append((i, (chip // lanes * 2 + core(i)) * lanes + chip % lanes))
        return lax.ppermute(x, AXES, pairs)

    def swap(x):
        return lax.ppermute(x, AXES, [(i, i ^ lanes) for i in range(n)])

    across, beside, second, third = (12, 12), (1, 1), (2, 8), (4, 3)
    late = pl.CostEstimate(flops=10**9, bytes_accessed=10**7, transcendentals=0)
    digits = call(
        digits_kernel,
        jax.ShapeDtypeStruct((rows, LANES), jnp.bfloat16),
        [pair_class],
        "digits",
        cost=late,
    )
    own, own_images, own_texts = call(
        pack_kernel, (block(2), block(1), block(1)), [image_emb, text_emb, digits], "pack"
    )
    halves = [visit(own_images, across), visit(own_texts, beside)]
    halves = call(halves_kernel, block(2), halves, "halves", cost=late)
    *sent, mine, other = call(join_kernel, (block(2),) * 4, [own, swap(own)], "join")
    got = [visit(x, masks) for x, masks in zip(sent, (second, third))]
    pair = call(pair_kernel, wide(8, LANES), [scale[None], shift[None]], "pair", 2)
    one, two = block(1, jnp.int16), block(2, jnp.int16)
    parts = call(
        tile_kernel,
        (two, two, one, one, two),
        [pair, mine, other, *got, swap(got[0]), swap(got[1]), halves, swap(halves)],
        "tile",
    )
    back = [visit(x, masks) for x, masks in zip(parts, (third, second, across, beside))]
    keep, kept_loss, give = call(
        add_kernel, (wide(rows, depth), wide(rows, LANES), one), [parts[4], back[0]], "add"
    )
    sums = call(
        more_kernel,
        (wide(2, rows, depth), wide(2, rows, LANES)) * 2,
        [keep, kept_loss, back[1], swap(give), *back[2:], image_emb, text_emb],
        "more",
        cost=late,
    )
    loss, grad_image, grad_text = call(
        functools.partial(final_kernel, n * rows),
        (wide(1, rows), wide(rows, depth), wide(rows, depth)),
        [*sums, swap(back[1])],
        "final",
    )
    return (loss[0], grad_image, grad_text)


def local(image_emb, text_emb, pair_class, scale, shift):
    if lax.axis_size("img") * lax.axis_size("txt") == 2 * 4 * 4 and lax.axis_size("txt") in (1, 2, 4):
        return chip_plan(image_emb, text_emb, pair_class, scale, shift)
    return tile_plan(image_emb, text_emb, pair_class, scale, shift)


def solution(mesh):
    in_specs = (P(AXES, None), P(AXES, None), P(AXES), P(), P())
    out_specs = (P(AXES), P(AXES, None), P(AXES, None))
    return jax.shard_map(local, mesh=mesh, in_specs=in_specs, out_specs=out_specs, check_vma=False)
```

```python
import functools

import jax
import jax.numpy as jnp
from jax import lax
from jax.experimental import pallas as pl
from jax.experimental.pallas import tpu as pltpu
from jax.sharding import PartitionSpec as P

AXES = ("img", "txt")
DIGITS = 4
LANES = 128
TOP = 32767.0


def unit_rows(rows):
    wide = rows.astype(jnp.float32)
    inverse = 1.0 / jnp.sqrt(jnp.sum(wide * wide, axis=1, keepdims=True) + 1e-06)
    return (wide * inverse, inverse)


def project_back(unit, inverse, pull):
    inner = jnp.sum(unit * pull, axis=1, keepdims=True)
    return (pull - unit * inner) * inverse


def tile_terms(rows_half, row_class, cols_half, col_class, scale, shift):
    logits = (
        scale
        * lax.dot_general(
            rows_half, cols_half, (((1,), (1,)), ((), ())), preferred_element_type=jnp.float32
        )
        + shift
    )
    sign = jnp.where(row_class[:, None] == col_class[None, :], 1.0, -1.0).astype(jnp.float32)
    margin = sign * logits
    loss_part = -jnp.sum(jax.nn.log_sigmoid(margin), axis=1)
    coef = (-sign * jax.nn.sigmoid(-margin) * scale).astype(jnp.bfloat16)
    return (coef, loss_part)


def tile_plan(image_emb, text_emb, pair_class, scale, shift):
    image_unit, image_inv = unit_rows(image_emb)
    text_unit, text_inv = unit_rows(text_emb)
    own_rows = text_emb.shape[0]
    pairs = own_rows * lax.axis_size("img") * lax.axis_size("txt")
    text_half = text_unit.astype(jnp.bfloat16)
    rows_half, row_class = (
        lax.all_gather(image_unit.astype(jnp.bfloat16), "txt", axis=0, tiled=True),
        lax.all_gather(pair_class, "txt", axis=0, tiled=True),
    )
    cols_half, col_class = (
        lax.all_gather(text_half, "img", axis=0, tiled=True),
        lax.all_gather(pair_class, "img", axis=0, tiled=True),
    )
    coef, loss_part = tile_terms(rows_half, row_class, cols_half, col_class, scale, shift)
    image_pull = jnp.dot(coef, cols_half, preferred_element_type=jnp.float32)
    text_pull = lax.psum_scatter(
        lax.dot_general(
            coef, rows_half, (((0,), (0,)), ((), ())), preferred_element_type=jnp.float32
        ),
        "img",
        scatter_dimension=0,
        tiled=True,
    )
    image_sum, loss_sum = (
        lax.psum_scatter(image_pull, "txt", scatter_dimension=0, tiled=True),
        lax.psum_scatter(loss_part, "txt", scatter_dimension=0, tiled=True),
    )
    row_loss = loss_sum / pairs
    grad_image = project_back(image_unit, image_inv, image_sum)
    grad_text = project_back(text_unit, text_inv, text_pull)
    return (row_loss, grad_image, grad_text)


def on_first_core():
    return lax.rem(lax.axis_index("img"), 2) == 0


def class_digits(classes):
    rows = classes.shape[1]
    across = jnp.broadcast_to(classes, (rows, rows))
    row = lax.broadcasted_iota(jnp.int32, (rows, rows), 0)
    column = lax.broadcasted_iota(jnp.int32, (rows, rows), 1)
    lane = lax.broadcasted_iota(jnp.int32, (rows, LANES), 1)
    digits = jnp.zeros((rows, LANES), jnp.float32)
    for k in range(DIGITS):
        byte = (lax.shift_right_logical(across, 8 * k) & 255).astype(jnp.float32)
        down = jnp.sum(jnp.where(row == column, byte, 0.0), axis=1, keepdims=True)
        digits = jnp.where(lane == k, down, digits)
    return digits.astype(jnp.bfloat16)


def digits_kernel(class_ref, digits_ref):
    digits_ref[...] = class_digits(class_ref[...][None, :])


def put_rows_of(image_ref, text_ref, digits, out_ref):
    rows, depth = image_ref.shape
    for start, source in ((0, image_ref), (rows, text_ref)):
        out_ref[start : start + rows, :depth] = unit_rows(source[...])[0].astype(jnp.bfloat16)
        out_ref[start : start + rows, depth:] = digits


def pack_kernel(image_ref, text_ref, digits_ref, out_ref):
    put_rows_of(image_ref, text_ref, digits_ref[...], out_ref)


def join_kernel(own_ref, got_image, got_text, got_class, *refs):
    *refs, got_ref = refs
    put_rows_of(got_image, got_text, class_digits(got_class[...][None, :]), got_ref)
    first = on_first_core()
    rows = own_ref.shape[0] // 2
    own, got = own_ref[...].astype(jnp.float32), got_ref[...].astype(jnp.float32)
    low, high = jnp.where(first, own, got), jnp.where(first, got, own)
    images = jnp.concatenate([low[:rows], high[:rows]], axis=0)
    texts = jnp.concatenate([low[rows:], high[rows:]], axis=0)
    mine, other = jnp.where(first, images, texts), jnp.where(first, texts, images)
    for ref, block in zip(refs, (images, texts, mine, mine, mine, other)):
        ref[...] = block.astype(jnp.bfloat16)


def far_kernel(upper_ref, lower_ref, out_ref):
    rows = upper_ref.shape[0]
    out_ref[:rows, :] = upper_ref[...]
    out_ref[rows:, :] = lower_ref[...]


def near_kernel(scale_ref, shift_ref, upper_ref, lower_ref, out_ref, pair_ref):
    rows = upper_ref.shape[0]
    out_ref[:rows, :] = upper_ref[...]
    out_ref[rows:, :] = lower_ref[...]
    row = lax.broadcasted_iota(jnp.int32, pair_ref.shape, 0)
    pair_ref[...] = jnp.where(row == 0, scale_ref[0], shift_ref[0])


def power_above(size):
    return jnp.ceil(jnp.log2(jnp.maximum(size, 1e-30)) + 0.01)


def nearest(values):
    return jnp.floor(values + 0.5).astype(jnp.int32)


def code(values, power):
    return nearest(values * (TOP / jnp.exp2(power))).astype(jnp.int16)


def decode(steps, power):
    return steps.astype(jnp.int32).astype(jnp.float32) * (jnp.exp2(power) * (1.0 / TOP))


def put_rows(outs, pull, loss):
    blocks, (rows, width) = len(outs), outs[0].shape
    depth = width - LANES
    power = power_above(jnp.max(jnp.abs(pull), axis=1, keepdims=True))
    steps = code(pull, power)
    lane = lax.broadcasted_iota(jnp.int32, (blocks * rows, LANES), 1)
    loss_power = power_above(loss)
    tail = jnp.where(lane == 0, power, 0.0)
    tail = jnp.where(lane == 1, loss_power, tail)
    tail = jnp.where(lane == 2, loss * (TOP / jnp.exp2(loss_power)), tail)
    tail = nearest(tail).astype(jnp.int16)
    for k, out in enumerate(outs):
        out[:, :depth] = steps[k * rows : (k + 1) * rows]
        out[:, depth:] = tail[k * rows : (k + 1) * rows]


def tile_terms_of(lines, columns, scale, shift):
    depth = lines.shape[1] - LANES
    logits = (
        scale
        * lax.dot_general(
            lines[:, :depth],
            columns[:, :depth],
            (((1,), (1,)), ((), ())),
            preferred_element_type=jnp.float32,
        )
        + shift
    )
    pick = (
        lax.broadcasted_iota(jnp.int32, (8, LANES), 0)
        == lax.broadcasted_iota(jnp.int32, (8, LANES), 1)
    )
    column_digits = lax.dot_general(
        pick.astype(jnp.bfloat16),
        columns[:, depth:],
        (((1,), (1,)), ((), ())),
        preferred_element_type=jnp.float32,
    )
    line_digits = lines[:, depth:].astype(jnp.float32)
    same = None
    for k in range(DIGITS):
        equal = line_digits[:, k : k + 1] == column_digits[k : k + 1, :]
        same = equal if same is None else same & equal
    sign = jnp.where(same, 1.0, -1.0).astype(jnp.float32)
    margin = sign * logits
    small = jnp.exp(-jnp.abs(margin))
    over = 1.0 / (1.0 + small)
    coef = -sign * jnp.where(margin >= 0, small * over, over) * scale
    return jnp.log1p(small) - jnp.minimum(margin, 0.0), coef


def pulls_of(loss, coef, columns):
    depth = columns.shape[1] - LANES
    pull = jnp.dot(
        coef.astype(jnp.bfloat16), columns[:, :depth], preferred_element_type=jnp.float32
    )
    return pull, jnp.sum(loss, axis=1, keepdims=True)


def tile_kernel(pair_ref, mine_ref, other_ref, far_ref, swapped_ref, near_ref, *outs):
    rows = mine_ref.shape[0]
    first = on_first_core()
    scale, shift = pair_ref[0:1, 0:1], pair_ref[1:2, 0:1]

    def pick(one, two):
        return jnp.where(first, one, two)

    def parted(ref):
        image, text = ref[:rows, :].astype(jnp.float32), ref[rows:, :].astype(jnp.float32)
        return pick(image, text).astype(jnp.bfloat16), pick(text, image).astype(jnp.bfloat16)

    (line, column), (other_line, other_column) = parted(far_ref), parted(swapped_ref)
    lines = jnp.concatenate([line, near_ref[:rows, :], mine_ref[...], other_line], axis=0)
    columns = jnp.concatenate([column, other_column, near_ref[rows:, :], other_ref[...]], axis=0)
    loss, coef = tile_terms_of(lines, columns, scale, shift)
    pull, loss_sum = pulls_of(loss[: 3 * rows], coef[: 3 * rows], columns)
    put_rows([outs[0]], pull[:rows], loss_sum[:rows])
    put_rows([outs[1]], *pulls_of(loss.T[:rows], coef.T[:rows], lines))
    half = rows // 2
    halves = []
    for part in (pull, loss_sum):
        low, high = part[rows : rows + half], part[rows + half : 2 * rows]
        halves.append((pick(low, high), pick(high, low)))
    for out, part, part_loss in zip(outs[2:4], *halves):
        put_rows([out], part, part_loss)
    put_rows([outs[4]], pull[2 * rows :], loss_sum[2 * rows :])


def total(parts, rows, depth):
    pull = jnp.zeros((rows, depth), jnp.float32)
    loss = jnp.zeros((rows, 1), jnp.float32)
    for part in parts:
        tail = part[:, depth:].astype(jnp.int32).astype(jnp.float32)
        pull = pull + decode(part[:, :depth], tail[:, 0:1])
        loss = loss + tail[:, 2:3] * (jnp.exp2(tail[:, 1:2]) * (1.0 / TOP))
    return pull, loss


def place_of(first, rows):
    own = pl.multiple_of(jnp.where(first, 0, rows), rows)
    return pl.ds(own, rows), pl.ds(pl.multiple_of(rows - own, rows), rows)


def add_kernel(own_ref, back_ref, keep_ref, loss_ref, give_ref):
    rows, depth = keep_ref.shape
    own, other = place_of(on_first_core(), rows)
    pull, loss = total([own_ref[other, :], back_ref[other, :]], rows, depth)
    put_rows([give_ref], pull, loss)
    keep_ref[...], loss = total([own_ref[own, :], back_ref[own, :]], rows, depth)
    loss_ref[...] = jnp.broadcast_to(loss, loss_ref.shape)


def more_kernel(keep_ref, kept_loss_ref, back_ref, got_ref, same_ref, cross_ref, image_ref, text_ref, *outs):
    sum_ref, sum_loss_ref, unit_ref, inverse_ref = outs
    rows, depth = keep_ref.shape
    own, _ = place_of(on_first_core(), rows)
    pull, loss = total([same_ref], rows, depth)
    sum_ref[0] = keep_ref[...] + pull
    sum_loss_ref[0] = kept_loss_ref[...] + loss
    sum_ref[1], loss = total([back_ref[own, :], got_ref, cross_ref], rows, depth)
    sum_loss_ref[1] = jnp.broadcast_to(loss, sum_loss_ref.shape[1:])
    for side, ref in enumerate((image_ref, text_ref)):
        unit, inverse = unit_rows(ref[...])
        unit_ref[side] = unit
        inverse_ref[side] = jnp.broadcast_to(inverse, inverse_ref.shape[1:])


def final_kernel(pairs, sum_ref, sum_loss_ref, unit_ref, inverse_ref, got_ref, loss_ref, grad_image_ref, grad_text_ref):
    first = on_first_core()
    rows, depth = sum_ref.shape[1:]
    own, _ = place_of(first, rows)
    pull, loss = total([got_ref[own, :]], rows, depth)
    pulls = (sum_ref[0] + pull, sum_ref[1])
    losses = (sum_loss_ref[0][:, 0:1] + loss, sum_loss_ref[1][:, 0:1])
    for side, (pull, out) in enumerate(
        (
            (jnp.where(first, pulls[0], pulls[1]), grad_image_ref),
            (jnp.where(first, pulls[1], pulls[0]), grad_text_ref),
        )
    ):
        out[...] = project_back(unit_ref[side], inverse_ref[side][:, 0:1], pull)
    row = lax.broadcasted_iota(jnp.int32, (rows, rows), 0)
    column = lax.broadcasted_iota(jnp.int32, (rows, rows), 1)
    loss = jnp.where(first, losses[0], losses[1])
    across = jnp.where(row == column, loss / pairs, 0.0)
    loss_ref[...] = jnp.sum(across, axis=0, keepdims=True)


def chip_plan(image_emb, text_emb, pair_class, scale, shift):
    rows, depth = image_emb.shape
    width = depth + LANES
    lanes = lax.axis_size("txt")
    n = lax.axis_size("img") * lanes
    vmem = pl.BlockSpec(memory_space=pltpu.VMEM)
    smem = pl.BlockSpec(memory_space=pltpu.SMEM)

    def call(kernel, shapes, operands, name, scalars=0, cost=None, scratch=()):
        return pl.pallas_call(
            kernel,
            scratch_shapes=scratch,
            cost_estimate=cost,
            out_shape=shapes,
            in_specs=[smem] * scalars + [vmem] * (len(operands) - scalars),
            out_specs=jax.tree.map(lambda _: vmem, shapes),
            compiler_params=pltpu.CompilerParams(vmem_limit_bytes=32 << 20),
            name=name,
        )(*operands)

    def block(count, dtype=jnp.bfloat16):
        return jax.ShapeDtypeStruct((count * rows, width), dtype)

    def wide(*shape):
        return jax.ShapeDtypeStruct(shape, jnp.float32)

    def core(i):
        return i // lanes % 2

    def visit(x, masks, cross):
        pairs = []
        for i in range(n):
            chip = (i // (2 * lanes) * lanes + i % lanes) ^ masks[core(i)]
            pairs.append((i, (chip // lanes * 2 + (core(i) ^ cross)) * lanes + chip % lanes))
        return lax.ppermute(x, AXES, pairs)

    def swap(x):
        return lax.ppermute(x, AXES, [(i, i ^ lanes) for i in range(n)])

    out_visits = (((12, 8), 0), ((2, 3), 0), ((4, 1), 0), ((4, 1), 1))
    back_visits = (((12, 3), 0), ((2, 8), 0), ((4, 1), 0), ((4, 1), 1))
    late = pl.CostEstimate(flops=10**9, bytes_accessed=10**7, transcendentals=0)
    digits = call(
        digits_kernel,
        jax.ShapeDtypeStruct((rows, LANES), jnp.bfloat16),
        [pair_class],
        "digits",
        cost=late,
    )
    own = call(pack_kernel, block(2), [image_emb, text_emb, digits], "pack")
    swapped = [swap(x) for x in (image_emb, text_emb, pair_class)]
    *sent, mine, other = call(
        join_kernel,
        (block(2),) * 6,
        [own, *swapped],
        "join",
        scratch=[pltpu.VMEM((2 * rows, width), jnp.bfloat16)],
    )
    got = [visit(x, *way) for x, way in zip(sent, out_visits)]
    far = call(far_kernel, block(4), got[:2], "far")
    near, pair = call(
        near_kernel,
        (block(4), wide(8, LANES)),
        [scale[None], shift[None], *got[2:]],
        "near",
        2,
        late,
    )
    one, two = block(1, jnp.int16), block(2, jnp.int16)
    parts = call(
        tile_kernel,
        (two, two, one, one, two),
        [pair, mine, other, far, swap(far), near],
        "tile",
    )
    back = [visit(x, *way) for x, way in zip(parts, back_visits)]
    keep, kept_loss, give = call(
        add_kernel, (wide(rows, depth), wide(rows, LANES), one), [parts[4], back[0]], "add"
    )
    sums = call(
        more_kernel,
        (wide(2, rows, depth), wide(2, rows, LANES)) * 2,
        [keep, kept_loss, back[1], swap(give), *back[2:], image_emb, text_emb],
        "more",
        cost=late,
    )
    loss, grad_image, grad_text = call(
        functools.partial(final_kernel, n * rows),
        (wide(1, rows), wide(rows, depth), wide(rows, depth)),
        [*sums, swap(back[1])],
        "final",
    )
    return (loss[0], grad_image, grad_text)


def local(image_emb, text_emb, pair_class, scale, shift):
    if lax.axis_size("img") * lax.axis_size("txt") == 2 * 4 * 4 and lax.axis_size("txt") in (1, 2, 4):
        return chip_plan(image_emb, text_emb, pair_class, scale, shift)
    return tile_plan(image_emb, text_emb, pair_class, scale, shift)


def solution(mesh):
    in_specs = (P(AXES, None), P(AXES, None), P(AXES), P(), P())
    out_specs = (P(AXES), P(AXES, None), P(AXES, None))
    return jax.shard_map(local, mesh=mesh, in_specs=in_specs, out_specs=out_specs, check_vma=False)
```

```python
import functools

import jax
import jax.numpy as jnp
from jax import lax
from jax.experimental import pallas as pl
from jax.experimental.pallas import tpu as pltpu
from jax.sharding import PartitionSpec as P

AXES = ("img", "txt")
DIGITS = 4
LANES = 128
TOP = 32767.0


def unit_rows(rows):
    wide = rows.astype(jnp.float32)
    inverse = 1.0 / jnp.sqrt(jnp.sum(wide * wide, axis=1, keepdims=True) + 1e-06)
    return (wide * inverse, inverse)


def project_back(unit, inverse, pull):
    inner = jnp.sum(unit * pull, axis=1, keepdims=True)
    return (pull - unit * inner) * inverse


def tile_terms(rows_half, row_class, cols_half, col_class, scale, shift):
    logits = (
        scale
        * lax.dot_general(
            rows_half, cols_half, (((1,), (1,)), ((), ())), preferred_element_type=jnp.float32
        )
        + shift
    )
    sign = jnp.where(row_class[:, None] == col_class[None, :], 1.0, -1.0).astype(jnp.float32)
    margin = sign * logits
    loss_part = -jnp.sum(jax.nn.log_sigmoid(margin), axis=1)
    coef = (-sign * jax.nn.sigmoid(-margin) * scale).astype(jnp.bfloat16)
    return (coef, loss_part)


def tile_plan(image_emb, text_emb, pair_class, scale, shift):
    image_unit, image_inv = unit_rows(image_emb)
    text_unit, text_inv = unit_rows(text_emb)
    own_rows = text_emb.shape[0]
    pairs = own_rows * lax.axis_size("img") * lax.axis_size("txt")
    text_half = text_unit.astype(jnp.bfloat16)
    rows_half, row_class = (
        lax.all_gather(image_unit.astype(jnp.bfloat16), "txt", axis=0, tiled=True),
        lax.all_gather(pair_class, "txt", axis=0, tiled=True),
    )
    cols_half, col_class = (
        lax.all_gather(text_half, "img", axis=0, tiled=True),
        lax.all_gather(pair_class, "img", axis=0, tiled=True),
    )
    coef, loss_part = tile_terms(rows_half, row_class, cols_half, col_class, scale, shift)
    image_pull = jnp.dot(coef, cols_half, preferred_element_type=jnp.float32)
    text_pull = lax.psum_scatter(
        lax.dot_general(
            coef, rows_half, (((0,), (0,)), ((), ())), preferred_element_type=jnp.float32
        ),
        "img",
        scatter_dimension=0,
        tiled=True,
    )
    image_sum, loss_sum = (
        lax.psum_scatter(image_pull, "txt", scatter_dimension=0, tiled=True),
        lax.psum_scatter(loss_part, "txt", scatter_dimension=0, tiled=True),
    )
    row_loss = loss_sum / pairs
    grad_image = project_back(image_unit, image_inv, image_sum)
    grad_text = project_back(text_unit, text_inv, text_pull)
    return (row_loss, grad_image, grad_text)


def on_first_core():
    return lax.rem(lax.axis_index("img"), 2) == 0


def class_digits(classes):
    rows = classes.shape[1]
    across = jnp.broadcast_to(classes, (rows, rows))
    row = lax.broadcasted_iota(jnp.int32, (rows, rows), 0)
    column = lax.broadcasted_iota(jnp.int32, (rows, rows), 1)
    lane = lax.broadcasted_iota(jnp.int32, (rows, LANES), 1)
    digits = jnp.zeros((rows, LANES), jnp.float32)
    for k in range(DIGITS):
        byte = (lax.shift_right_logical(across, 8 * k) & 255).astype(jnp.float32)
        down = jnp.sum(jnp.where(row == column, byte, 0.0), axis=1, keepdims=True)
        digits = jnp.where(lane == k, down, digits)
    return digits.astype(jnp.bfloat16)


def digits_kernel(class_ref, digits_ref):
    digits_ref[...] = class_digits(class_ref[...][None, :])


def put_rows_of(image_ref, text_ref, digits, out_ref):
    rows, depth = image_ref.shape
    for start, source in ((0, image_ref), (rows, text_ref)):
        out_ref[start : start + rows, :depth] = unit_rows(source[...])[0].astype(jnp.bfloat16)
        out_ref[start : start + rows, depth:] = digits


def pack_kernel(image_ref, text_ref, digits_ref, out_ref):
    put_rows_of(image_ref, text_ref, digits_ref[...], out_ref)


def join_kernel(own_ref, got_image, got_text, got_class, *refs):
    *refs, got_ref = refs
    put_rows_of(got_image, got_text, class_digits(got_class[...][None, :]), got_ref)
    first = on_first_core()
    rows = own_ref.shape[0] // 2
    own, got = own_ref[...].astype(jnp.float32), got_ref[...].astype(jnp.float32)
    low, high = jnp.where(first, own, got), jnp.where(first, got, own)
    images = jnp.concatenate([low[:rows], high[:rows]], axis=0)
    texts = jnp.concatenate([low[rows:], high[rows:]], axis=0)
    mine, other = jnp.where(first, images, texts), jnp.where(first, texts, images)
    for ref, block in zip(refs, (images, texts, mine, mine, mine, other)):
        ref[...] = block.astype(jnp.bfloat16)


def near_kernel(upper_ref, lower_ref, out_ref):
    rows = upper_ref.shape[0]
    out_ref[:rows, :] = upper_ref[...]
    out_ref[rows:, :] = lower_ref[...]


def far_kernel(scale_ref, shift_ref, upper_ref, lower_ref, out_ref, pair_ref):
    near_kernel(upper_ref, lower_ref, out_ref)
    row = lax.broadcasted_iota(jnp.int32, pair_ref.shape, 0)
    pair_ref[...] = jnp.where(row == 0, scale_ref[0], shift_ref[0])


def power_above(size):
    return jnp.ceil(jnp.log2(jnp.maximum(size, 1e-30)) + 0.01)


def nearest(values):
    return jnp.floor(values + 0.5).astype(jnp.int32)


def code(values, power):
    return nearest(values * (TOP / jnp.exp2(power))).astype(jnp.int16)


def decode(steps, power):
    return steps.astype(jnp.int32).astype(jnp.float32) * (jnp.exp2(power) * (1.0 / TOP))


def put_rows(outs, pull, loss):
    blocks, (rows, width) = len(outs), outs[0].shape
    depth = width - LANES
    power = power_above(jnp.max(jnp.abs(pull), axis=1, keepdims=True))
    steps = code(pull, power)
    lane = lax.broadcasted_iota(jnp.int32, (blocks * rows, LANES), 1)
    loss_power = power_above(loss)
    tail = jnp.where(lane == 0, power, 0.0)
    tail = jnp.where(lane == 1, loss_power, tail)
    tail = jnp.where(lane == 2, loss * (TOP / jnp.exp2(loss_power)), tail)
    tail = nearest(tail).astype(jnp.int16)
    for k, out in enumerate(outs):
        out[:, :depth] = steps[k * rows : (k + 1) * rows]
        out[:, depth:] = tail[k * rows : (k + 1) * rows]


def tile_terms_of(lines, columns, scale, shift):
    depth = lines.shape[1] - LANES
    logits = (
        scale
        * lax.dot_general(
            lines[:, :depth],
            columns[:, :depth],
            (((1,), (1,)), ((), ())),
            preferred_element_type=jnp.float32,
        )
        + shift
    )
    pick = (
        lax.broadcasted_iota(jnp.int32, (8, LANES), 0)
        == lax.broadcasted_iota(jnp.int32, (8, LANES), 1)
    )
    column_digits = lax.dot_general(
        pick.astype(jnp.bfloat16),
        columns[:, depth:],
        (((1,), (1,)), ((), ())),
        preferred_element_type=jnp.float32,
    )
    line_digits = lines[:, depth:].astype(jnp.float32)
    same = None
    for k in range(DIGITS):
        equal = line_digits[:, k : k + 1] == column_digits[k : k + 1, :]
        same = equal if same is None else same & equal
    sign = jnp.where(same, 1.0, -1.0).astype(jnp.float32)
    margin = sign * logits
    small = jnp.exp(-jnp.abs(margin))
    over = 1.0 / (1.0 + small)
    coef = -sign * jnp.where(margin >= 0, small * over, over) * scale
    return jnp.log1p(small) - jnp.minimum(margin, 0.0), coef


def pulls_of(loss, coef, columns):
    depth = columns.shape[1] - LANES
    pull = jnp.dot(
        coef.astype(jnp.bfloat16), columns[:, :depth], preferred_element_type=jnp.float32
    )
    return pull, jnp.sum(loss, axis=1, keepdims=True)


def tile_kernel(pair_ref, mine_ref, other_ref, far_ref, swapped_ref, near_ref, *outs):
    rows = mine_ref.shape[0]
    first = on_first_core()
    scale, shift = pair_ref[0:1, 0:1], pair_ref[1:2, 0:1]

    def pick(one, two):
        return jnp.where(first, one, two)

    def parted(ref):
        image, text = ref[:rows, :].astype(jnp.float32), ref[rows:, :].astype(jnp.float32)
        return pick(image, text).astype(jnp.bfloat16), pick(text, image).astype(jnp.bfloat16)

    (line, column), (other_line, other_column) = parted(far_ref), parted(swapped_ref)
    lines = jnp.concatenate([line, near_ref[:rows, :], mine_ref[...], other_line], axis=0)
    columns = jnp.concatenate([column, other_column, near_ref[rows:, :], other_ref[...]], axis=0)
    loss, coef = tile_terms_of(lines, columns, scale, shift)
    pull, loss_sum = pulls_of(loss[: 3 * rows], coef[: 3 * rows], columns)
    put_rows([outs[0]], pull[:rows], loss_sum[:rows])
    put_rows([outs[1]], *pulls_of(loss.T[:rows], coef.T[:rows], lines))
    half = rows // 2
    halves = []
    for part in (pull, loss_sum):
        low, high = part[rows : rows + half], part[rows + half : 2 * rows]
        halves.append((pick(low, high), pick(high, low)))
    for out, part, part_loss in zip(outs[2:4], *halves):
        put_rows([out], part, part_loss)
    put_rows([outs[4]], pull[2 * rows :], loss_sum[2 * rows :])


def total(parts, rows, depth):
    pull = jnp.zeros((rows, depth), jnp.float32)
    loss = jnp.zeros((rows, 1), jnp.float32)
    for part in parts:
        tail = part[:, depth:].astype(jnp.int32).astype(jnp.float32)
        pull = pull + decode(part[:, :depth], tail[:, 0:1])
        loss = loss + tail[:, 2:3] * (jnp.exp2(tail[:, 1:2]) * (1.0 / TOP))
    return pull, loss


def place_of(first, rows):
    own = pl.multiple_of(jnp.where(first, 0, rows), rows)
    return pl.ds(own, rows), pl.ds(pl.multiple_of(rows - own, rows), rows)


def add_kernel(own_ref, back_ref, keep_ref, loss_ref, give_ref):
    rows, depth = keep_ref.shape
    own, other = place_of(on_first_core(), rows)
    pull, loss = total([own_ref[other, :], back_ref[other, :]], rows, depth)
    put_rows([give_ref], pull, loss)
    keep_ref[...], loss = total([own_ref[own, :], back_ref[own, :]], rows, depth)
    loss_ref[...] = jnp.broadcast_to(loss, loss_ref.shape)


def more_kernel(keep_ref, kept_loss_ref, back_ref, got_ref, same_ref, cross_ref, image_ref, text_ref, *outs):
    sum_ref, sum_loss_ref, unit_ref, inverse_ref = outs
    rows, depth = keep_ref.shape
    own, _ = place_of(on_first_core(), rows)
    pull, loss = total([same_ref], rows, depth)
    sum_ref[0] = keep_ref[...] + pull
    sum_loss_ref[0] = kept_loss_ref[...] + loss
    sum_ref[1], loss = total([back_ref[own, :], got_ref, cross_ref], rows, depth)
    sum_loss_ref[1] = jnp.broadcast_to(loss, sum_loss_ref.shape[1:])
    for side, ref in enumerate((image_ref, text_ref)):
        unit, inverse = unit_rows(ref[...])
        unit_ref[side] = unit
        inverse_ref[side] = jnp.broadcast_to(inverse, inverse_ref.shape[1:])


def final_kernel(pairs, sum_ref, sum_loss_ref, unit_ref, inverse_ref, got_ref, loss_ref, grad_image_ref, grad_text_ref):
    first = on_first_core()
    rows, depth = sum_ref.shape[1:]
    own, _ = place_of(first, rows)
    pull, loss = total([got_ref[own, :]], rows, depth)
    pulls = (sum_ref[0] + pull, sum_ref[1])
    losses = (sum_loss_ref[0][:, 0:1] + loss, sum_loss_ref[1][:, 0:1])
    for side, (pull, out) in enumerate(
        (
            (jnp.where(first, pulls[0], pulls[1]), grad_image_ref),
            (jnp.where(first, pulls[1], pulls[0]), grad_text_ref),
        )
    ):
        out[...] = project_back(unit_ref[side], inverse_ref[side][:, 0:1], pull)
    row = lax.broadcasted_iota(jnp.int32, (rows, rows), 0)
    column = lax.broadcasted_iota(jnp.int32, (rows, rows), 1)
    loss = jnp.where(first, losses[0], losses[1])
    across = jnp.where(row == column, loss / pairs, 0.0)
    loss_ref[...] = jnp.sum(across, axis=0, keepdims=True)


def chip_plan(image_emb, text_emb, pair_class, scale, shift):
    rows, depth = image_emb.shape
    width = depth + LANES
    lanes = lax.axis_size("txt")
    n = lax.axis_size("img") * lanes
    vmem = pl.BlockSpec(memory_space=pltpu.VMEM)
    smem = pl.BlockSpec(memory_space=pltpu.SMEM)

    def call(kernel, shapes, operands, name, scalars=0, cost=None, scratch=()):
        return pl.pallas_call(
            kernel,
            scratch_shapes=scratch,
            cost_estimate=cost,
            out_shape=shapes,
            in_specs=[smem] * scalars + [vmem] * (len(operands) - scalars),
            out_specs=jax.tree.map(lambda _: vmem, shapes),
            compiler_params=pltpu.CompilerParams(vmem_limit_bytes=32 << 20),
            name=name,
        )(*operands)

    def block(count, dtype=jnp.bfloat16):
        return jax.ShapeDtypeStruct((count * rows, width), dtype)

    def wide(*shape):
        return jax.ShapeDtypeStruct(shape, jnp.float32)

    def core(i):
        return i // lanes % 2

    def visit(x, masks, cross):
        pairs = []
        for i in range(n):
            chip = (i // (2 * lanes) * lanes + i % lanes) ^ masks[core(i)]
            pairs.append((i, (chip // lanes * 2 + (core(i) ^ cross)) * lanes + chip % lanes))
        return lax.ppermute(x, AXES, pairs)

    def swap(x):
        return lax.ppermute(x, AXES, [(i, i ^ lanes) for i in range(n)])

    out_visits = (((12, 8), 0), ((2, 3), 0), ((4, 1), 0), ((4, 1), 1))
    back_visits = (((12, 3), 0), ((2, 8), 0), ((4, 1), 0), ((4, 1), 1))
    late = pl.CostEstimate(flops=10**9, bytes_accessed=10**7, transcendentals=0)
    digits = call(
        digits_kernel,
        jax.ShapeDtypeStruct((rows, LANES), jnp.bfloat16),
        [pair_class],
        "digits",
        cost=late,
    )
    own = call(pack_kernel, block(2), [image_emb, text_emb, digits], "pack")
    swapped = [swap(x) for x in (image_emb, text_emb, pair_class)]
    *sent, mine, other = call(
        join_kernel,
        (block(2),) * 6,
        [own, *swapped],
        "join",
        scratch=[pltpu.VMEM((2 * rows, width), jnp.bfloat16)],
    )
    got = [visit(x, *way) for x, way in zip(sent, out_visits)]
    far, pair = call(
        far_kernel, (block(4), wide(8, LANES)), [scale[None], shift[None], *got[:2]], "far", 2
    )
    near = call(near_kernel, block(4), got[2:], "near", cost=late)
    one, two = block(1, jnp.int16), block(2, jnp.int16)
    parts = call(
        tile_kernel,
        (two, two, one, one, two),
        [pair, mine, other, far, swap(far), near],
        "tile",
    )
    back = [visit(x, *way) for x, way in zip(parts, back_visits)]
    keep, kept_loss, give = call(
        add_kernel, (wide(rows, depth), wide(rows, LANES), one), [parts[4], back[0]], "add"
    )
    sums = call(
        more_kernel,
        (wide(2, rows, depth), wide(2, rows, LANES)) * 2,
        [keep, kept_loss, back[1], swap(give), *back[2:], image_emb, text_emb],
        "more",
        cost=late,
    )
    loss, grad_image, grad_text = call(
        functools.partial(final_kernel, n * rows),
        (wide(1, rows), wide(rows, depth), wide(rows, depth)),
        [*sums, swap(back[1])],
        "final",
    )
    return (loss[0], grad_image, grad_text)


def local(image_emb, text_emb, pair_class, scale, shift):
    if lax.axis_size("img") * lax.axis_size("txt") == 2 * 4 * 4 and lax.axis_size("txt") in (1, 2, 4):
        return chip_plan(image_emb, text_emb, pair_class, scale, shift)
    return tile_plan(image_emb, text_emb, pair_class, scale, shift)


def solution(mesh):
    in_specs = (P(AXES, None), P(AXES, None), P(AXES), P(), P())
    out_specs = (P(AXES), P(AXES, None), P(AXES, None))
    return jax.shard_map(local, mesh=mesh, in_specs=in_specs, out_specs=out_specs, check_vma=False)
```

```python
import functools

import jax
import jax.numpy as jnp
from jax import lax
from jax.experimental import pallas as pl
from jax.experimental.pallas import tpu as pltpu
from jax.sharding import PartitionSpec as P

AXES = ("img", "txt")
DIGITS = 4
LANES = 128
TOP = 32767.0


def unit_rows(rows):
    wide = rows.astype(jnp.float32)
    inverse = 1.0 / jnp.sqrt(jnp.sum(wide * wide, axis=1, keepdims=True) + 1e-06)
    return (wide * inverse, inverse)


def project_back(unit, inverse, pull):
    inner = jnp.sum(unit * pull, axis=1, keepdims=True)
    return (pull - unit * inner) * inverse


def tile_terms(rows_half, row_class, cols_half, col_class, scale, shift):
    logits = (
        scale
        * lax.dot_general(
            rows_half, cols_half, (((1,), (1,)), ((), ())), preferred_element_type=jnp.float32
        )
        + shift
    )
    sign = jnp.where(row_class[:, None] == col_class[None, :], 1.0, -1.0).astype(jnp.float32)
    margin = sign * logits
    loss_part = -jnp.sum(jax.nn.log_sigmoid(margin), axis=1)
    coef = (-sign * jax.nn.sigmoid(-margin) * scale).astype(jnp.bfloat16)
    return (coef, loss_part)


def tile_plan(image_emb, text_emb, pair_class, scale, shift):
    image_unit, image_inv = unit_rows(image_emb)
    text_unit, text_inv = unit_rows(text_emb)
    own_rows = text_emb.shape[0]
    pairs = own_rows * lax.axis_size("img") * lax.axis_size("txt")
    text_half = text_unit.astype(jnp.bfloat16)
    rows_half, row_class = (
        lax.all_gather(image_unit.astype(jnp.bfloat16), "txt", axis=0, tiled=True),
        lax.all_gather(pair_class, "txt", axis=0, tiled=True),
    )
    cols_half, col_class = (
        lax.all_gather(text_half, "img", axis=0, tiled=True),
        lax.all_gather(pair_class, "img", axis=0, tiled=True),
    )
    coef, loss_part = tile_terms(rows_half, row_class, cols_half, col_class, scale, shift)
    image_pull = jnp.dot(coef, cols_half, preferred_element_type=jnp.float32)
    text_pull = lax.psum_scatter(
        lax.dot_general(
            coef, rows_half, (((0,), (0,)), ((), ())), preferred_element_type=jnp.float32
        ),
        "img",
        scatter_dimension=0,
        tiled=True,
    )
    image_sum, loss_sum = (
        lax.psum_scatter(image_pull, "txt", scatter_dimension=0, tiled=True),
        lax.psum_scatter(loss_part, "txt", scatter_dimension=0, tiled=True),
    )
    row_loss = loss_sum / pairs
    grad_image = project_back(image_unit, image_inv, image_sum)
    grad_text = project_back(text_unit, text_inv, text_pull)
    return (row_loss, grad_image, grad_text)


def on_first_core():
    return lax.rem(lax.axis_index("img"), 2) == 0


def class_digits(classes):
    rows = classes.shape[1]
    across = jnp.broadcast_to(classes, (rows, rows))
    row = lax.broadcasted_iota(jnp.int32, (rows, rows), 0)
    column = lax.broadcasted_iota(jnp.int32, (rows, rows), 1)
    lane = lax.broadcasted_iota(jnp.int32, (rows, LANES), 1)
    digits = jnp.zeros((rows, LANES), jnp.float32)
    for k in range(DIGITS):
        byte = (lax.shift_right_logical(across, 8 * k) & 255).astype(jnp.float32)
        down = jnp.sum(jnp.where(row == column, byte, 0.0), axis=1, keepdims=True)
        digits = jnp.where(lane == k, down, digits)
    return digits.astype(jnp.bfloat16)


def digits_kernel(class_ref, digits_ref):
    digits_ref[...] = class_digits(class_ref[...][None, :])


def put_rows_of(image_ref, text_ref, digits, out_ref):
    rows, depth = image_ref.shape
    for start, source in ((0, image_ref), (rows, text_ref)):
        out_ref[start : start + rows, :depth] = unit_rows(source[...])[0].astype(jnp.bfloat16)
        out_ref[start : start + rows, depth:] = digits


def pack_kernel(image_ref, text_ref, digits_ref, out_ref):
    put_rows_of(image_ref, text_ref, digits_ref[...], out_ref)


def join_kernel(own_ref, got_image, got_text, got_class, *refs):
    *refs, got_ref = refs
    put_rows_of(got_image, got_text, class_digits(got_class[...][None, :]), got_ref)
    first = on_first_core()
    rows = own_ref.shape[0] // 2
    own, got = own_ref[...].astype(jnp.float32), got_ref[...].astype(jnp.float32)
    low, high = jnp.where(first, own, got), jnp.where(first, got, own)
    images = jnp.concatenate([low[:rows], high[:rows]], axis=0)
    texts = jnp.concatenate([low[rows:], high[rows:]], axis=0)
    mine, other = jnp.where(first, images, texts), jnp.where(first, texts, images)
    for ref, block in zip(refs, (images, texts, mine, mine, mine, other)):
        ref[...] = block.astype(jnp.bfloat16)


def far_kernel(upper_ref, lower_ref, out_ref):
    rows = upper_ref.shape[0]
    out_ref[:rows, :] = upper_ref[...]
    out_ref[rows:, :] = lower_ref[...]


def near_kernel(scale_ref, shift_ref, upper_ref, lower_ref, out_ref, pair_ref):
    rows = upper_ref.shape[0]
    out_ref[:rows, :] = upper_ref[...]
    out_ref[rows:, :] = lower_ref[...]
    row = lax.broadcasted_iota(jnp.int32, pair_ref.shape, 0)
    pair_ref[...] = jnp.where(row == 0, scale_ref[0], shift_ref[0])


def power_above(size):
    return jnp.ceil(jnp.log2(jnp.maximum(size, 1e-30)) + 0.01)


def nearest(values):
    return jnp.floor(values + 0.5).astype(jnp.int32)


def code(values, power):
    return nearest(values * (TOP / jnp.exp2(power))).astype(jnp.int16)


def decode(steps, power):
    return steps.astype(jnp.int32).astype(jnp.float32) * (jnp.exp2(power) * (1.0 / TOP))


def put_rows(outs, pull, loss):
    blocks, (rows, width) = len(outs), outs[0].shape
    depth = width - LANES
    power = power_above(jnp.max(jnp.abs(pull), axis=1, keepdims=True))
    steps = code(pull, power)
    lane = lax.broadcasted_iota(jnp.int32, (blocks * rows, LANES), 1)
    loss_power = power_above(loss)
    tail = jnp.where(lane == 0, power, 0.0)
    tail = jnp.where(lane == 1, loss_power, tail)
    tail = jnp.where(lane == 2, loss * (TOP / jnp.exp2(loss_power)), tail)
    tail = nearest(tail).astype(jnp.int16)
    for k, out in enumerate(outs):
        out[:, :depth] = steps[k * rows : (k + 1) * rows]
        out[:, depth:] = tail[k * rows : (k + 1) * rows]


def tile_terms_of(lines, columns, scale, shift):
    depth = lines.shape[1] - LANES
    logits = (
        scale
        * lax.dot_general(
            lines[:, :depth],
            columns[:, :depth],
            (((1,), (1,)), ((), ())),
            preferred_element_type=jnp.float32,
        )
        + shift
    )
    pick = (
        lax.broadcasted_iota(jnp.int32, (8, LANES), 0)
        == lax.broadcasted_iota(jnp.int32, (8, LANES), 1)
    )
    column_digits = lax.dot_general(
        pick.astype(jnp.bfloat16),
        columns[:, depth:],
        (((1,), (1,)), ((), ())),
        preferred_element_type=jnp.float32,
    )
    line_digits = lines[:, depth:].astype(jnp.float32)
    same = None
    for k in range(DIGITS):
        equal = line_digits[:, k : k + 1] == column_digits[k : k + 1, :]
        same = equal if same is None else same & equal
    sign = jnp.where(same, 1.0, -1.0).astype(jnp.float32)
    margin = sign * logits
    small = jnp.exp(-jnp.abs(margin))
    over = 1.0 / (1.0 + small)
    coef = -sign * jnp.where(margin >= 0, small * over, over) * scale
    return jnp.log1p(small) - jnp.minimum(margin, 0.0), coef


def pulls_of(loss, coef, columns):
    depth = columns.shape[1] - LANES
    pull = jnp.dot(
        coef.astype(jnp.bfloat16), columns[:, :depth], preferred_element_type=jnp.float32
    )
    return pull, jnp.sum(loss, axis=1, keepdims=True)


def tile_kernel(pair_ref, mine_ref, other_ref, far_ref, swapped_ref, near_ref, *outs):
    rows = mine_ref.shape[0]
    first = on_first_core()
    scale, shift = pair_ref[0:1, 0:1], pair_ref[1:2, 0:1]

    def pick(one, two):
        return jnp.where(first, one, two)

    def parted(ref):
        image, text = ref[:rows, :].astype(jnp.float32), ref[rows:, :].astype(jnp.float32)
        return pick(image, text).astype(jnp.bfloat16), pick(text, image).astype(jnp.bfloat16)

    (line, column), (other_line, other_column) = parted(far_ref), parted(swapped_ref)
    lines = jnp.concatenate([line, near_ref[:rows, :], mine_ref[...], other_line], axis=0)
    columns = jnp.concatenate([column, other_column, near_ref[rows:, :], other_ref[...]], axis=0)
    loss, coef = tile_terms_of(lines, columns, scale, shift)
    pull, loss_sum = pulls_of(loss[: 3 * rows], coef[: 3 * rows], columns)
    put_rows([outs[0]], pull[:rows], loss_sum[:rows])
    put_rows([outs[1]], *pulls_of(loss.T[:rows], coef.T[:rows], lines))
    half = rows // 2
    halves = []
    for part in (pull, loss_sum):
        low, high = part[rows : rows + half], part[rows + half : 2 * rows]
        halves.append((pick(low, high), pick(high, low)))
    for out, part, part_loss in zip(outs[2:4], *halves):
        put_rows([out], part, part_loss)
    put_rows([outs[4]], pull[2 * rows :], loss_sum[2 * rows :])


def total(parts, rows, depth):
    pull = jnp.zeros((rows, depth), jnp.float32)
    loss = jnp.zeros((rows, 1), jnp.float32)
    for part in parts:
        tail = part[:, depth:].astype(jnp.int32).astype(jnp.float32)
        pull = pull + decode(part[:, :depth], tail[:, 0:1])
        loss = loss + tail[:, 2:3] * (jnp.exp2(tail[:, 1:2]) * (1.0 / TOP))
    return pull, loss


def place_of(first, rows):
    own = pl.multiple_of(jnp.where(first, 0, rows), rows)
    return pl.ds(own, rows), pl.ds(pl.multiple_of(rows - own, rows), rows)


def add_kernel(own_ref, back_ref, keep_ref, loss_ref, give_ref):
    rows, depth = keep_ref.shape
    own, other = place_of(on_first_core(), rows)
    pull, loss = total([own_ref[other, :], back_ref[other, :]], rows, depth)
    put_rows([give_ref], pull, loss)
    keep_ref[...], loss = total([own_ref[own, :], back_ref[own, :]], rows, depth)
    loss_ref[...] = jnp.broadcast_to(loss, loss_ref.shape)


def give_kernel(back_ref, give_ref):
    _, other = place_of(on_first_core(), give_ref.shape[0])
    give_ref[...] = back_ref[other, :]


def more_kernel(keep_ref, kept_loss_ref, back_ref, got_ref, same_ref, cross_ref, image_ref, text_ref, *outs):
    sum_ref, sum_loss_ref, unit_ref, inverse_ref = outs
    rows, depth = keep_ref.shape
    own, _ = place_of(on_first_core(), rows)
    pull, loss = total([same_ref], rows, depth)
    sum_ref[0] = keep_ref[...] + pull
    sum_loss_ref[0] = kept_loss_ref[...] + loss
    sum_ref[1], loss = total([back_ref[own, :], got_ref, cross_ref], rows, depth)
    sum_loss_ref[1] = jnp.broadcast_to(loss, sum_loss_ref.shape[1:])
    for side, ref in enumerate((image_ref, text_ref)):
        unit, inverse = unit_rows(ref[...])
        unit_ref[side] = unit
        inverse_ref[side] = jnp.broadcast_to(inverse, inverse_ref.shape[1:])


def final_kernel(pairs, sum_ref, sum_loss_ref, unit_ref, inverse_ref, got_ref, loss_ref, grad_image_ref, grad_text_ref):
    first = on_first_core()
    rows, depth = sum_ref.shape[1:]
    pull, loss = total([got_ref], rows, depth)
    pulls = (sum_ref[0] + pull, sum_ref[1])
    losses = (sum_loss_ref[0][:, 0:1] + loss, sum_loss_ref[1][:, 0:1])
    for side, (pull, out) in enumerate(
        (
            (jnp.where(first, pulls[0], pulls[1]), grad_image_ref),
            (jnp.where(first, pulls[1], pulls[0]), grad_text_ref),
        )
    ):
        out[...] = project_back(unit_ref[side], inverse_ref[side][:, 0:1], pull)
    row = lax.broadcasted_iota(jnp.int32, (rows, rows), 0)
    column = lax.broadcasted_iota(jnp.int32, (rows, rows), 1)
    loss = jnp.where(first, losses[0], losses[1])
    across = jnp.where(row == column, loss / pairs, 0.0)
    loss_ref[...] = jnp.sum(across, axis=0, keepdims=True)


def chip_plan(image_emb, text_emb, pair_class, scale, shift):
    rows, depth = image_emb.shape
    width = depth + LANES
    lanes = lax.axis_size("txt")
    n = lax.axis_size("img") * lanes
    vmem = pl.BlockSpec(memory_space=pltpu.VMEM)
    smem = pl.BlockSpec(memory_space=pltpu.SMEM)

    def call(kernel, shapes, operands, name, scalars=0, cost=None, scratch=()):
        return pl.pallas_call(
            kernel,
            scratch_shapes=scratch,
            cost_estimate=cost,
            out_shape=shapes,
            in_specs=[smem] * scalars + [vmem] * (len(operands) - scalars),
            out_specs=jax.tree.map(lambda _: vmem, shapes),
            compiler_params=pltpu.CompilerParams(vmem_limit_bytes=32 << 20),
            name=name,
        )(*operands)

    def block(count, dtype=jnp.bfloat16):
        return jax.ShapeDtypeStruct((count * rows, width), dtype)

    def wide(*shape):
        return jax.ShapeDtypeStruct(shape, jnp.float32)

    def core(i):
        return i // lanes % 2

    def visit(x, masks, cross):
        pairs = []
        for i in range(n):
            chip = (i // (2 * lanes) * lanes + i % lanes) ^ masks[core(i)]
            pairs.append((i, (chip // lanes * 2 + (core(i) ^ cross)) * lanes + chip % lanes))
        return lax.ppermute(x, AXES, pairs)

    def swap(x):
        return lax.ppermute(x, AXES, [(i, i ^ lanes) for i in range(n)])

    out_visits = (((12, 8), 0), ((2, 3), 0), ((4, 1), 0), ((4, 1), 1))
    back_visits = (((12, 3), 0), ((2, 8), 0), ((4, 1), 0), ((4, 1), 1))
    late = pl.CostEstimate(flops=10**9, bytes_accessed=10**7, transcendentals=0)
    digits = call(
        digits_kernel,
        jax.ShapeDtypeStruct((rows, LANES), jnp.bfloat16),
        [pair_class],
        "digits",
        cost=late,
    )
    own = call(pack_kernel, block(2), [image_emb, text_emb, digits], "pack")
    swapped = [swap(x) for x in (image_emb, text_emb, pair_class)]
    *sent, mine, other = call(
        join_kernel,
        (block(2),) * 6,
        [own, *swapped],
        "join",
        scratch=[pltpu.VMEM((2 * rows, width), jnp.bfloat16)],
    )
    got = [visit(x, *way) for x, way in zip(sent, out_visits)]
    far = call(far_kernel, block(4), got[:2], "far")
    near, pair = call(
        near_kernel,
        (block(4), wide(8, LANES)),
        [scale[None], shift[None], *got[2:]],
        "near",
        2,
        late,
    )
    one, two = block(1, jnp.int16), block(2, jnp.int16)
    parts = call(
        tile_kernel,
        (two, two, one, one, two),
        [pair, mine, other, far, swap(far), near],
        "tile",
    )
    back = [visit(x, *way) for x, way in zip(parts, back_visits)]
    keep, kept_loss, give = call(
        add_kernel, (wide(rows, depth), wide(rows, LANES), one), [parts[4], back[0]], "add"
    )
    sums = call(
        more_kernel,
        (wide(2, rows, depth), wide(2, rows, LANES)) * 2,
        [keep, kept_loss, back[1], swap(give), *back[2:], image_emb, text_emb],
        "more",
        cost=late,
    )
    loss, grad_image, grad_text = call(
        functools.partial(final_kernel, n * rows),
        (wide(1, rows), wide(rows, depth), wide(rows, depth)),
        [*sums, swap(call(give_kernel, one, [back[1]], "give"))],
        "final",
    )
    return (loss[0], grad_image, grad_text)


def local(image_emb, text_emb, pair_class, scale, shift):
    if lax.axis_size("img") * lax.axis_size("txt") == 2 * 4 * 4 and lax.axis_size("txt") in (1, 2, 4):
        return chip_plan(image_emb, text_emb, pair_class, scale, shift)
    return tile_plan(image_emb, text_emb, pair_class, scale, shift)


def solution(mesh):
    in_specs = (P(AXES, None), P(AXES, None), P(AXES), P(), P())
    out_specs = (P(AXES), P(AXES, None), P(AXES, None))
    return jax.shard_map(local, mesh=mesh, in_specs=in_specs, out_specs=out_specs, check_vma=False)
```
